256 devices in a mesh: fsdp: 64 (over z, y, core), tensor: 4 (over x).
Axes of the slice: x: 4, y: 4, z: 8, core: 2. Of those that a mesh axis runs over, the one named last changes fastest.
Arguments:
- momentum: bfloat16 [16384, 26624], P('fsdp', 'tensor'), may hold values from -6 to 6
- q_basis: float32 [256, 26624], P('fsdp', 'tensor'), may hold values from -0.0390625 to 0.0390625
Outputs:
- new_momentum: bfloat16 [16384, 26624], P('fsdp', 'tensor')
- update: bfloat16 [16384, 26624], P('fsdp', 'tensor')
- q_next: float32 [256, 26624], P('fsdp', 'tensor')
The draws below stay inside these ranges and needn't reach their ends.
All inputs are finite; a program needn't handle non-finite values.
Results may differ from the reference program's by a relative error of at most 0.0073.
Values may be sent and summed in bfloat16 or wider, within the bound.
No kernel may reach another device: no remote copies, remote signals or barrier semaphores. Data moves between devices by JAX's collectives and lax.ppermute only.
A program may use at most 64 MiB of HBM per device.

```python
import math
import jax
import jax.numpy as jnp
from jax import lax

ROWS = 16384
COLS = 26624
RANK = 256


def shard_levels(own_key, extent, shards, low, high):
    level, own = 1.0, jax.random.fold_in(own_key, 6)
    for dim, parts in shards:
        steps = jnp.exp(jax.random.uniform(jax.random.fold_in(own, dim), (parts,), jnp.float32, low / len(shards), high / len(shards)))
        level = level * jnp.repeat(steps, extent[dim] // parts).reshape([-1 if axis == dim else 1 for axis in range(len(extent))])
    return level


def scatter_about(rng, extent, width, most, split=(), held_as=jnp.bfloat16):
    values = jax.random.normal(rng, extent, jnp.float32) * width
    if len(split) > 0:
        values = shard_levels(rng, extent, split, -0.22, 0.18) * values
    return jnp.clip(values, min=-most, max=most).astype(held_as)


def setup_inputs(seed: int = 0) -> dict:
    key_of = jax.random.split(jax.random.key(seed), 3)
    return {
        "momentum": scatter_about(key_of[0], (ROWS, COLS), 1.0, 6.0, ((0, 64), (1, 4))),
        "q_basis": scatter_about(key_of[1], (RANK, COLS), COLS ** -0.5, 0.0390625, ((0, 64), (1, 4)), jnp.float32),
    }


momentum_decay = 0.95

def reference(momentum, q_basis):
    basis_half = q_basis.astype(jnp.bfloat16)
    projected = jnp.dot(momentum.astype(jnp.float32), basis_half.T.astype(jnp.float32), preferred_element_type=jnp.float32)
    gram_matrix = jnp.dot(projected.T.astype(jnp.float32), projected.astype(jnp.float32), preferred_element_type=jnp.float32, precision=lax.Precision.HIGHEST)
    ridge = 0.001 * jnp.trace(gram_matrix) / RANK
    gram_matrix = gram_matrix + ridge * jnp.eye(RANK, dtype=jnp.float32)
    factor = jnp.linalg.cholesky(gram_matrix)
    solved = lax.linalg.triangular_solve(factor, projected, left_side=False, lower=True, transpose_a=True)
    orthonormal = solved.astype(jnp.bfloat16)
    right_factor = jnp.dot(orthonormal.T.astype(jnp.float32), momentum.astype(jnp.float32), preferred_element_type=jnp.float32)
    lengths = jnp.sqrt(lax.optimization_barrier(jnp.sum(right_factor * right_factor, axis=1)) + 1e-06)
    q_next = right_factor / lengths[:, None]
    right_half = right_factor.astype(jnp.bfloat16)
    basis_next = q_next.astype(jnp.bfloat16)
    removed = jnp.dot(orthonormal.astype(jnp.float32), right_half.astype(jnp.float32), preferred_element_type=jnp.float32)
    new_momentum = (momentum.astype(jnp.float32) - (1.0 - momentum_decay) * removed).astype(jnp.bfloat16)
    scaling = math.sqrt(ROWS * COLS / RANK)
    direction = jnp.dot(orthonormal.astype(jnp.float32), basis_next.astype(jnp.float32), preferred_element_type=jnp.float32)
    update = (direction * scaling).astype(jnp.bfloat16)
    return (new_momentum, update, q_next)
```

```python
import math

import jax
import jax.numpy as jnp
from jax import lax
from jax.sharding import Mesh
from jax.sharding import PartitionSpec as P

momentum_decay = 0.95
f32, bf16 = jnp.float32, jnp.bfloat16
HIGHEST = lax.Precision.HIGHEST


def swap_cores(block):
    return lax.ppermute(block, "c", [(0, 1), (1, 0)])


def gather(block, axes, parts):
    copies = jnp.broadcast_to(block[None], (parts,) + block.shape)
    return lax.all_to_all(copies, axes, 0, 0)


def scatter_sum(block, axes, parts):
    pieces = block.reshape((parts, block.shape[0] // parts) + block.shape[1:])
    return jnp.sum(lax.all_to_all(pieces, axes, 0, 0).astype(f32), axis=0)


def per_device(sizes, momentum, q_basis):
    nz, ny, nx = sizes
    rows, cols = momentum.shape
    half = cols // 2
    shard_rank = q_basis.shape[0]
    rank = shard_rank * nz * ny * 2
    core = lax.axis_index("c")

    def mine(array):
        return lax.dynamic_slice_in_dim(array, core * half, half, 1)

    def theirs(array):
        return lax.dynamic_slice_in_dim(array, (1 - core) * half, half, 1)

    def both(own, other):
        first = core == 0
        return jnp.concatenate([jnp.where(first, own, other), jnp.where(first, other, own)])

    basis_half = q_basis.astype(bf16)
    basis_chip = both(mine(basis_half), swap_cores(theirs(basis_half)))
    momentum_chip = both(mine(momentum), swap_cores(theirs(momentum)))

    basis_z = gather(basis_chip, "z", nz)
    basis_zy = gather(basis_z, "y", ny)
    basis_whole = basis_zy.transpose(1, 0, 2, 3).reshape(rank, half)
    partial_proj = lax.dot_general(
        momentum_chip, basis_whole, (((1,), (1,)), ((), ())), preferred_element_type=f32
    )
    proj_piece = scatter_sum(partial_proj, ("x", "c"), nx * 2)
    projected = gather(proj_piece, ("x", "c"), nx * 2).reshape(2 * rows, rank)

    gram_chip = jnp.dot(projected.T, projected, preferred_element_type=f32, precision=HIGHEST)
    place = lax.axis_index("x") * 2 + core
    part = rank // (nx * 2)
    gram_rows = lax.dynamic_slice_in_dim(gram_chip, place * part, part, 0)
    gram_rows = jnp.sum(gather(gram_rows, "y", ny), axis=0)
    gram_rows = jnp.sum(gather(gram_rows, "z", nz), axis=0)
    gram_matrix = gather(gram_rows, ("x", "c"), nx * 2).reshape(rank, rank)

    ridge = 0.001 * jnp.trace(gram_matrix) / rank
    factor = jnp.linalg.cholesky(gram_matrix + ridge * jnp.eye(rank, dtype=f32))
    solved = lax.linalg.triangular_solve(
        factor, projected, left_side=False, lower=True, transpose_a=True
    )
    orthonormal = solved.astype(bf16)

    right = lax.dot_general(
        momentum_chip, orthonormal, (((0,), (0,)), ((), ())), preferred_element_type=f32
    ).astype(bf16)
    right = scatter_sum(right, "y", ny).astype(bf16)
    right = scatter_sum(right, "z", nz).astype(bf16)
    right = gather(right, "z", nz).reshape(half // ny, rank)
    right = gather(right, "y", ny).reshape(half, rank)
    squares = lax.psum(jnp.sum(jnp.square(right.astype(f32)), axis=0), ("x", "c"))
    lengths = jnp.sqrt(squares + 1e-06)
    right_half = both(right, swap_cores(right))

    own_orth = lax.dynamic_slice_in_dim(orthonormal, core * rows, rows, 0)
    own_solved = lax.dynamic_slice_in_dim(solved, core * rows, rows, 0)
    total_rows = rows * nz * ny * 2
    total_cols = cols * nx
    scaling = math.sqrt(total_rows * total_cols / rank)
    scaled = (own_solved * (scaling / lengths)[None, :]).astype(bf16)

    def times_right(left):
        return lax.dot_general(
            left, right_half, (((1,), (1,)), ((), ())), preferred_element_type=f32
        )

    new_momentum = (
        momentum.astype(f32) - (1.0 - momentum_decay) * times_right(own_orth)
    ).astype(bf16)
    update = times_right(scaled).astype(bf16)
    position = (lax.axis_index("z") * ny + lax.axis_index("y")) * 2 + core
    first_row = position * shard_rank
    ranks = first_row + jnp.arange(shard_rank)
    picked = (ranks[:, None] == jnp.arange(rank)[None, :]).astype(bf16)
    own_lengths = lax.dynamic_slice_in_dim(lengths, first_row, shard_rank, 0)
    q_next = times_right(picked) / own_lengths[:, None]
    return (new_momentum, update, q_next)


def solution(mesh):
    nz, ny, nx = 8, 4, 4
    split = Mesh(mesh.devices.reshape(nz, ny, 2, nx), ("z", "y", "c", "x"))
    spec = P(("z", "y", "c"), "x")
    return jax.shard_map(
        lambda momentum, q_basis: per_device((nz, ny, nx), momentum, q_basis),
        mesh=split,
        in_specs=(spec, spec),
        out_specs=(spec, spec, spec),
        check_vma=False,
    )
```

```python
import math

import jax
import jax.numpy as jnp
from jax import lax
from jax.experimental import pallas as pl
from jax.experimental.pallas import tpu as pltpu
from jax.sharding import Mesh
from jax.sharding import PartitionSpec as P

momentum_decay = 0.95
f32, bf16 = jnp.float32, jnp.bfloat16
HIGHEST = lax.Precision.HIGHEST
VMEM = pl.BlockSpec(memory_space=pltpu.VMEM)
PIVOTS = 8


def inverse_factor_kernel(gram_ref, inverse_ref, work_ref):
    rank = gram_ref.shape[0]
    gram = gram_ref[...]
    diagonal = lax.broadcasted_iota(jnp.int32, gram.shape, 0) == lax.broadcasted_iota(
        jnp.int32, gram.shape, 1
    )
    ridge = 0.001 * jnp.sum(jnp.where(diagonal, gram, 0.0)) / rank
    work_ref[...] = jnp.where(diagonal, gram + ridge, gram)
    lane = lax.broadcasted_iota(jnp.int32, (1, rank), 1)

    def wide(value):
        return jnp.concatenate([value] * (rank // 128), axis=1)

    steps = range(PIVOTS)
    for start in range(0, rank, PIVOTS):
        end = start + PIVOTS
        block = work_ref[start:end, :]
        spread = [jnp.broadcast_to(block[:, start + t : start + t + 1], (PIVOTS, 128)) for t in steps]
        core = [[spread[t][s : s + 1, :] for t in range(s + 1)] for s in steps]
        inside = (lane >= start) & (lane < end)
        row = [
            jnp.where(inside, (lane == start + s).astype(f32), block[s : s + 1, :]) for s in steps
        ]
        inverse = [None] * PIVOTS
        ratio = [[None] * PIVOTS for _ in steps]
        for t in steps:
            inverse[t] = 1.0 / core[t][t]
            for s in range(t + 1, PIVOTS):
                ratio[s][t] = core[s][t] * inverse[t]
            for s in range(t + 1, PIVOTS):
                for u in range(t + 1, s + 1):
                    core[s][u] = core[s][u] - ratio[s][t] * core[u][t]
                row[s] = row[s] - wide(ratio[s][t]) * row[t]
        for s in steps:
            scaled = row[s] * wide(lax.rsqrt(core[s][s]))
            inverse_ref[start + s : start + s + 1, :] = jnp.where(lane < end, scaled, 0.0)
        if end < rank:
            solved = [row[s] * wide(inverse[s]) for s in steps]
            for s in reversed(steps):
                for t in range(s):
                    solved[t] = solved[t] - wide(ratio[s][t]) * solved[s]
            below = work_ref[end:, :]
            rest = jnp.where(inside, 0.0, below)
            for t in steps:
                rest = rest - below[:, start + t : start + t + 1] * solved[t]
            work_ref[end:, :] = rest


def inverse_factor(gram_matrix):
    return pl.pallas_call(
        inverse_factor_kernel,
        out_shape=jax.ShapeDtypeStruct(gram_matrix.shape, f32),
        in_specs=[VMEM],
        out_specs=VMEM,
        scratch_shapes=[pltpu.VMEM(gram_matrix.shape, f32)],
        compiler_params=pltpu.CompilerParams(vmem_limit_bytes=8 * 2**20),
    )(gram_matrix)


def cross_kernel(momentum_ref, terms_ref, out_ref):
    rank = out_ref.shape[1]
    product = lax.dot_general(
        momentum_ref[...], terms_ref[...], (((0,), (0,)), ((), ())), preferred_element_type=f32
    )
    out_ref[...] = (
        product[:, 2 * rank :] + product[:, rank : 2 * rank] + product[:, :rank]
    )


def cross(momentum, projected):
    rows, cols = momentum.shape
    rank = projected.shape[1]
    high = lax.reduce_precision(projected, 8, 7)
    left = projected - high
    middle = lax.reduce_precision(left, 8, 7)
    low = left - middle
    terms = jnp.concatenate([high, middle, low], axis=1).astype(bf16)
    block = 256
    return pl.pallas_call(
        cross_kernel,
        out_shape=jax.ShapeDtypeStruct((cols, rank), f32),
        grid=(cols // block,),
        in_specs=[
            pl.BlockSpec((rows, block), lambda i: (0, i)),
            pl.BlockSpec((rows, 3 * rank), lambda i: (0, 0)),
        ],
        out_specs=pl.BlockSpec((block, rank), lambda i: (i, 0)),
        compiler_params=pltpu.CompilerParams(vmem_limit_bytes=16 * 2**20),
        cost_estimate=pl.CostEstimate(
            flops=6 * rows * cols * rank, bytes_accessed=2 * rows * cols + 4 * cols * rank, transcendentals=0
        ),
    )(momentum, terms)


def swap_cores(block):
    return lax.ppermute(block, "c", [(0, 1), (1, 0)])


def shift(block, axis, parts, by):
    return lax.ppermute(block, axis, [(i, (i + by) % parts) for i in range(parts)])


def sum_four(block, axis):
    right, across, left = (shift(block, axis, 4, by) for by in (1, 2, 3))
    return (block + across) + (right + left)


def gather(block, axes, parts):
    copies = jnp.broadcast_to(block[None], (parts,) + block.shape)
    return lax.all_to_all(copies, axes, 0, 0)


def scatter_sum(block, axes, parts):
    pieces = block.reshape((parts, block.shape[0] // parts) + block.shape[1:])
    return jnp.sum(lax.all_to_all(pieces, axes, 0, 0).astype(f32), axis=0)


def per_device(sizes, momentum, q_basis):
    nz, ny, nx = sizes
    rows, cols = momentum.shape
    half = cols // 2
    shard_rank = q_basis.shape[0]
    rank = shard_rank * nz * ny * 2
    core = lax.axis_index("c")

    def mine(array):
        return lax.dynamic_slice_in_dim(array, core * half, half, 1)

    def theirs(array):
        return lax.dynamic_slice_in_dim(array, (1 - core) * half, half, 1)

    def both(own, other):
        first = core == 0
        return jnp.concatenate([jnp.where(first, own, other), jnp.where(first, other, own)])

    basis_half = q_basis.astype(bf16)
    basis_chip = both(mine(basis_half), swap_cores(theirs(basis_half)))
    momentum_chip = both(mine(momentum), swap_cores(theirs(momentum)))

    basis_z = gather(basis_chip, "z", nz)
    basis_zy = gather(basis_z, "y", ny)
    basis_whole = basis_zy.transpose(1, 0, 2, 3).reshape(rank, half)
    partial_proj = lax.dot_general(
        momentum_chip, basis_whole, (((1,), (1,)), ((), ())), preferred_element_type=f32
    )
    proj_own = lax.dynamic_slice_in_dim(partial_proj, core * rows, rows, 0)
    proj_other = lax.dynamic_slice_in_dim(partial_proj, (1 - core) * rows, rows, 0)
    projected = sum_four(proj_own + swap_cores(proj_other), "x")

    gram_own = jnp.dot(projected.T, projected, preferred_element_type=f32, precision=HIGHEST)
    place = lax.axis_index("x") * 2
    part = rank // (nx * 2)
    gram_keep = lax.dynamic_slice_in_dim(gram_own, (place + core) * part, part, 0)
    gram_send = lax.dynamic_slice_in_dim(gram_own, (place + 1 - core) * part, part, 0)
    gram_rows = sum_four(gram_keep + swap_cores(gram_send), "y")
    gram_rows = jnp.sum(gather(gram_rows, "z", nz), axis=0)
    gram_matrix = gather(gram_rows, ("x", "c"), nx * 2).reshape(rank, rank)

    right = cross(momentum_chip, both(projected, swap_cores(projected)))
    piece = half // ny
    at_y = lax.axis_index("y")
    pieces = [
        lax.dynamic_slice_in_dim(right, lax.rem(at_y + by, ny) * piece, piece, 0) for by in range(ny)
    ]
    right = pieces[0] + sum(shift(pieces[by], "y", ny, by) for by in range(1, ny))

    inverse = inverse_factor(gram_matrix)

    def whiten(array):
        return lax.dot_general(
            array, inverse, (((1,), (1,)), ((), ())), preferred_element_type=f32, precision=HIGHEST
        )

    solved = whiten(projected)
    orthonormal = solved.astype(bf16)
    right = scatter_sum(whiten(right).astype(bf16), "z", nz).astype(bf16)
    right = gather(right, "z", nz).reshape(piece, rank)
    right = gather(right, "y", ny).reshape(half, rank)
    squares = jnp.sum(jnp.square(right.astype(f32)), axis=0, keepdims=True)
    squares = sum_four(squares + swap_cores(squares), "x")
    lengths = jnp.sqrt(squares + 1e-06)
    right_half = both(right, swap_cores(right))

    total_rows = rows * nz * ny * 2
    total_cols = cols * nx
    scaling = math.sqrt(total_rows * total_cols / rank)
    scaled = (solved * (scaling / lengths)).astype(bf16)

    def times_right(left):
        return lax.dot_general(
            left, right_half, (((1,), (1,)), ((), ())), preferred_element_type=f32
        )

    new_momentum = (
        momentum.astype(f32) - (1.0 - momentum_decay) * times_right(orthonormal)
    ).astype(bf16)
    update = times_right(scaled).astype(bf16)
    position = (lax.axis_index("z") * ny + lax.axis_index("y")) * 2 + core
    first_row = position * shard_rank
    ranks = first_row + jnp.arange(shard_rank)
    picked = (ranks[:, None] == jnp.arange(rank)[None, :]).astype(bf16)
    own_lengths = lax.dynamic_slice_in_dim(lengths[0], first_row, shard_rank, 0)
    q_next = times_right(picked) / own_lengths[:, None]
    return (new_momentum, update, q_next)


def solution(mesh):
    nz, ny, nx = 8, 4, 4
    split = Mesh(mesh.devices.reshape(nz, ny, 2, nx), ("z", "y", "c", "x"))
    spec = P(("z", "y", "c"), "x")
    return jax.shard_map(
        lambda momentum, q_basis: per_device((nz, ny, nx), momentum, q_basis),
        mesh=split,
        in_specs=(spec, spec),
        out_specs=(spec, spec, spec),
        check_vma=False,
    )
```

```python
import math

import jax
import jax.numpy as jnp
from jax import lax
from jax.experimental import pallas as pl
from jax.experimental.pallas import tpu as pltpu
from jax.sharding import Mesh
from jax.sharding import PartitionSpec as P

momentum_decay = 0.95
f32, bf16 = jnp.float32, jnp.bfloat16
HIGHEST = lax.Precision.HIGHEST
VMEM = pl.BlockSpec(memory_space=pltpu.VMEM)
SMEM = pl.BlockSpec(memory_space=pltpu.SMEM)
ANY = pl.BlockSpec(memory_space=pl.ANY)
BOTH_LAST = (((1,), (1,)), ((), ()))
BOTH_FIRST = (((0,), (0,)), ((), ()))
MIB = 2**20
NZ, NY, NX = 8, 4, 4
PIVOTS = 8
RING_FROM = (0, 1, 3, 2, 2)
AT_Y, AT_CORE, AT_X, FIRST_RANK = range(4)


def ahead(index, by, parts):
    return lax.rem(index + by, parts)


def stored_start(group):
    return (group % NY) * NZ * PIVOTS + (group // NY) * PIVOTS


def inverse_factor_kernel(at_ref, own_ref, next_ref, across_ref, last_ref, inverse_ref, work_ref):
    rank = work_ref.shape[0]
    part = rank // (NX * 2)
    for by, ref in enumerate((own_ref, next_ref, across_ref, last_ref)):
        base = ahead(at_ref[AT_X], by, NX) * 2
        for other in range(2):
            at_core = (at_ref[AT_CORE] + other) % 2
            start = pl.multiple_of((base + at_core) * part, part)
            work_ref[pl.ds(start, part), :] = ref[other * part : (other + 1) * part, :]
    gram = work_ref[...]
    diagonal = lax.broadcasted_iota(jnp.int32, gram.shape, 0) == lax.broadcasted_iota(
        jnp.int32, gram.shape, 1
    )
    ridge = 0.001 * jnp.sum(jnp.where(diagonal, gram, 0.0)) / rank
    work_ref[...] = jnp.where(diagonal, gram + ridge, gram)
    lane = lax.broadcasted_iota(jnp.int32, (1, rank), 1)
    per_y = NZ * PIVOTS
    order = (lane % per_y) // PIVOTS * (NY * PIVOTS) + lane // per_y * PIVOTS + lane % PIVOTS

    def wide(value):
        return jnp.concatenate([value] * (rank // 128), axis=1)

    steps = range(PIVOTS)
    for group in range(rank // PIVOTS):
        start, end = group * PIVOTS, (group + 1) * PIVOTS
        at = stored_start(group)
        block = work_ref[at : at + PIVOTS, :]
        spread = [jnp.broadcast_to(block[:, at + t : at + t + 1], (PIVOTS, 128)) for t in steps]
        core = [[spread[t][s : s + 1, :] for t in range(s + 1)] for s in steps]
        inside = (order >= start) & (order < end)
        row = [jnp.where(inside, (lane == at + s).astype(f32), block[s : s + 1, :]) for s in steps]
        inverse = [None] * PIVOTS
        ratio = [[None] * PIVOTS for _ in steps]
        for t in steps:
            inverse[t] = 1.0 / core[t][t]
            for s in range(t + 1, PIVOTS):
                ratio[s][t] = core[s][t] * inverse[t]
            for s in range(t + 1, PIVOTS):
                for u in range(t + 1, s + 1):
                    core[s][u] = core[s][u] - ratio[s][t] * core[u][t]
                row[s] = row[s] - wide(ratio[s][t]) * row[t]
        for s in steps:
            scaled = row[s] * wide(lax.rsqrt(core[s][s]))
            inverse_ref[start + s : start + s + 1, :] = jnp.where(order < end, scaled, 0.0)
        solved = [row[s] * wide(inverse[s]) for s in steps]
        for s in reversed(steps):
            for t in range(s):
                solved[t] = solved[t] - wide(ratio[s][t]) * solved[s]
        for at_y in range(NY):
            at_z = group // NY + (0 if at_y > group % NY else 1)
            if at_z == NZ:
                continue
            rows = slice(at_y * per_y + at_z * PIVOTS, (at_y + 1) * per_y)
            below = work_ref[rows, :]
            rest = jnp.where(inside, 0.0, below)
            for t in steps:
                rest = rest - below[:, at + t : at + t + 1] * solved[t]
            work_ref[rows, :] = rest


def inverse_factor(at, pieces):
    rank = pieces[0].shape[1]
    return pl.pallas_call(
        inverse_factor_kernel,
        out_shape=jax.ShapeDtypeStruct((rank, rank), f32),
        in_specs=[SMEM] + [VMEM] * 4,
        out_specs=VMEM,
        scratch_shapes=[pltpu.VMEM((rank, rank), f32)],
        compiler_params=pltpu.CompilerParams(vmem_limit_bytes=8 * MIB),
    )(at, *pieces)


def project_kernel(at_ref, mine_ref, other_ref, *refs):
    pieces, (out_mine_ref, out_other_ref, basis_ref) = refs[:5], refs[5:]
    per_y = pieces[0].shape[0]
    for n, ref in enumerate(pieces):
        size = ref.shape[0]
        start = ahead(at_ref[AT_Y], RING_FROM[n], NY) * per_y + (size if n == 4 else 0)
        basis_ref[pl.ds(pl.multiple_of(start, size), size), :] = ref[...]
    basis = basis_ref[...]
    product_mine = lax.dot_general(mine_ref[...], basis, BOTH_LAST, preferred_element_type=f32)
    product_other = lax.dot_general(other_ref[...], basis, BOTH_LAST, preferred_element_type=f32)
    first = pl.program_id(0) == 0

    @pl.when(first)
    def _():
        out_mine_ref[...] = product_mine
        out_other_ref[...] = product_other

    @pl.when(jnp.logical_not(first))
    def _():
        out_mine_ref[...] += product_mine
        out_other_ref[...] += product_other


def project(at, mine, other, pieces):
    rows, cols = mine.shape
    rank = pieces[0].shape[0] * NY
    width = cols // 2

    def columns(height):
        return pl.BlockSpec((height, width), lambda i: (0, i))

    whole = pl.BlockSpec((rows, rank), lambda i: (0, 0))
    return pl.pallas_call(
        project_kernel,
        out_shape=[jax.ShapeDtypeStruct((rows, rank), f32)] * 2,
        grid=(2,),
        in_specs=[SMEM, columns(rows), columns(rows)] + [columns(p.shape[0]) for p in pieces],
        out_specs=[whole, whole],
        scratch_shapes=[pltpu.VMEM((rank, width), bf16)],
        compiler_params=pltpu.CompilerParams(vmem_limit_bytes=32 * MIB),
        cost_estimate=pl.CostEstimate(
            flops=4 * rows * cols * rank, bytes_accessed=6 * rows * cols, transcendentals=0
        ),
    )(at, mine, other, *pieces)


def cross_kernel(at_ref, mine_ref, other_ref, left_mine_ref, left_other_ref, *refs):
    pieces, (terms_ref, whole_ref) = refs[:NY], refs[NY:]
    rows, rank = left_mine_ref.shape
    step = pl.program_id(0)
    width = mine_ref.shape[1]

    @pl.when(step == 0)
    def _():
        for n, ref in enumerate((left_mine_ref, left_other_ref)):
            left = ref[...]
            for t in range(3):
                term = left.astype(bf16)
                terms_ref[n * rows : (n + 1) * rows, t * rank : (t + 1) * rank] = term
                left = left - term.astype(f32)

    momentum = jnp.concatenate([mine_ref[...], other_ref[...]], axis=0)
    product = lax.dot_general(momentum, terms_ref[...], BOTH_FIRST, preferred_element_type=f32)
    total = (product[:, 2 * rank :] + product[:, rank : 2 * rank]) + product[:, :rank]
    whole_ref[pl.ds(pl.multiple_of(step * width, width), width), :] = total

    @pl.when(step == pl.num_programs(0) - 1)
    def _():
        size = pieces[0].shape[0]
        for by, ref in enumerate(pieces):
            start = pl.multiple_of(ahead(at_ref[AT_Y], by, NY) * size, size)
            ref[...] = whole_ref[pl.ds(start, size), :]


def cross(at, mine, other, left_mine, left_other):
    rows, cols = mine.shape
    rank = left_mine.shape[1]
    width, size = cols // 2, cols // NY
    columns = pl.BlockSpec((rows, width), lambda i: (0, i))
    left = pl.BlockSpec((rows, rank), lambda i: (0, 0))
    piece = pl.BlockSpec((size, rank), lambda i: (0, 0))
    return pl.pallas_call(
        cross_kernel,
        out_shape=[jax.ShapeDtypeStruct((size, rank), f32)] * NY,
        grid=(2,),
        in_specs=[SMEM, columns, columns, left, left],
        out_specs=[piece] * NY,
        scratch_shapes=[pltpu.VMEM((2 * rows, 3 * rank), bf16), pltpu.VMEM((cols, rank), f32)],
        compiler_params=pltpu.CompilerParams(vmem_limit_bytes=40 * MIB),
        cost_estimate=pl.CostEstimate(
            flops=12 * rows * cols * rank, bytes_accessed=4 * rows * cols + 8 * cols * rank, transcendentals=0
        ),
    )(at, mine, other, left_mine, left_other)


def finish_kernel(scaling, at_ref, momentum_ref, solved_ref, squares_ref, *refs):
    pieces = refs[:10]
    new_momentum_ref, update_ref, q_next_ref, right_ref, left_ref, inverse_ref, semaphores = refs[10:]
    rows, rank = solved_ref.shape
    step = pl.program_id(0)
    width = momentum_ref.shape[1]
    shard_rank = q_next_ref.shape[0]
    size = pieces[0].shape[0]

    @pl.when(step == 0)
    def _():
        copies = []
        for n, ref in enumerate(pieces):
            side = at_ref[AT_CORE] if n < 5 else 1 - at_ref[AT_CORE]
            start = (side * NY + ahead(at_ref[AT_Y], RING_FROM[n % 5], NY)) * size
            start = pl.multiple_of(start + (ref.shape[0] if n % 5 == 4 else 0), 16)
            copy = pltpu.make_async_copy(
                ref, right_ref.at[pl.ds(start, ref.shape[0]), :], semaphores.at[n]
            )
            copy.start()
            copies.append(copy)
        solved = solved_ref[...]
        squares = jnp.sum(squares_ref[...], axis=0, keepdims=True)
        inverse_lengths = lax.rsqrt(squares + 1e-06)
        left_ref[:rows, :] = solved.astype(bf16)
        left_ref[rows : 2 * rows, :] = (solved * (scaling * inverse_lengths)).astype(bf16)
        wanted = lax.broadcasted_iota(jnp.int32, (16, rank), 0) + at_ref[FIRST_RANK]
        picked = jnp.where(wanted == lax.broadcasted_iota(jnp.int32, (16, rank), 1), 1.0, 0.0)
        left_ref[2 * rows :, :] = picked.astype(bf16)
        own = jnp.sum(picked * inverse_lengths, axis=1, keepdims=True)
        inverse_ref[...] = jnp.broadcast_to(own, inverse_ref.shape)
        for copy in copies:
            copy.wait()

    right = right_ref[pl.ds(pl.multiple_of(step * width, width), width), :]
    product = lax.dot_general(left_ref[...], right, BOTH_LAST, preferred_element_type=f32)
    momentum = momentum_ref[...].astype(f32)
    new_momentum_ref[...] = (momentum - (1.0 - momentum_decay) * product[:rows]).astype(bf16)
    update_ref[...] = product[rows : 2 * rows].astype(bf16)
    q_next_ref[...] = (
        product[2 * rows : 2 * rows + shard_rank] * inverse_ref[:shard_rank, :1]
    )


def finish(at, momentum, solved, squares, pieces, scaling, shard_rank):
    rows, cols = momentum.shape
    rank = solved.shape[1]
    width = cols // 4
    columns = pl.BlockSpec((rows, width), lambda i: (0, i))
    out = jax.ShapeDtypeStruct((rows, cols), bf16)
    return pl.pallas_call(
        lambda *refs: finish_kernel(scaling, *refs),
        out_shape=[out, out, jax.ShapeDtypeStruct((shard_rank, cols), f32)],
        grid=(4,),
        in_specs=[
            SMEM,
            columns,
            pl.BlockSpec(solved.shape, lambda i: (0, 0)),
            pl.BlockSpec(squares.shape, lambda i: (0, 0)),
        ]
        + [ANY] * 10,
        out_specs=[columns, columns, pl.BlockSpec((shard_rank, width), lambda i: (0, i))],
        scratch_shapes=[
            pltpu.VMEM((cols, rank), bf16),
            pltpu.VMEM((2 * rows + 16, rank), bf16),
            pltpu.VMEM((16, 128), f32),
            pltpu.SemaphoreType.DMA((10,)),
        ],
        compiler_params=pltpu.CompilerParams(vmem_limit_bytes=40 * MIB),
        cost_estimate=pl.CostEstimate(
            flops=4 * rows * cols * rank, bytes_accessed=8 * rows * cols, transcendentals=0
        ),
    )(at, momentum, solved, squares, *pieces)


def swap_cores(block):
    return lax.ppermute(block, "c", [(0, 1), (1, 0)])


def from_ahead(block, axis, by, parts=4):
    return lax.ppermute(block, axis, [((i + by) % parts, i) for i in range(parts)])


def sum_four(block, axis):
    one, two, three = (from_ahead(block, axis, by) for by in (1, 2, 3))
    return (block + two) + (one + three)


def ring_of_four(block, axis, beside=None):
    middle = block.shape[0] // 2
    one, three = from_ahead(block, axis, 1), from_ahead(block, axis, 3)
    one, three, beside = lax.optimization_barrier((one, three, beside))
    across = (from_ahead(three[:middle], axis, 3), from_ahead(one[middle:], axis, 1))
    return (block, one, three) + across, beside


def gather(block, axes, parts):
    copies = jnp.broadcast_to(block[None], (parts,) + block.shape)
    return lax.all_to_all(copies, axes, 0, 0)


def scatter_sum(block, axes, parts):
    pieces = block.reshape((parts, block.shape[0] // parts) + block.shape[1:])
    return jnp.sum(lax.all_to_all(pieces, axes, 0, 0).astype(f32), axis=0)


def per_device(momentum, q_basis):
    rows, cols = momentum.shape
    half = cols // 2
    shard_rank = q_basis.shape[0]
    rank = shard_rank * NZ * NY * 2
    core, at_x, at_y = lax.axis_index("c"), lax.axis_index("x"), lax.axis_index("y")
    position = (lax.axis_index("z") * NY + at_y) * 2 + core
    at = jnp.stack([at_y, core, at_x, position * shard_rank]).astype(jnp.int32)

    def columns(array, of_core):
        return lax.dynamic_slice_in_dim(array, of_core * half, half, 1)

    basis_half = q_basis.astype(bf16)
    basis_own = columns(basis_half, core)
    basis_other = swap_cores(columns(basis_half, 1 - core))
    basis_chip = jnp.concatenate(
        [jnp.where(core == 0, basis_own, basis_other), jnp.where(core == 0, basis_other, basis_own)]
    )
    later, basis_chip = lax.optimization_barrier((momentum, basis_chip))
    mine = columns(later, core)
    other = swap_cores(columns(later, 1 - core))

    basis_z = gather(basis_chip, "z", NZ).reshape(rank // NY, half)
    basis, other = ring_of_four(basis_z, "y", other)
    proj_mine, proj_other = project(at, mine, other, basis)
    projected = sum_four(proj_mine + swap_cores(proj_other), "x")

    gram_own = jnp.dot(projected.T, projected, preferred_element_type=f32, precision=HIGHEST)
    part = rank // (NX * 2)

    def gram_part(of_core):
        return lax.dynamic_slice_in_dim(gram_own, (at_x * 2 + of_core) * part, part, 0)

    gram_rows = sum_four(gram_part(core) + swap_cores(gram_part(1 - core)), "y")
    gram_rows = jnp.sum(gather(gram_rows, "z", NZ), axis=0)
    gram_chip = jnp.concatenate([gram_rows, swap_cores(gram_rows)])
    inverse = inverse_factor(
        at, [gram_chip] + [from_ahead(gram_chip, "x", by) for by in (1, 2, 3)]
    )

    crossed = cross(at, mine, other, projected, swap_cores(projected))
    right = crossed[0] + sum(from_ahead(crossed[by], "y", NY - by) for by in (1, 2, 3))

    def whiten(array):
        return lax.dot_general(
            array, inverse, BOTH_LAST, preferred_element_type=f32, precision=HIGHEST
        )

    solved = whiten(projected)
    right = scatter_sum(whiten(right).astype(bf16), "z", NZ).astype(bf16)
    right = gather(right, "z", NZ).reshape(half // NY, rank)
    squares = jnp.sum(jnp.square(right.astype(f32)), axis=0, keepdims=True)
    squares = gather(squares, ("y", "c", "x"), NY * 2 * NX).reshape(NY * 2 * NX, rank)
    pieces, squares = ring_of_four(right, "y", squares)
    pieces = pieces + tuple(swap_cores(piece) for piece in pieces)

    total_rows = rows * NZ * NY * 2
    total_cols = cols * NX
    scaling = math.sqrt(total_rows * total_cols / rank)
    return tuple(finish(at, momentum, solved, squares, pieces, scaling, shard_rank))


def solution(mesh):
    split = Mesh(mesh.devices.reshape(NZ, NY, 2, NX), ("z", "y", "c", "x"))
    spec = P(("z", "y", "c"), "x")
    return jax.shard_map(
        per_device,
        mesh=split,
        in_specs=(spec, spec),
        out_specs=(spec, spec, spec),
        check_vma=False,
    )
```

```python
import math

import jax
import jax.numpy as jnp
from jax import lax
from jax.experimental import pallas as pl
from jax.experimental.pallas import tpu as pltpu
from jax.sharding import Mesh
from jax.sharding import PartitionSpec as P

momentum_decay = 0.95
f32, bf16 = jnp.float32, jnp.bfloat16
HIGHEST = lax.Precision.HIGHEST
VMEM = pl.BlockSpec(memory_space=pltpu.VMEM)
SMEM = pl.BlockSpec(memory_space=pltpu.SMEM)
ANY = pl.BlockSpec(memory_space=pl.ANY)
BOTH_LAST = (((1,), (1,)), ((), ()))
BOTH_FIRST = (((0,), (0,)), ((), ()))
MIB = 2**20
NZ, NY, NX = 8, 4, 4
PIVOTS = 8
RING_FROM = (0, 1, 3, 2, 2)
AT_Y, AT_CORE, AT_X, FIRST_RANK = range(4)


def ahead(index, by, parts):
    return lax.rem(index + by, parts)


def inverse_factor_kernel(at_ref, own_ref, next_ref, across_ref, last_ref, inverse_ref, work_ref, half_ref, done_ref):
    rank = work_ref.shape[0]
    part = rank // (NX * 2)
    for by, ref in enumerate((own_ref, next_ref, across_ref, last_ref)):
        base = ahead(at_ref[AT_X], by, NX) * 2
        for other in range(2):
            at_core = (at_ref[AT_CORE] + other) % 2
            start = pl.multiple_of((base + at_core) * part, part)
            work_ref[pl.ds(start, part), :] = ref[other * part : (other + 1) * part, :]
    gram = work_ref[...]
    diagonal = lax.broadcasted_iota(jnp.int32, gram.shape, 0) == lax.broadcasted_iota(
        jnp.int32, gram.shape, 1
    )
    ridge = 0.001 * jnp.sum(jnp.where(diagonal, gram, 0.0)) / rank
    work_ref[...] = jnp.where(diagonal, gram + ridge, gram)
    lane = lax.broadcasted_iota(jnp.int32, (1, rank), 1)
    per_y, per_half = NZ * PIVOTS, NZ * PIVOTS // 2
    half = rank // 2
    order = (lane % per_y) // PIVOTS * (NY * PIVOTS) + lane // per_y * PIVOTS + lane % PIVOTS

    def of_half(array, second):
        starts = [y * per_y + second * per_half for y in range(NY)]
        return jnp.concatenate([array[start : start + per_half] for start in starts], axis=0)

    half_ref[...] = of_half(work_ref[...], 0)

    def wide(value):
        return jnp.concatenate([value] * (rank // 128), axis=1)

    steps = range(PIVOTS)

    def eliminate(second, carry):
        for group in range(half // PIVOTS):
            at_z, at_y = divmod(group, NY)
            first_row = at_y * per_half + at_z * PIVOTS
            at = at_y * per_y + at_z * PIVOTS
            block = half_ref[first_row : first_row + PIVOTS, :]
            spread = [jnp.broadcast_to(block[:, at + t : at + t + 1], (PIVOTS, 128)) for t in steps]
            core = [[spread[t][s : s + 1, :] for t in range(s + 1)] for s in steps]
            inside = (lane >= at) & (lane < at + PIVOTS)
            row = [jnp.where(inside, (lane == at + s).astype(f32), block[s : s + 1, :]) for s in steps]
            inverse = [None] * PIVOTS
            ratio = [[None] * PIVOTS for _ in steps]
            for t in steps:
                inverse[t] = 1.0 / core[t][t]
                for s in range(t + 1, PIVOTS):
                    ratio[s][t] = core[s][t] * inverse[t]
                for s in range(t + 1, PIVOTS):
                    for u in range(t + 1, s + 1):
                        core[s][u] = core[s][u] - ratio[s][t] * core[u][t]
                    row[s] = row[s] - wide(ratio[s][t]) * row[t]
            for s in steps:
                done_ref[group * PIVOTS + s : group * PIVOTS + s + 1, :] = row[s] * wide(
                    lax.rsqrt(core[s][s])
                )
            solved = [row[s] * wide(inverse[s]) for s in steps]
            for s in reversed(steps):
                for t in range(s):
                    solved[t] = solved[t] - wide(ratio[s][t]) * solved[s]
            for y in range(NY):
                next_z = at_z + (0 if y > at_y else 1)
                if next_z == NZ // 2:
                    continue
                rows = slice(y * per_half + next_z * PIVOTS, (y + 1) * per_half)
                below = half_ref[rows, :]
                rest = jnp.where(inside, 0.0, below)
                for t in steps:
                    rest = rest - below[:, at + t : at + t + 1] * solved[t]
                half_ref[rows, :] = rest

        @pl.when(second == 0)
        def _():
            done = done_ref[...]
            lower = order <= lax.broadcasted_iota(jnp.int32, (half, rank), 0)
            inverse_ref[:half, :] = jnp.where(lower, done, 0.0)
            done = jnp.where(lower | (order >= half), done, 0.0)
            product = lax.dot_general(
                done, done, BOTH_FIRST, preferred_element_type=f32, precision=HIGHEST
            )
            rest = jnp.where(order < half, 0.0, of_half(work_ref[...], 1)) - of_half(product, 1)
            half_ref[...] = pltpu.roll(rest, rank - per_half, 1)

        @pl.when(second == 1)
        def _():
            inverse_ref[half:, :] = jnp.where(
                order <= lax.broadcasted_iota(jnp.int32, (half, rank), 0) + half,
                pltpu.roll(done_ref[...], per_half, 1),
                0.0,
            )

        return carry

    lax.fori_loop(0, 2, eliminate, 0)


def inverse_factor(at, pieces):
    rank = pieces[0].shape[1]
    return pl.pallas_call(
        inverse_factor_kernel,
        out_shape=jax.ShapeDtypeStruct((rank, rank), f32),
        in_specs=[SMEM] + [VMEM] * 4,
        out_specs=VMEM,
        scratch_shapes=[pltpu.VMEM((rows, rank), f32) for rows in (rank, rank // 2, rank // 2)],
        compiler_params=pltpu.CompilerParams(vmem_limit_bytes=8 * MIB),
    )(at, *pieces)


def project_kernel(at_ref, mine_ref, other_ref, *refs):
    pieces, (out_mine_ref, out_other_ref, basis_ref) = refs[:5], refs[5:]
    per_y = pieces[0].shape[0]
    for n, ref in enumerate(pieces):
        size = ref.shape[0]
        start = ahead(at_ref[AT_Y], RING_FROM[n], NY) * per_y + (size if n == 4 else 0)
        basis_ref[pl.ds(pl.multiple_of(start, size), size), :] = ref[...]
    width = mine_ref.shape[1] // 2
    out_mine_ref[...] = jnp.zeros_like(out_mine_ref)
    out_other_ref[...] = jnp.zeros_like(out_other_ref)

    def add(step, carry):
        columns = pl.ds(pl.multiple_of(step * width, 128), width)
        basis = basis_ref[:, columns]
        for ref, out_ref in ((mine_ref, out_mine_ref), (other_ref, out_other_ref)):
            out_ref[...] += lax.dot_general(
                ref[:, columns], basis, BOTH_LAST, preferred_element_type=f32
            )
        return carry

    lax.fori_loop(0, 2, add, 0)


def project(at, mine, other, pieces):
    rows, cols = mine.shape
    rank = pieces[0].shape[0] * NY
    return pl.pallas_call(
        project_kernel,
        out_shape=[jax.ShapeDtypeStruct((rows, rank), f32)] * 2,
        in_specs=[SMEM] + [VMEM] * 7,
        out_specs=[VMEM, VMEM],
        scratch_shapes=[pltpu.VMEM((rank, cols), bf16)],
        compiler_params=pltpu.CompilerParams(vmem_limit_bytes=12 * MIB),
        cost_estimate=pl.CostEstimate(
            flops=4 * rows * cols * rank, bytes_accessed=6 * rows * cols, transcendentals=0
        ),
    )(at, mine, other, *pieces)


def cross_kernel(at_ref, mine_ref, other_ref, left_mine_ref, left_other_ref, *refs):
    pieces, (terms_ref, whole_ref) = refs[:NY], refs[NY:]
    rows, rank = left_mine_ref.shape
    for n, ref in enumerate((left_mine_ref, left_other_ref)):
        left = ref[...]
        for t in range(3):
            term = left.astype(bf16)
            terms_ref[n * rows : (n + 1) * rows, t * rank : (t + 1) * rank] = term
            left = left - term.astype(f32)
    width = mine_ref.shape[1] // 2

    def multiply(step, carry):
        columns = pl.ds(pl.multiple_of(step * width, 128), width)
        momentum = jnp.concatenate([mine_ref[:, columns], other_ref[:, columns]], axis=0)
        product = lax.dot_general(momentum, terms_ref[...], BOTH_FIRST, preferred_element_type=f32)
        total = (product[:, 2 * rank :] + product[:, rank : 2 * rank]) + product[:, :rank]
        whole_ref[columns, :] = total
        return carry

    lax.fori_loop(0, 2, multiply, 0)
    size = pieces[0].shape[0]
    for by, ref in enumerate(pieces):
        start = pl.multiple_of(ahead(at_ref[AT_Y], by, NY) * size, size)
        ref[...] = whole_ref[pl.ds(start, size), :]


def cross(at, mine, other, left_mine, left_other):
    rows, cols = mine.shape
    rank = left_mine.shape[1]
    return pl.pallas_call(
        cross_kernel,
        out_shape=[jax.ShapeDtypeStruct((cols // NY, rank), f32)] * NY,
        in_specs=[SMEM] + [VMEM] * 4,
        out_specs=[VMEM] * NY,
        scratch_shapes=[pltpu.VMEM((2 * rows, 3 * rank), bf16), pltpu.VMEM((cols, rank), f32)],
        compiler_params=pltpu.CompilerParams(vmem_limit_bytes=16 * MIB),
        cost_estimate=pl.CostEstimate(
            flops=12 * rows * cols * rank, bytes_accessed=4 * rows * cols + 8 * cols * rank, transcendentals=0
        ),
    )(at, mine, other, left_mine, left_other)


def finish_kernel(scaling, at_ref, momentum_ref, solved_ref, squares_ref, *refs):
    pieces = refs[:10]
    new_momentum_ref, update_ref, q_next_ref, right_ref, left_ref, inverse_ref, semaphores = refs[10:]
    rows, rank = solved_ref.shape
    step = pl.program_id(0)
    width = momentum_ref.shape[1]
    shard_rank = q_next_ref.shape[0]
    size = pieces[0].shape[0]

    @pl.when(step == 0)
    def _():
        copies = []
        for n, ref in enumerate(pieces):
            side = at_ref[AT_CORE] if n < 5 else 1 - at_ref[AT_CORE]
            start = (side * NY + ahead(at_ref[AT_Y], RING_FROM[n % 5], NY)) * size
            start = pl.multiple_of(start + (ref.shape[0] if n % 5 == 4 else 0), 16)
            copy = pltpu.make_async_copy(
                ref, right_ref.at[pl.ds(start, ref.shape[0]), :], semaphores.at[n]
            )
            copy.start()
            copies.append(copy)
        solved = solved_ref[...]
        squares = jnp.sum(squares_ref[...], axis=0, keepdims=True)
        inverse_lengths = lax.rsqrt(squares + 1e-06)
        left_ref[:rows, :] = solved.astype(bf16)
        left_ref[rows : 2 * rows, :] = (solved * (scaling * inverse_lengths)).astype(bf16)
        wanted = lax.broadcasted_iota(jnp.int32, (16, rank), 0) + at_ref[FIRST_RANK]
        picked = jnp.where(wanted == lax.broadcasted_iota(jnp.int32, (16, rank), 1), 1.0, 0.0)
        left_ref[2 * rows :, :] = picked.astype(bf16)
        own = jnp.sum(picked * inverse_lengths, axis=1, keepdims=True)
        inverse_ref[...] = jnp.broadcast_to(own, inverse_ref.shape)
        for copy in copies:
            copy.wait()

    right = right_ref[pl.ds(pl.multiple_of(step * width, width), width), :]
    product = lax.dot_general(left_ref[...], right, BOTH_LAST, preferred_element_type=f32)
    momentum = momentum_ref[...].astype(f32)
    new_momentum_ref[...] = (momentum - (1.0 - momentum_decay) * product[:rows]).astype(bf16)
    update_ref[...] = product[rows : 2 * rows].astype(bf16)
    q_next_ref[...] = (
        product[2 * rows : 2 * rows + shard_rank] * inverse_ref[:shard_rank, :1]
    )


def finish(at, momentum, solved, squares, pieces, scaling, shard_rank):
    rows, cols = momentum.shape
    rank = solved.shape[1]
    width = cols // 4
    columns = pl.BlockSpec((rows, width), lambda i: (0, i))
    out = jax.ShapeDtypeStruct((rows, cols), bf16)
    return pl.pallas_call(
        lambda *refs: finish_kernel(scaling, *refs),
        out_shape=[out, out, jax.ShapeDtypeStruct((shard_rank, cols), f32)],
        grid=(4,),
        in_specs=[
            SMEM,
            columns,
            pl.BlockSpec(solved.shape, lambda i: (0, 0)),
            pl.BlockSpec(squares.shape, lambda i: (0, 0)),
        ]
        + [ANY] * 10,
        out_specs=[columns, columns, pl.BlockSpec((shard_rank, width), lambda i: (0, i))],
        scratch_shapes=[
            pltpu.VMEM((cols, rank), bf16),
            pltpu.VMEM((2 * rows + 16, rank), bf16),
            pltpu.VMEM((16, 128), f32),
            pltpu.SemaphoreType.DMA((10,)),
        ],
        compiler_params=pltpu.CompilerParams(vmem_limit_bytes=20 * MIB),
        cost_estimate=pl.CostEstimate(
            flops=4 * rows * cols * rank, bytes_accessed=8 * rows * cols, transcendentals=0
        ),
    )(at, momentum, solved, squares, *pieces)


def swap_cores(block):
    return lax.ppermute(block, "c", [(0, 1), (1, 0)])


def from_ahead(block, axis, by, parts=4):
    return lax.ppermute(block, axis, [((i + by) % parts, i) for i in range(parts)])


def sum_four(block, axis):
    one, two, three = (from_ahead(block, axis, by) for by in (1, 2, 3))
    return (block + two) + (one + three)


def ring_of_four(block, axis, beside=None):
    middle = block.shape[0] // 2
    one, three = from_ahead(block, axis, 1), from_ahead(block, axis, 3)
    one, three, beside = lax.optimization_barrier((one, three, beside))
    across = (from_ahead(three[:middle], axis, 3), from_ahead(one[middle:], axis, 1))
    return (block, one, three) + across, beside


def gather(block, axes, parts):
    copies = jnp.broadcast_to(block[None], (parts,) + block.shape)
    return lax.all_to_all(copies, axes, 0, 0)


def scatter_sum(block, axes, parts):
    pieces = block.reshape((parts, block.shape[0] // parts) + block.shape[1:])
    return jnp.sum(lax.all_to_all(pieces, axes, 0, 0).astype(f32), axis=0)


def per_device(momentum, q_basis):
    rows, cols = momentum.shape
    half = cols // 2
    shard_rank = q_basis.shape[0]
    rank = shard_rank * NZ * NY * 2
    core, at_x, at_y = lax.axis_index("c"), lax.axis_index("x"), lax.axis_index("y")
    position = (lax.axis_index("z") * NY + at_y) * 2 + core
    at = jnp.stack([at_y, core, at_x, position * shard_rank]).astype(jnp.int32)

    def columns(array, of_core):
        return lax.dynamic_slice_in_dim(array, of_core * half, half, 1)

    basis_half = q_basis.astype(bf16)
    basis_own = columns(basis_half, core)
    basis_other = swap_cores(columns(basis_half, 1 - core))
    basis_chip = jnp.concatenate(
        [jnp.where(core == 0, basis_own, basis_other), jnp.where(core == 0, basis_other, basis_own)]
    )
    later, basis_chip = lax.optimization_barrier((momentum, basis_chip))
    mine = columns(later, core)
    other = swap_cores(columns(later, 1 - core))

    basis_z = gather(basis_chip, "z", NZ).reshape(rank // NY, half)
    basis, other = ring_of_four(basis_z, "y", other)
    proj_mine, proj_other = project(at, mine, other, basis)
    projected = sum_four(proj_mine + swap_cores(proj_other), "x")

    gram_own = jnp.dot(projected.T, projected, preferred_element_type=f32, precision=HIGHEST)
    part = rank // (NX * 2)

    def gram_part(of_core):
        return lax.dynamic_slice_in_dim(gram_own, (at_x * 2 + of_core) * part, part, 0)

    gram_rows = sum_four(gram_part(core) + swap_cores(gram_part(1 - core)), "y")
    gram_rows = jnp.sum(gather(gram_rows, "z", NZ), axis=0)
    gram_chip = jnp.concatenate([gram_rows, swap_cores(gram_rows)])
    inverse = inverse_factor(
        at, [gram_chip] + [from_ahead(gram_chip, "x", by) for by in (1, 2, 3)]
    )

    crossed = cross(at, mine, other, projected, swap_cores(projected))
    right = crossed[0] + sum(from_ahead(crossed[by], "y", NY - by) for by in (1, 2, 3))

    def whiten(array):
        return lax.dot_general(
            array, inverse, BOTH_LAST, preferred_element_type=f32, precision=HIGHEST
        )

    solved = whiten(projected)
    right = scatter_sum(whiten(right).astype(bf16), "z", NZ).astype(bf16)
    right = gather(right, "z", NZ).reshape(half // NY, rank)
    squares = jnp.sum(jnp.square(right.astype(f32)), axis=0, keepdims=True)
    squares = gather(squares, ("y", "c", "x"), NY * 2 * NX).reshape(NY * 2 * NX, rank)
    pieces, squares = ring_of_four(right, "y", squares)
    pieces = pieces + tuple(swap_cores(piece) for piece in pieces)

    total_rows = rows * NZ * NY * 2
    total_cols = cols * NX
    scaling = math.sqrt(total_rows * total_cols / rank)
    return tuple(finish(at, momentum, solved, squares, pieces, scaling, shard_rank))


def solution(mesh):
    split = Mesh(mesh.devices.reshape(NZ, NY, 2, NX), ("z", "y", "c", "x"))
    spec = P(("z", "y", "c"), "x")
    return jax.shard_map(
        per_device,
        mesh=split,
        in_specs=(spec, spec),
        out_specs=(spec, spec, spec),
        check_vma=False,
    )
```

```python
import math

import jax
import jax.numpy as jnp
from jax import lax
from jax.experimental import pallas as pl
from jax.experimental.pallas import tpu as pltpu
from jax.sharding import Mesh
from jax.sharding import PartitionSpec as P

momentum_decay = 0.95
f32, bf16 = jnp.float32, jnp.bfloat16
HIGHEST = lax.Precision.HIGHEST
VMEM = pl.BlockSpec(memory_space=pltpu.VMEM)
SMEM = pl.BlockSpec(memory_space=pltpu.SMEM)
ANY = pl.BlockSpec(memory_space=pl.ANY)
BOTH_LAST = (((1,), (1,)), ((), ()))
BOTH_FIRST = (((0,), (0,)), ((), ()))
MIB = 2**20
NZ, NY, NX = 8, 4, 4
PIVOTS = 8
RING_FROM = (0, 1, 3, 2, 2)
AT_Y, AT_CORE, AT_X, FIRST_RANK = range(4)


def ahead(index, by, parts):
    return lax.rem(index + by, parts)


def inverse_factor_kernel(at_ref, own_ref, next_ref, across_ref, last_ref, inverse_ref, work_ref, half_ref, done_ref):
    rank = work_ref.shape[0]
    part = rank // (NX * 2)
    for by, ref in enumerate((own_ref, next_ref, across_ref, last_ref)):
        base = ahead(at_ref[AT_X], by, NX) * 2
        for other in range(2):
            at_core = (at_ref[AT_CORE] + other) % 2
            start = pl.multiple_of((base + at_core) * part, part)
            work_ref[pl.ds(start, part), :] = ref[other * part : (other + 1) * part, :]
    gram = work_ref[...]
    diagonal = lax.broadcasted_iota(jnp.int32, gram.shape, 0) == lax.broadcasted_iota(
        jnp.int32, gram.shape, 1
    )
    ridge = 0.001 * jnp.sum(jnp.where(diagonal, gram, 0.0)) / rank
    work_ref[...] = jnp.where(diagonal, gram + ridge, gram)
    lane = lax.broadcasted_iota(jnp.int32, (1, rank), 1)
    per_y, per_half = NZ * PIVOTS, NZ * PIVOTS // 2
    half = rank // 2
    order = (lane % per_y) // PIVOTS * (NY * PIVOTS) + lane // per_y * PIVOTS + lane % PIVOTS

    def of_half(array, second):
        starts = [y * per_y + second * per_half for y in range(NY)]
        return jnp.concatenate([array[start : start + per_half] for start in starts], axis=0)

    half_ref[...] = of_half(work_ref[...], 0)

    def wide(value):
        return jnp.concatenate([value] * (rank // 128), axis=1)

    steps = range(PIVOTS)

    def eliminate(second, carry):
        for group in range(half // PIVOTS):
            at_z, at_y = divmod(group, NY)
            first_row = at_y * per_half + at_z * PIVOTS
            at = at_y * per_y + at_z * PIVOTS
            block = half_ref[first_row : first_row + PIVOTS, :]
            spread = [jnp.broadcast_to(block[:, at + t : at + t + 1], (PIVOTS, 128)) for t in steps]
            core = [[spread[t][s : s + 1, :] for t in range(s + 1)] for s in steps]
            inside = (lane >= at) & (lane < at + PIVOTS)
            row = [jnp.where(inside, (lane == at + s).astype(f32), block[s : s + 1, :]) for s in steps]
            inverse = [None] * PIVOTS
            ratio = [[None] * PIVOTS for _ in steps]
            for t in steps:
                inverse[t] = 1.0 / core[t][t]
                for s in range(t + 1, PIVOTS):
                    ratio[s][t] = core[s][t] * inverse[t]
                for s in range(t + 1, PIVOTS):
                    for u in range(t + 1, s + 1):
                        core[s][u] = core[s][u] - ratio[s][t] * core[u][t]
                    row[s] = row[s] - wide(ratio[s][t]) * row[t]
            for s in steps:
                done_ref[group * PIVOTS + s : group * PIVOTS + s + 1, :] = row[s] * wide(
                    lax.rsqrt(core[s][s])
                )
            solved = [row[s] * wide(inverse[s]) for s in steps]
            for s in reversed(steps):
                for t in range(s):
                    solved[t] = solved[t] - wide(ratio[s][t]) * solved[s]
            for y in range(NY):
                next_z = at_z + (0 if y > at_y else 1)
                if next_z == NZ // 2:
                    continue
                rows = slice(y * per_half + next_z * PIVOTS, (y + 1) * per_half)
                below = half_ref[rows, :]
                rest = jnp.where(inside, 0.0, below)
                for t in steps:
                    rest = rest - below[:, at + t : at + t + 1] * solved[t]
                half_ref[rows, :] = rest

        @pl.when(second == 0)
        def _():
            done = done_ref[...]
            lower = order <= lax.broadcasted_iota(jnp.int32, (half, rank), 0)
            inverse_ref[:half, :] = jnp.where(lower, done, 0.0)
            done = jnp.where(lower | (order >= half), done, 0.0)
            product = lax.dot_general(
                done, done, BOTH_FIRST, preferred_element_type=f32, precision=HIGHEST
            )
            rest = jnp.where(order < half, 0.0, of_half(work_ref[...], 1)) - of_half(product, 1)
            half_ref[...] = pltpu.roll(rest, rank - per_half, 1)

        @pl.when(second == 1)
        def _():
            inverse_ref[half:, :] = jnp.where(
                order <= lax.broadcasted_iota(jnp.int32, (half, rank), 0) + half,
                pltpu.roll(done_ref[...], per_half, 1),
                0.0,
            )

        return carry

    lax.fori_loop(0, 2, eliminate, 0)


def inverse_factor(at, pieces):
    rank = pieces[0].shape[1]
    return pl.pallas_call(
        inverse_factor_kernel,
        out_shape=jax.ShapeDtypeStruct((rank, rank), f32),
        in_specs=[SMEM] + [VMEM] * 4,
        out_specs=VMEM,
        scratch_shapes=[pltpu.VMEM((rows, rank), f32) for rows in (rank, rank // 2, rank // 2)],
        compiler_params=pltpu.CompilerParams(vmem_limit_bytes=8 * MIB),
    )(at, *pieces)


def core_half(rows, width):
    return pl.BlockSpec((rows, width), lambda i, at: (0, at[AT_CORE] * 2 + i))


def project_kernel(at_ref, mine_ref, other_ref, *refs):
    pieces, (out_mine_ref, out_other_ref, basis_ref) = refs[:NY], refs[NY:]
    for by, ref in enumerate(pieces):
        size = ref.shape[0]
        start = pl.multiple_of(ahead(at_ref[AT_Y], by, NY) * size, size)
        basis_ref[pl.ds(start, size), :] = ref[...]
    basis = basis_ref[...]
    product_mine = lax.dot_general(mine_ref[...], basis, BOTH_LAST, preferred_element_type=f32)
    product_other = lax.dot_general(other_ref[...], basis, BOTH_LAST, preferred_element_type=f32)
    first = pl.program_id(0) == 0

    @pl.when(first)
    def _():
        out_mine_ref[...] = product_mine
        out_other_ref[...] = product_other

    @pl.when(jnp.logical_not(first))
    def _():
        out_mine_ref[...] += product_mine
        out_other_ref[...] += product_other


def project(at, mine, other, pieces):
    rows, cols = mine.shape
    rank = pieces[0].shape[0] * NY
    width = cols // 4
    whole = pl.BlockSpec((rows, rank), lambda i, at: (0, 0))
    piece = pl.BlockSpec((rank // NY, width), lambda i, at: (0, i))
    return pl.pallas_call(
        project_kernel,
        out_shape=[jax.ShapeDtypeStruct((rows, rank), f32)] * 2,
        grid_spec=pltpu.PrefetchScalarGridSpec(
            num_scalar_prefetch=1,
            grid=(2,),
            in_specs=[core_half(rows, width), core_half(rows, width)] + [piece] * NY,
            out_specs=[whole, whole],
            scratch_shapes=[pltpu.VMEM((rank, width), bf16)],
        ),
        compiler_params=pltpu.CompilerParams(vmem_limit_bytes=14 * MIB),
        cost_estimate=pl.CostEstimate(
            flops=2 * rows * cols * rank, bytes_accessed=3 * rows * cols, transcendentals=0
        ),
    )(at, mine, other, *pieces)


def gram_kernel(at_ref, own_ref, one_ref, two_ref, three_ref, projected_ref, keep_ref, send_ref, gram_ref):
    projected = (own_ref[...] + two_ref[...]) + (one_ref[...] + three_ref[...])
    projected_ref[...] = projected
    gram_ref[...] = lax.dot_general(
        projected, projected, BOTH_FIRST, preferred_element_type=f32, precision=HIGHEST
    )
    part = keep_ref.shape[0]
    for other, ref in enumerate((keep_ref, send_ref)):
        place = at_ref[AT_X] * 2 + (at_ref[AT_CORE] + other) % 2
        ref[...] = gram_ref[pl.ds(pl.multiple_of(place * part, part), part), :]


def gram_rows_of(at, pieces):
    rows, rank = pieces[0].shape
    part = jax.ShapeDtypeStruct((rank // (NX * 2), rank), f32)
    return pl.pallas_call(
        gram_kernel,
        out_shape=[jax.ShapeDtypeStruct((rows, rank), f32), part, part],
        in_specs=[SMEM] + [VMEM] * 4,
        out_specs=[VMEM] * 3,
        scratch_shapes=[pltpu.VMEM((rank, rank), f32)],
        compiler_params=pltpu.CompilerParams(vmem_limit_bytes=8 * MIB),
    )(at, *pieces)


def cross_kernel(at_ref, mine_ref, other_ref, left_mine_ref, left_other_ref, *refs):
    pieces, (terms_ref, whole_ref) = refs[:NY], refs[NY:]
    rows, rank = left_mine_ref.shape
    step = pl.program_id(0)
    width = mine_ref.shape[1]

    @pl.when(step == 0)
    def _():
        for n, ref in enumerate((left_mine_ref, left_other_ref)):
            left = ref[...]
            for t in range(3):
                term = left.astype(bf16)
                terms_ref[n * rows : (n + 1) * rows, t * rank : (t + 1) * rank] = term
                left = left - term.astype(f32)

    momentum = jnp.concatenate([mine_ref[...], other_ref[...]], axis=0)
    product = lax.dot_general(momentum, terms_ref[...], BOTH_FIRST, preferred_element_type=f32)
    total = (product[:, 2 * rank :] + product[:, rank : 2 * rank]) + product[:, :rank]
    whole_ref[pl.ds(pl.multiple_of(step * width, 128), width), :] = total

    @pl.when(step == pl.num_programs(0) - 1)
    def _():
        size = pieces[0].shape[0]
        for by, ref in enumerate(pieces):
            start = pl.multiple_of(ahead(at_ref[AT_Y], by, NY) * size, size)
            ref[...] = whole_ref[pl.ds(start, size), :]


def cross(at, mine, other, left_mine, left_other):
    rows, cols = mine.shape
    rank = left_mine.shape[1]
    half = cols // 2
    width, size = half // 2, half // NY
    left = pl.BlockSpec((rows, rank), lambda i, at: (0, 0))
    piece = pl.BlockSpec((size, rank), lambda i, at: (0, 0))
    return pl.pallas_call(
        cross_kernel,
        out_shape=[jax.ShapeDtypeStruct((size, rank), f32)] * NY,
        grid_spec=pltpu.PrefetchScalarGridSpec(
            num_scalar_prefetch=1,
            grid=(2,),
            in_specs=[core_half(rows, width), core_half(rows, width), left, left],
            out_specs=[piece] * NY,
            scratch_shapes=[pltpu.VMEM((2 * rows, 3 * rank), bf16), pltpu.VMEM((half, rank), f32)],
        ),
        compiler_params=pltpu.CompilerParams(vmem_limit_bytes=26 * MIB),
        cost_estimate=pl.CostEstimate(
            flops=6 * rows * cols * rank, bytes_accessed=2 * rows * cols + 4 * cols * rank, transcendentals=0
        ),
    )(at, mine, other, left_mine, left_other)


def finish_kernel(scaling, at_ref, momentum_ref, solved_ref, squares_ref, *refs):
    pieces = refs[:10]
    new_momentum_ref, update_ref, q_next_ref, right_ref, left_ref, inverse_ref, semaphores = refs[10:]
    rows, rank = solved_ref.shape
    step = pl.program_id(0)
    width = momentum_ref.shape[1]
    shard_rank = q_next_ref.shape[0]
    size = pieces[0].shape[0]

    @pl.when(step == 0)
    def _():
        copies = []
        for n, ref in enumerate(pieces):
            side = at_ref[AT_CORE] if n < 5 else 1 - at_ref[AT_CORE]
            start = (side * NY + ahead(at_ref[AT_Y], RING_FROM[n % 5], NY)) * size
            start = pl.multiple_of(start + (ref.shape[0] if n % 5 == 4 else 0), 16)
            copy = pltpu.make_async_copy(
                ref, right_ref.at[pl.ds(start, ref.shape[0]), :], semaphores.at[n]
            )
            copy.start()
            copies.append(copy)
        solved = solved_ref[...]
        squares = jnp.sum(squares_ref[...], axis=0, keepdims=True)
        inverse_lengths = lax.rsqrt(squares + 1e-06)
        left_ref[:rows, :] = solved.astype(bf16)
        left_ref[rows : 2 * rows, :] = (solved * (scaling * inverse_lengths)).astype(bf16)
        wanted = lax.broadcasted_iota(jnp.int32, (16, rank), 0) + at_ref[FIRST_RANK]
        picked = jnp.where(wanted == lax.broadcasted_iota(jnp.int32, (16, rank), 1), 1.0, 0.0)
        left_ref[2 * rows :, :] = picked.astype(bf16)
        own = jnp.sum(picked * inverse_lengths, axis=1, keepdims=True)
        inverse_ref[...] = jnp.broadcast_to(own, inverse_ref.shape)
        for copy in copies:
            copy.wait()

    right = right_ref[pl.ds(pl.multiple_of(step * width, width), width), :]
    product = lax.dot_general(left_ref[...], right, BOTH_LAST, preferred_element_type=f32)
    momentum = momentum_ref[...].astype(f32)
    new_momentum_ref[...] = (momentum - (1.0 - momentum_decay) * product[:rows]).astype(bf16)
    update_ref[...] = product[rows : 2 * rows].astype(bf16)
    q_next_ref[...] = (
        product[2 * rows : 2 * rows + shard_rank] * inverse_ref[:shard_rank, :1]
    )


def finish(at, momentum, solved, squares, pieces, scaling, shard_rank):
    rows, cols = momentum.shape
    rank = solved.shape[1]
    width = cols // 4
    columns = pl.BlockSpec((rows, width), lambda i: (0, i))
    out = jax.ShapeDtypeStruct((rows, cols), bf16)
    return pl.pallas_call(
        lambda *refs: finish_kernel(scaling, *refs),
        out_shape=[out, out, jax.ShapeDtypeStruct((shard_rank, cols), f32)],
        grid=(4,),
        in_specs=[
            SMEM,
            columns,
            pl.BlockSpec(solved.shape, lambda i: (0, 0)),
            pl.BlockSpec(squares.shape, lambda i: (0, 0)),
        ]
        + [ANY] * 10,
        out_specs=[columns, columns, pl.BlockSpec((shard_rank, width), lambda i: (0, i))],
        scratch_shapes=[
            pltpu.VMEM((cols, rank), bf16),
            pltpu.VMEM((2 * rows + 16, rank), bf16),
            pltpu.VMEM((16, 128), f32),
            pltpu.SemaphoreType.DMA((10,)),
        ],
        compiler_params=pltpu.CompilerParams(vmem_limit_bytes=20 * MIB),
        cost_estimate=pl.CostEstimate(
            flops=4 * rows * cols * rank, bytes_accessed=8 * rows * cols, transcendentals=0
        ),
    )(at, momentum, solved, squares, *pieces)


def swap_cores(block):
    return lax.ppermute(block, "c", [(0, 1), (1, 0)])


def from_ahead(block, axis, by, parts=4):
    return lax.ppermute(block, axis, [((i + by) % parts, i) for i in range(parts)])


def all_of_four(block, axis):
    return [block] + [from_ahead(block, axis, by) for by in (1, 2, 3)]


def sum_four(block, axis):
    own, one, two, three = all_of_four(block, axis)
    return (own + two) + (one + three)


def ring_of_four(block, axis, beside):
    middle = block.shape[0] // 2
    one, three = from_ahead(block, axis, 1), from_ahead(block, axis, 3)
    one, three, beside = lax.optimization_barrier((one, three, beside))
    across = (from_ahead(three[:middle], axis, 3), from_ahead(one[middle:], axis, 1))
    return (block, one, three) + across, beside


def gather(block, axes, parts):
    copies = jnp.broadcast_to(block[None], (parts,) + block.shape)
    return lax.all_to_all(copies, axes, 0, 0)


def scatter_sum(block, axes, parts):
    pieces = block.reshape((parts, block.shape[0] // parts) + block.shape[1:])
    return jnp.sum(lax.all_to_all(pieces, axes, 0, 0).astype(f32), axis=0)


def per_device(momentum, q_basis):
    rows, cols = momentum.shape
    half = cols // 2
    shard_rank = q_basis.shape[0]
    rank = shard_rank * NZ * NY * 2
    core, at_x, at_y = lax.axis_index("c"), lax.axis_index("x"), lax.axis_index("y")
    position = (lax.axis_index("z") * NY + at_y) * 2 + core
    at = jnp.stack([at_y, core, at_x, position * shard_rank]).astype(jnp.int32)

    def columns(array, of_core):
        return lax.dynamic_slice_in_dim(array, of_core * half, half, 1)

    momentum_other = swap_cores(momentum)
    basis_half = q_basis.astype(bf16)
    basis_own = columns(basis_half, core)
    basis_other = swap_cores(columns(basis_half, 1 - core))
    basis_chip = jnp.concatenate(
        [jnp.where(core == 0, basis_own, basis_other), jnp.where(core == 0, basis_other, basis_own)]
    )
    basis_z = gather(basis_chip, "z", NZ).reshape(rank // NY, half)
    basis = all_of_four(basis_z, "y")
    proj_mine, proj_other = project(at, momentum, momentum_other, basis)
    projected, gram_keep, gram_send = gram_rows_of(
        at, all_of_four(proj_mine + swap_cores(proj_other), "x")
    )
    gram_rows = sum_four(gram_keep + swap_cores(gram_send), "y")
    gram_rows = jnp.sum(gather(gram_rows, "z", NZ), axis=0)
    gram_chip = jnp.concatenate([gram_rows, swap_cores(gram_rows)])
    inverse = inverse_factor(at, all_of_four(gram_chip, "x"))

    crossed = cross(at, momentum, momentum_other, projected, swap_cores(projected))
    right = crossed[0] + sum(from_ahead(crossed[by], "y", NY - by) for by in (1, 2, 3))

    def whiten(array):
        return lax.dot_general(
            array, inverse, BOTH_LAST, preferred_element_type=f32, precision=HIGHEST
        )

    solved = whiten(projected)
    right = scatter_sum(whiten(right).astype(bf16), "z", NZ).astype(bf16)
    right = gather(right, "z", NZ).reshape(half // NY, rank)
    squares = jnp.sum(jnp.square(right.astype(f32)), axis=0, keepdims=True)
    squares = gather(squares, ("y", "c", "x"), NY * 2 * NX).reshape(NY * 2 * NX, rank)
    pieces, (squares, swapped) = ring_of_four(right, "y", (squares, swap_cores(right)))
    pieces = pieces + (swapped,) + tuple(swap_cores(piece) for piece in pieces[1:])

    total_rows = rows * NZ * NY * 2
    total_cols = cols * NX
    scaling = math.sqrt(total_rows * total_cols / rank)
    return tuple(finish(at, momentum, solved, squares, pieces, scaling, shard_rank))


def solution(mesh):
    split = Mesh(mesh.devices.reshape(NZ, NY, 2, NX), ("z", "y", "c", "x"))
    spec = P(("z", "y", "c"), "x")
    return jax.shard_map(
        per_device,
        mesh=split,
        in_specs=(spec, spec),
        out_specs=(spec, spec, spec),
        check_vma=False,
    )
```

```python
import math

import jax
import jax.numpy as jnp
from jax import lax
from jax.experimental import pallas as pl
from jax.experimental.pallas import tpu as pltpu
from jax.sharding import Mesh
from jax.sharding import PartitionSpec as P

momentum_decay = 0.95
f32, bf16 = jnp.float32, jnp.bfloat16
HIGHEST = lax.Precision.HIGHEST
VMEM = pl.BlockSpec(memory_space=pltpu.VMEM)
SMEM = pl.BlockSpec(memory_space=pltpu.SMEM)
ANY = pl.BlockSpec(memory_space=pl.ANY)
BOTH_LAST = (((1,), (1,)), ((), ()))
BOTH_FIRST = (((0,), (0,)), ((), ()))
MIB = 2**20
NZ, NY, NX = 8, 4, 4
PIVOTS = 8
RING_FROM = (0, 1, 3, 2, 2)
AT_Y, AT_CORE, AT_X, FIRST_RANK = range(4)


def ahead(index, by, parts):
    return lax.rem(index + by, parts)


def inverse_factor_kernel(at_ref, own_ref, next_ref, across_ref, last_ref, inverse_ref, work_ref, half_ref, done_ref):
    rank = work_ref.shape[0]
    part = rank // (NX * 2)
    for by, ref in enumerate((own_ref, next_ref, across_ref, last_ref)):
        base = ahead(at_ref[AT_X], by, NX) * 2
        for other in range(2):
            at_core = (at_ref[AT_CORE] + other) % 2
            start = pl.multiple_of((base + at_core) * part, part)
            work_ref[pl.ds(start, part), :] = ref[other * part : (other + 1) * part, :]
    gram = work_ref[...]
    diagonal = lax.broadcasted_iota(jnp.int32, gram.shape, 0) == lax.broadcasted_iota(
        jnp.int32, gram.shape, 1
    )
    ridge = 0.001 * jnp.sum(jnp.where(diagonal, gram, 0.0)) / rank
    work_ref[...] = jnp.where(diagonal, gram + ridge, gram)
    lane = lax.broadcasted_iota(jnp.int32, (1, rank), 1)
    per_y, per_half = NZ * PIVOTS, NZ * PIVOTS // 2
    half = rank // 2
    order = (lane % per_y) // PIVOTS * (NY * PIVOTS) + lane // per_y * PIVOTS + lane % PIVOTS

    def of_half(array, second):
        starts = [y * per_y + second * per_half for y in range(NY)]
        return jnp.concatenate([array[start : start + per_half] for start in starts], axis=0)

    half_ref[...] = of_half(work_ref[...], 0)

    def wide(value):
        return jnp.concatenate([value] * (rank // 128), axis=1)

    steps = range(PIVOTS)

    def eliminate(second, carry):
        for group in range(half // PIVOTS):
            at_z, at_y = divmod(group, NY)
            first_row = at_y * per_half + at_z * PIVOTS
            at = at_y * per_y + at_z * PIVOTS
            block = half_ref[first_row : first_row + PIVOTS, :]
            spread = [jnp.broadcast_to(block[:, at + t : at + t + 1], (PIVOTS, 128)) for t in steps]
            core = [[spread[t][s : s + 1, :] for t in range(s + 1)] for s in steps]
            inside = (lane >= at) & (lane < at + PIVOTS)
            row = [jnp.where(inside, (lane == at + s).astype(f32), block[s : s + 1, :]) for s in steps]
            inverse = [None] * PIVOTS
            ratio = [[None] * PIVOTS for _ in steps]
            for t in steps:
                inverse[t] = 1.0 / core[t][t]
                for s in range(t + 1, PIVOTS):
                    ratio[s][t] = core[s][t] * inverse[t]
                for s in range(t + 1, PIVOTS):
                    for u in range(t + 1, s + 1):
                        core[s][u] = core[s][u] - ratio[s][t] * core[u][t]
                    row[s] = row[s] - wide(ratio[s][t]) * row[t]
            for s in steps:
                done_ref[group * PIVOTS + s : group * PIVOTS + s + 1, :] = row[s] * wide(
                    lax.rsqrt(core[s][s])
                )
            solved = [row[s] * wide(inverse[s]) for s in steps]
            for s in reversed(steps):
                for t in range(s):
                    solved[t] = solved[t] - wide(ratio[s][t]) * solved[s]
            for y in range(NY):
                next_z = at_z + (0 if y > at_y else 1)
                if next_z == NZ // 2:
                    continue
                rows = slice(y * per_half + next_z * PIVOTS, (y + 1) * per_half)
                below = half_ref[rows, :]
                rest = jnp.where(inside, 0.0, below)
                for t in steps:
                    rest = rest - below[:, at + t : at + t + 1] * solved[t]
                half_ref[rows, :] = rest

        @pl.when(second == 0)
        def _():
            done = done_ref[...]
            lower = order <= lax.broadcasted_iota(jnp.int32, (half, rank), 0)
            inverse_ref[:half, :] = jnp.where(lower, done, 0.0)
            done = jnp.where(lower | (order >= half), done, 0.0)
            product = lax.dot_general(
                done, done, BOTH_FIRST, preferred_element_type=f32, precision=HIGHEST
            )
            rest = jnp.where(order < half, 0.0, of_half(work_ref[...], 1)) - of_half(product, 1)
            half_ref[...] = pltpu.roll(rest, rank - per_half, 1)

        @pl.when(second == 1)
        def _():
            inverse_ref[half:, :] = jnp.where(
                order <= lax.broadcasted_iota(jnp.int32, (half, rank), 0) + half,
                pltpu.roll(done_ref[...], per_half, 1),
                0.0,
            )

        return carry

    lax.fori_loop(0, 2, eliminate, 0)


def inverse_factor(at, pieces):
    rank = pieces[0].shape[1]
    return pl.pallas_call(
        inverse_factor_kernel,
        out_shape=jax.ShapeDtypeStruct((rank, rank), f32),
        in_specs=[SMEM] + [VMEM] * 4,
        out_specs=VMEM,
        scratch_shapes=[pltpu.VMEM((rows, rank), f32) for rows in (rank, rank // 2, rank // 2)],
        compiler_params=pltpu.CompilerParams(vmem_limit_bytes=8 * MIB),
        cost_estimate=pl.CostEstimate(flops=10**9, bytes_accessed=2**20, transcendentals=0),
    )(at, *pieces)


def project_kernel(at_ref, mine_ref, other_ref, *refs):
    pieces, (out_mine_ref, out_other_ref, basis_ref) = refs[:NY], refs[NY:]
    for by, ref in enumerate(pieces):
        size = ref.shape[0]
        start = pl.multiple_of(ahead(at_ref[AT_Y], by, NY) * size, size)
        basis_ref[pl.ds(start, size), :] = ref[...]
    width = mine_ref.shape[1] // 2
    out_mine_ref[...] = jnp.zeros_like(out_mine_ref)
    out_other_ref[...] = jnp.zeros_like(out_other_ref)

    def add(step, carry):
        columns = pl.ds(pl.multiple_of(step * width, 128), width)
        basis = basis_ref[:, columns]
        for ref, out_ref in ((mine_ref, out_mine_ref), (other_ref, out_other_ref)):
            out_ref[...] += lax.dot_general(
                ref[:, columns], basis, BOTH_LAST, preferred_element_type=f32
            )
        return carry

    lax.fori_loop(0, 2, add, 0)


def project(at, mine, other, pieces):
    rows, cols = mine.shape
    rank = pieces[0].shape[0] * NY
    return pl.pallas_call(
        project_kernel,
        out_shape=[jax.ShapeDtypeStruct((rows, rank), f32)] * 2,
        in_specs=[SMEM] + [VMEM] * 6,
        out_specs=[VMEM, VMEM],
        scratch_shapes=[pltpu.VMEM((rank, cols), bf16)],
        compiler_params=pltpu.CompilerParams(vmem_limit_bytes=12 * MIB),
        cost_estimate=pl.CostEstimate(
            flops=4 * rows * cols * rank, bytes_accessed=6 * rows * cols, transcendentals=0
        ),
    )(at, mine, other, *pieces)


def small(kernel, out, *args):
    specs = [SMEM if arg.dtype == jnp.int32 else VMEM for arg in args]
    return pl.pallas_call(
        kernel,
        out_shape=out,
        in_specs=specs,
        out_specs=VMEM,
        compiler_params=pltpu.CompilerParams(vmem_limit_bytes=8 * MIB),
        cost_estimate=pl.CostEstimate(flops=2**20, bytes_accessed=2**20, transcendentals=0),
    )(*args)


def add(one, two):
    def kernel(one_ref, two_ref, out_ref):
        out_ref[...] = one_ref[...] + two_ref[...]

    return small(kernel, jax.ShapeDtypeStruct(one.shape, f32), one, two)


def sum_four_copies(pieces, copies):
    def kernel(own_ref, one_ref, two_ref, three_ref, out_ref):
        total = (own_ref[...] + two_ref[...]) + (one_ref[...] + three_ref[...])
        for n in range(copies):
            out_ref[n] = total

    return small(kernel, jax.ShapeDtypeStruct((copies,) + pieces[0].shape, f32), *pieces)


def sum_copies(pieces, copies):
    def kernel(pieces_ref, out_ref):
        total = jnp.sum(pieces_ref[...].astype(f32), axis=0).astype(pieces_ref.dtype)
        for n in range(copies):
            out_ref[n] = total

    shape = (copies,) + pieces.shape[1:]
    return small(kernel, jax.ShapeDtypeStruct(shape, pieces.dtype), pieces)


def basis_copies(at, basis, received, copies):
    shard_rank, half = received.shape

    def kernel(at_ref, basis_ref, received_ref, out_ref):
        core = at_ref[AT_CORE]
        own = basis_ref[:, pl.ds(pl.multiple_of(core * half, half), half)]
        other = received_ref[...]
        first = jnp.where(core == 0, own, other)
        second = jnp.where(core == 0, other, own)
        chip = jnp.concatenate([first, second], axis=0).astype(bf16)
        for n in range(copies):
            out_ref[n] = chip

    return small(kernel, jax.ShapeDtypeStruct((copies, 2 * shard_rank, half), bf16), at, basis, received)


def square_copies(right, copies):
    rank = right.shape[1]

    def kernel(right_ref, out_ref):
        right = right_ref[...].astype(f32)
        out_ref[...] = jnp.broadcast_to(
            jnp.sum(right * right, axis=0, keepdims=True), out_ref.shape
        )

    return small(kernel, jax.ShapeDtypeStruct((copies * 8, rank), f32), right)


def whiten(inverse, pieces, out):
    def kernel(inverse_ref, *refs):
        total = refs[0][...]
        for ref in refs[1:-1]:
            total = total + ref[...]
        refs[-1][...] = lax.dot_general(
            total, inverse_ref[...], BOTH_LAST, preferred_element_type=f32, precision=HIGHEST
        ).astype(out)

    return small(kernel, jax.ShapeDtypeStruct(pieces[0].shape, out), inverse, *pieces)


def gram_kernel(at_ref, own_ref, one_ref, two_ref, three_ref, projected_ref, keep_ref, send_ref, gram_ref):
    projected = (own_ref[...] + two_ref[...]) + (one_ref[...] + three_ref[...])
    projected_ref[...] = projected
    gram_ref[...] = lax.dot_general(
        projected, projected, BOTH_FIRST, preferred_element_type=f32, precision=HIGHEST
    )
    part = keep_ref.shape[0]
    for other, ref in enumerate((keep_ref, send_ref)):
        place = at_ref[AT_X] * 2 + (at_ref[AT_CORE] + other) % 2
        ref[...] = gram_ref[pl.ds(pl.multiple_of(place * part, part), part), :]


def gram_rows_of(at, pieces):
    rows, rank = pieces[0].shape
    part = jax.ShapeDtypeStruct((rank // (NX * 2), rank), f32)
    return pl.pallas_call(
        gram_kernel,
        out_shape=[jax.ShapeDtypeStruct((rows, rank), f32), part, part],
        in_specs=[SMEM] + [VMEM] * 4,
        out_specs=[VMEM] * 3,
        scratch_shapes=[pltpu.VMEM((rank, rank), f32)],
        compiler_params=pltpu.CompilerParams(vmem_limit_bytes=8 * MIB),
        cost_estimate=pl.CostEstimate(flops=2**28, bytes_accessed=2**20, transcendentals=0),
    )(at, *pieces)


def cross_kernel(at_ref, mine_ref, other_ref, left_mine_ref, left_other_ref, *refs):
    pieces, (terms_ref, whole_ref) = refs[:NY], refs[NY:]
    rows, rank = left_mine_ref.shape
    for n, ref in enumerate((left_mine_ref, left_other_ref)):
        left = ref[...]
        for t in range(3):
            term = left.astype(bf16)
            terms_ref[n * rows : (n + 1) * rows, t * rank : (t + 1) * rank] = term
            left = left - term.astype(f32)
    width = mine_ref.shape[1] // 2

    def multiply(step, carry):
        columns = pl.ds(pl.multiple_of(step * width, 128), width)
        momentum = jnp.concatenate([mine_ref[:, columns], other_ref[:, columns]], axis=0)
        product = lax.dot_general(momentum, terms_ref[...], BOTH_FIRST, preferred_element_type=f32)
        total = (product[:, 2 * rank :] + product[:, rank : 2 * rank]) + product[:, :rank]
        whole_ref[columns, :] = total
        return carry

    lax.fori_loop(0, 2, multiply, 0)
    size = pieces[0].shape[0]
    for by, ref in enumerate(pieces):
        start = pl.multiple_of(ahead(at_ref[AT_Y], by, NY) * size, size)
        ref[...] = whole_ref[pl.ds(start, size), :]


def cross(at, mine, other, left_mine, left_other):
    rows, cols = mine.shape
    rank = left_mine.shape[1]
    return pl.pallas_call(
        cross_kernel,
        out_shape=[jax.ShapeDtypeStruct((cols // NY, rank), f32)] * NY,
        in_specs=[SMEM] + [VMEM] * 4,
        out_specs=[VMEM] * NY,
        scratch_shapes=[pltpu.VMEM((2 * rows, 3 * rank), bf16), pltpu.VMEM((cols, rank), f32)],
        compiler_params=pltpu.CompilerParams(vmem_limit_bytes=16 * MIB),
        cost_estimate=pl.CostEstimate(
            flops=12 * rows * cols * rank, bytes_accessed=4 * rows * cols + 8 * cols * rank, transcendentals=0
        ),
    )(at, mine, other, left_mine, left_other)


def finish_kernel(scaling, at_ref, momentum_ref, solved_ref, squares_ref, *refs):
    pieces = refs[:10]
    new_momentum_ref, update_ref, q_next_ref, right_ref, left_ref, inverse_ref, semaphores = refs[10:]
    rows, rank = solved_ref.shape
    step = pl.program_id(0)
    width = momentum_ref.shape[1]
    shard_rank = q_next_ref.shape[0]
    size = pieces[0].shape[0]

    @pl.when(step == 0)
    def _():
        copies = []
        for n, ref in enumerate(pieces):
            side = at_ref[AT_CORE] if n < 5 else 1 - at_ref[AT_CORE]
            start = (side * NY + ahead(at_ref[AT_Y], RING_FROM[n % 5], NY)) * size
            start = pl.multiple_of(start + (ref.shape[0] if n % 5 == 4 else 0), 16)
            copy = pltpu.make_async_copy(
                ref, right_ref.at[pl.ds(start, ref.shape[0]), :], semaphores.at[n]
            )
            copy.start()
            copies.append(copy)
        solved = solved_ref[...]
        squares = jnp.sum(squares_ref[...], axis=0, keepdims=True) / 8
        inverse_lengths = lax.rsqrt(squares + 1e-06)
        left_ref[:rows, :] = solved.astype(bf16)
        left_ref[rows : 2 * rows, :] = (solved * (scaling * inverse_lengths)).astype(bf16)
        wanted = lax.broadcasted_iota(jnp.int32, (16, rank), 0) + at_ref[FIRST_RANK]
        picked = jnp.where(wanted == lax.broadcasted_iota(jnp.int32, (16, rank), 1), 1.0, 0.0)
        left_ref[2 * rows :, :] = picked.astype(bf16)
        own = jnp.sum(picked * inverse_lengths, axis=1, keepdims=True)
        inverse_ref[...] = jnp.broadcast_to(own, inverse_ref.shape)
        for copy in copies:
            copy.wait()

    right = right_ref[pl.ds(pl.multiple_of(step * width, width), width), :]
    product = lax.dot_general(left_ref[...], right, BOTH_LAST, preferred_element_type=f32)
    momentum = momentum_ref[...].astype(f32)
    new_momentum_ref[...] = (momentum - (1.0 - momentum_decay) * product[:rows]).astype(bf16)
    update_ref[...] = product[rows : 2 * rows].astype(bf16)
    q_next_ref[...] = (
        product[2 * rows : 2 * rows + shard_rank] * inverse_ref[:shard_rank, :1]
    )


def finish(at, momentum, solved, squares, pieces, scaling, shard_rank):
    rows, cols = momentum.shape
    rank = solved.shape[1]
    width = cols // 4
    columns = pl.BlockSpec((rows, width), lambda i: (0, i))
    out = jax.ShapeDtypeStruct((rows, cols), bf16)
    return pl.pallas_call(
        lambda *refs: finish_kernel(scaling, *refs),
        out_shape=[out, out, jax.ShapeDtypeStruct((shard_rank, cols), f32)],
        grid=(4,),
        in_specs=[
            SMEM,
            columns,
            pl.BlockSpec(solved.shape, lambda i: (0, 0)),
            pl.BlockSpec(squares.shape, lambda i: (0, 0)),
        ]
        + [ANY] * 10,
        out_specs=[columns, columns, pl.BlockSpec((shard_rank, width), lambda i: (0, i))],
        scratch_shapes=[
            pltpu.VMEM((cols, rank), bf16),
            pltpu.VMEM((2 * rows + 16, rank), bf16),
            pltpu.VMEM((16, 128), f32),
            pltpu.SemaphoreType.DMA((10,)),
        ],
        compiler_params=pltpu.CompilerParams(vmem_limit_bytes=20 * MIB),
        cost_estimate=pl.CostEstimate(
            flops=4 * rows * cols * rank, bytes_accessed=8 * rows * cols, transcendentals=0
        ),
    )(at, momentum, solved, squares, *pieces)


def swap_cores(block):
    return lax.ppermute(block, "c", [(0, 1), (1, 0)])


def from_ahead(block, axis, by, parts=4):
    return lax.ppermute(block, axis, [((i + by) % parts, i) for i in range(parts)])


def all_of_four(block, axis):
    return [block] + [from_ahead(block, axis, by) for by in (1, 2, 3)]


def ring_of_four(block, axis, beside=None):
    middle = block.shape[0] // 2
    one, three = from_ahead(block, axis, 1), from_ahead(block, axis, 3)
    one, three, beside = lax.optimization_barrier((one, three, beside))
    across = (from_ahead(three[:middle], axis, 3), from_ahead(one[middle:], axis, 1))
    return (block, one, three) + across, beside


def exchange(pieces, axes):
    return lax.all_to_all(pieces, axes, 0, 0)


def per_device(momentum, q_basis):
    rows, cols = momentum.shape
    half = cols // 2
    shard_rank = q_basis.shape[0]
    rank = shard_rank * NZ * NY * 2
    core, at_x, at_y = lax.axis_index("c"), lax.axis_index("x"), lax.axis_index("y")
    position = (lax.axis_index("z") * NY + at_y) * 2 + core
    at = jnp.stack([at_y, core, at_x, position * shard_rank]).astype(jnp.int32)


    def columns(array, of_core):
        return lax.dynamic_slice_in_dim(array, of_core * half, half, 1)

    received = swap_cores(columns(q_basis, 1 - core))
    later, received = lax.optimization_barrier((momentum, received))
    mine = columns(later, core)
    other = swap_cores(columns(later, 1 - core))

    basis = exchange(basis_copies(at, q_basis, received, NZ), "z").reshape(rank // NY, half)
    basis = all_of_four(basis, "y")
    proj_mine, proj_other = project(at, mine, other, basis)
    proj_chip = add(proj_mine, swap_cores(proj_other))
    projected, gram_keep, gram_send = gram_rows_of(at, all_of_four(proj_chip, "x"))

    gram_rows = add(gram_keep, swap_cores(gram_send))
    gram_rows, proj_swapped = lax.optimization_barrier((gram_rows, swap_cores(projected)))
    gram_rows = all_of_four(gram_rows, "y")
    gram_rows = sum_copies(exchange(sum_four_copies(gram_rows, NZ), "z"), 1)[0]
    gram_chip = jnp.concatenate([gram_rows, swap_cores(gram_rows)])
    inverse = inverse_factor(at, all_of_four(gram_chip, "x"))

    crossed = cross(at, mine, other, projected, proj_swapped)
    right = [crossed[0]] + [from_ahead(crossed[by], "y", NY - by) for by in (1, 2, 3)]
    right = whiten(inverse, right, bf16).reshape(NZ, half // (NY * NZ), rank)
    right = exchange(sum_copies(exchange(right, "z"), NZ), "z").reshape(half // NY, rank)
    solved = whiten(inverse, [projected], f32)

    parts = NY * 2 * NX
    squares = square_copies(right, parts).reshape(parts, 8, rank)
    squares = exchange(squares, ("y", "c", "x")).reshape(parts * 8, rank)
    pieces, (squares, swapped) = ring_of_four(right, "y", (squares, swap_cores(right)))
    pieces = pieces + (swapped,) + tuple(swap_cores(piece) for piece in pieces[1:])

    total_rows = rows * NZ * NY * 2
    total_cols = cols * NX
    scaling = math.sqrt(total_rows * total_cols / rank)
    return tuple(finish(at, momentum, solved, squares, pieces, scaling, shard_rank))


def solution(mesh):
    split = Mesh(mesh.devices.reshape(NZ, NY, 2, NX), ("z", "y", "c", "x"))
    spec = P(("z", "y", "c"), "x")
    return jax.shard_map(
        per_device,
        mesh=split,
        in_specs=(spec, spec),
        out_specs=(spec, spec, spec),
        check_vma=False,
    )
```

```python
import math

import jax
import jax.numpy as jnp
from jax import lax
from jax.experimental import pallas as pl
from jax.experimental.pallas import tpu as pltpu
from jax.sharding import Mesh
from jax.sharding import PartitionSpec as P

momentum_decay = 0.95
f32, bf16 = jnp.float32, jnp.bfloat16
HIGHEST = lax.Precision.HIGHEST
VMEM = pl.BlockSpec(memory_space=pltpu.VMEM)
SMEM = pl.BlockSpec(memory_space=pltpu.SMEM)
ANY = pl.BlockSpec(memory_space=pl.ANY)
BOTH_LAST = (((1,), (1,)), ((), ()))
BOTH_FIRST = (((0,), (0,)), ((), ()))
MIB = 2**20
NZ, NY, NX = 8, 4, 4
PIVOTS = 8
RING_FROM = (0, 1, 3, 2, 2)
AT_Y, AT_CORE, AT_X, FIRST_RANK = range(4)


def ahead(index, by, parts):
    return lax.rem(index + by, parts)


def inverse_factor_kernel(at_ref, own_ref, next_ref, across_ref, last_ref, inverse_ref, work_ref, half_ref, done_ref):
    rank = work_ref.shape[0]
    part = rank // (NX * 2)
    for by, ref in enumerate((own_ref, next_ref, across_ref, last_ref)):
        base = ahead(at_ref[AT_X], by, NX) * 2
        for other in range(2):
            at_core = (at_ref[AT_CORE] + other) % 2
            start = pl.multiple_of((base + at_core) * part, part)
            work_ref[pl.ds(start, part), :] = ref[other * part : (other + 1) * part, :]
    gram = work_ref[...]
    diagonal = lax.broadcasted_iota(jnp.int32, gram.shape, 0) == lax.broadcasted_iota(
        jnp.int32, gram.shape, 1
    )
    ridge = 0.001 * jnp.sum(jnp.where(diagonal, gram, 0.0)) / rank
    work_ref[...] = jnp.where(diagonal, gram + ridge, gram)
    lane = lax.broadcasted_iota(jnp.int32, (1, rank), 1)
    per_y, per_half = NZ * PIVOTS, NZ * PIVOTS // 2
    half = rank // 2
    order = (lane % per_y) // PIVOTS * (NY * PIVOTS) + lane // per_y * PIVOTS + lane % PIVOTS

    def of_half(array, second):
        starts = [y * per_y + second * per_half for y in range(NY)]
        return jnp.concatenate([array[start : start + per_half] for start in starts], axis=0)

    half_ref[...] = of_half(work_ref[...], 0)

    def wide(value):
        return jnp.concatenate([value] * (rank // 128), axis=1)

    steps = range(PIVOTS)

    def eliminate(second, carry):
        for group in range(half // PIVOTS):
            at_z, at_y = divmod(group, NY)
            first_row = at_y * per_half + at_z * PIVOTS
            at = at_y * per_y + at_z * PIVOTS
            block = half_ref[first_row : first_row + PIVOTS, :]
            spread = [jnp.broadcast_to(block[:, at + t : at + t + 1], (PIVOTS, 128)) for t in steps]
            core = [[spread[t][s : s + 1, :] for t in range(s + 1)] for s in steps]
            inside = (lane >= at) & (lane < at + PIVOTS)
            row = [jnp.where(inside, (lane == at + s).astype(f32), block[s : s + 1, :]) for s in steps]
            inverse = [None] * PIVOTS
            ratio = [[None] * PIVOTS for _ in steps]
            for t in steps:
                inverse[t] = 1.0 / core[t][t]
                for s in range(t + 1, PIVOTS):
                    ratio[s][t] = core[s][t] * inverse[t]
                for s in range(t + 1, PIVOTS):
                    for u in range(t + 1, s + 1):
                        core[s][u] = core[s][u] - ratio[s][t] * core[u][t]
                    row[s] = row[s] - wide(ratio[s][t]) * row[t]
            for s in steps:
                done_ref[group * PIVOTS + s : group * PIVOTS + s + 1, :] = row[s] * wide(
                    lax.rsqrt(core[s][s])
                )
            solved = [row[s] * wide(inverse[s]) for s in steps]
            for s in reversed(steps):
                for t in range(s):
                    solved[t] = solved[t] - wide(ratio[s][t]) * solved[s]
            for y in range(NY):
                next_z = at_z + (0 if y > at_y else 1)
                if next_z == NZ // 2:
                    continue
                rows = slice(y * per_half + next_z * PIVOTS, (y + 1) * per_half)
                below = half_ref[rows, :]
                rest = jnp.where(inside, 0.0, below)
                for t in steps:
                    rest = rest - below[:, at + t : at + t + 1] * solved[t]
                half_ref[rows, :] = rest

        @pl.when(second == 0)
        def _():
            done = done_ref[...]
            lower = order <= lax.broadcasted_iota(jnp.int32, (half, rank), 0)
            inverse_ref[:half, :] = jnp.where(lower, done, 0.0)
            done = jnp.where(lower | (order >= half), done, 0.0)
            product = lax.dot_general(
                done, done, BOTH_FIRST, preferred_element_type=f32, precision=HIGHEST
            )
            rest = jnp.where(order < half, 0.0, of_half(work_ref[...], 1)) - of_half(product, 1)
            half_ref[...] = pltpu.roll(rest, rank - per_half, 1)

        @pl.when(second == 1)
        def _():
            inverse_ref[half:, :] = jnp.where(
                order <= lax.broadcasted_iota(jnp.int32, (half, rank), 0) + half,
                pltpu.roll(done_ref[...], per_half, 1),
                0.0,
            )

        return carry

    lax.fori_loop(0, 2, eliminate, 0)


def inverse_factor(at, pieces):
    rank = pieces[0].shape[1]
    return pl.pallas_call(
        inverse_factor_kernel,
        out_shape=jax.ShapeDtypeStruct((rank, rank), f32),
        in_specs=[SMEM] + [VMEM] * 4,
        out_specs=VMEM,
        scratch_shapes=[pltpu.VMEM((rows, rank), f32) for rows in (rank, rank // 2, rank // 2)],
        compiler_params=pltpu.CompilerParams(vmem_limit_bytes=8 * MIB),
        cost_estimate=pl.CostEstimate(flops=10**9, bytes_accessed=2**20, transcendentals=0),
    )(at, *pieces)


def project_kernel(at_ref, mine_ref, other_ref, *refs):
    pieces, (out_mine_ref, out_other_ref, basis_ref) = refs[:NY], refs[NY:]
    for by, ref in enumerate(pieces):
        size = ref.shape[0]
        start = pl.multiple_of(ahead(at_ref[AT_Y], by, NY) * size, size)
        basis_ref[pl.ds(start, size), :] = ref[...]
    width = mine_ref.shape[1] // 2
    out_mine_ref[...] = jnp.zeros_like(out_mine_ref)
    out_other_ref[...] = jnp.zeros_like(out_other_ref)

    def add(step, carry):
        columns = pl.ds(pl.multiple_of(step * width, 128), width)
        basis = basis_ref[:, columns]
        for ref, out_ref in ((mine_ref, out_mine_ref), (other_ref, out_other_ref)):
            out_ref[...] += lax.dot_general(
                ref[:, columns], basis, BOTH_LAST, preferred_element_type=f32
            )
        return carry

    lax.fori_loop(0, 2, add, 0)


def project(at, mine, other, pieces):
    rows, cols = mine.shape
    rank = pieces[0].shape[0] * NY
    return pl.pallas_call(
        project_kernel,
        out_shape=[jax.ShapeDtypeStruct((rows, rank), f32)] * 2,
        in_specs=[SMEM] + [VMEM] * 6,
        out_specs=[VMEM, VMEM],
        scratch_shapes=[pltpu.VMEM((rank, cols), bf16)],
        compiler_params=pltpu.CompilerParams(vmem_limit_bytes=12 * MIB),
        cost_estimate=pl.CostEstimate(
            flops=4 * rows * cols * rank, bytes_accessed=6 * rows * cols, transcendentals=0
        ),
    )(at, mine, other, *pieces)


def small(kernel, out, *args):
    specs = [SMEM if arg.dtype == jnp.int32 else VMEM for arg in args]
    return pl.pallas_call(
        kernel,
        out_shape=out,
        in_specs=specs,
        out_specs=VMEM,
        compiler_params=pltpu.CompilerParams(vmem_limit_bytes=8 * MIB),
        cost_estimate=pl.CostEstimate(flops=2**20, bytes_accessed=2**20, transcendentals=0),
    )(*args)


def add(one, two):
    def kernel(one_ref, two_ref, out_ref):
        out_ref[...] = one_ref[...] + two_ref[...]

    return small(kernel, jax.ShapeDtypeStruct(one.shape, f32), one, two)


def sum_four_copies(pieces, copies):
    def kernel(own_ref, one_ref, two_ref, three_ref, out_ref):
        total = (own_ref[...] + two_ref[...]) + (one_ref[...] + three_ref[...])
        for n in range(copies):
            out_ref[n] = total

    return small(kernel, jax.ShapeDtypeStruct((copies,) + pieces[0].shape, f32), *pieces)


def sum_copies(pieces, copies):
    def kernel(pieces_ref, out_ref):
        total = jnp.sum(pieces_ref[...].astype(f32), axis=0).astype(pieces_ref.dtype)
        for n in range(copies):
            out_ref[n] = total

    shape = (copies,) + pieces.shape[1:]
    return small(kernel, jax.ShapeDtypeStruct(shape, pieces.dtype), pieces)


def cut(at, momentum):
    rows, cols = momentum.shape
    half = cols // 2

    def kernel(at_ref, momentum_ref, mine_ref, theirs_ref, semaphores):
        copies = []
        for n, ref in enumerate((mine_ref, theirs_ref)):
            start = pl.multiple_of((at_ref[AT_CORE] + n) % 2 * half, 128)
            source = momentum_ref.at[:, pl.ds(start, half)]
            copies.append(pltpu.make_async_copy(source, ref, semaphores.at[n]))
        for copy in copies:
            copy.start()
        for copy in copies:
            copy.wait()

    return pl.pallas_call(
        kernel,
        out_shape=[jax.ShapeDtypeStruct((rows, half), bf16)] * 2,
        in_specs=[SMEM, ANY],
        out_specs=[VMEM, VMEM],
        scratch_shapes=[pltpu.SemaphoreType.DMA((2,))],
        compiler_params=pltpu.CompilerParams(vmem_limit_bytes=58 * MIB),
        cost_estimate=pl.CostEstimate(flops=0, bytes_accessed=4 * rows * cols, transcendentals=0),
    )(at, momentum)


def basis_copies(at, basis, received, copies):
    shard_rank, half = received.shape

    def kernel(at_ref, basis_ref, received_ref, out_ref):
        core = at_ref[AT_CORE]
        own = basis_ref[:, pl.ds(pl.multiple_of(core * half, half), half)]
        other = received_ref[...]
        first = jnp.where(core == 0, own, other)
        second = jnp.where(core == 0, other, own)
        chip = jnp.concatenate([first, second], axis=0).astype(bf16)
        for n in range(copies):
            out_ref[n] = chip

    return small(kernel, jax.ShapeDtypeStruct((copies, 2 * shard_rank, half), bf16), at, basis, received)


def square_copies(right, copies):
    rank = right.shape[1]

    def kernel(right_ref, out_ref):
        right = right_ref[...].astype(f32)
        total = jnp.sum(right * right, axis=0, keepdims=True)
        for n in range(copies):
            out_ref[n] = total

    return small(kernel, jax.ShapeDtypeStruct((copies, 1, rank), f32), right)


def whiten(inverse, pieces, out):
    def kernel(inverse_ref, *refs):
        total = refs[0][...]
        for ref in refs[1:-1]:
            total = total + ref[...]
        refs[-1][...] = lax.dot_general(
            total, inverse_ref[...], BOTH_LAST, preferred_element_type=f32, precision=HIGHEST
        ).astype(out)

    return small(kernel, jax.ShapeDtypeStruct(pieces[0].shape, out), inverse, *pieces)


def gram_kernel(at_ref, own_ref, one_ref, two_ref, three_ref, projected_ref, keep_ref, send_ref, gram_ref):
    projected = (own_ref[...] + two_ref[...]) + (one_ref[...] + three_ref[...])
    projected_ref[...] = projected
    gram_ref[...] = lax.dot_general(
        projected, projected, BOTH_FIRST, preferred_element_type=f32, precision=HIGHEST
    )
    part = keep_ref.shape[0]
    for other, ref in enumerate((keep_ref, send_ref)):
        place = at_ref[AT_X] * 2 + (at_ref[AT_CORE] + other) % 2
        ref[...] = gram_ref[pl.ds(pl.multiple_of(place * part, part), part), :]


def gram_rows_of(at, pieces):
    rows, rank = pieces[0].shape
    part = jax.ShapeDtypeStruct((rank // (NX * 2), rank), f32)
    return pl.pallas_call(
        gram_kernel,
        out_shape=[jax.ShapeDtypeStruct((rows, rank), f32), part, part],
        in_specs=[SMEM] + [VMEM] * 4,
        out_specs=[VMEM] * 3,
        scratch_shapes=[pltpu.VMEM((rank, rank), f32)],
        compiler_params=pltpu.CompilerParams(vmem_limit_bytes=8 * MIB),
        cost_estimate=pl.CostEstimate(flops=2**28, bytes_accessed=2**20, transcendentals=0),
    )(at, *pieces)


def cross_kernel(at_ref, mine_ref, other_ref, left_mine_ref, left_other_ref, *refs):
    pieces, (terms_ref, whole_ref) = refs[:NY], refs[NY:]
    rows, rank = left_mine_ref.shape
    for n, ref in enumerate((left_mine_ref, left_other_ref)):
        left = ref[...]
        for t in range(3):
            term = left.astype(bf16)
            terms_ref[n * rows : (n + 1) * rows, t * rank : (t + 1) * rank] = term
            left = left - term.astype(f32)
    width = mine_ref.shape[1] // 2

    def multiply(step, carry):
        columns = pl.ds(pl.multiple_of(step * width, 128), width)
        momentum = jnp.concatenate([mine_ref[:, columns], other_ref[:, columns]], axis=0)
        product = lax.dot_general(momentum, terms_ref[...], BOTH_FIRST, preferred_element_type=f32)
        total = (product[:, 2 * rank :] + product[:, rank : 2 * rank]) + product[:, :rank]
        whole_ref[columns, :] = total
        return carry

    lax.fori_loop(0, 2, multiply, 0)
    size = pieces[0].shape[0]
    for by, ref in enumerate(pieces):
        start = pl.multiple_of(ahead(at_ref[AT_Y], by, NY) * size, size)
        ref[...] = whole_ref[pl.ds(start, size), :]


def cross(at, mine, other, left_mine, left_other):
    rows, cols = mine.shape
    rank = left_mine.shape[1]
    return pl.pallas_call(
        cross_kernel,
        out_shape=[jax.ShapeDtypeStruct((cols // NY, rank), f32)] * NY,
        in_specs=[SMEM] + [VMEM] * 4,
        out_specs=[VMEM] * NY,
        scratch_shapes=[pltpu.VMEM((2 * rows, 3 * rank), bf16), pltpu.VMEM((cols, rank), f32)],
        compiler_params=pltpu.CompilerParams(vmem_limit_bytes=16 * MIB),
        cost_estimate=pl.CostEstimate(
            flops=12 * rows * cols * rank, bytes_accessed=4 * rows * cols + 8 * cols * rank, transcendentals=0
        ),
    )(at, mine, other, left_mine, left_other)


def finish_kernel(scaling, at_ref, momentum_ref, solved_ref, squares_ref, *refs):
    pieces = refs[:10]
    new_momentum_ref, update_ref, q_next_ref, right_ref, left_ref, inverse_ref, semaphores = refs[10:]
    rows, rank = solved_ref.shape
    step = pl.program_id(0)
    width = momentum_ref.shape[1]
    shard_rank = q_next_ref.shape[0]
    size = pieces[0].shape[0]

    @pl.when(step == 0)
    def _():
        copies = []
        for n, ref in enumerate(pieces):
            side = at_ref[AT_CORE] if n < 5 else 1 - at_ref[AT_CORE]
            start = (side * NY + ahead(at_ref[AT_Y], RING_FROM[n % 5], NY)) * size
            start = pl.multiple_of(start + (ref.shape[0] if n % 5 == 4 else 0), 16)
            copy = pltpu.make_async_copy(
                ref, right_ref.at[pl.ds(start, ref.shape[0]), :], semaphores.at[n]
            )
            copy.start()
            copies.append(copy)
        solved = solved_ref[...]
        squares = jnp.sum(squares_ref[...], axis=0)
        inverse_lengths = lax.rsqrt(squares + 1e-06)
        left_ref[:rows, :] = solved.astype(bf16)
        left_ref[rows : 2 * rows, :] = (solved * (scaling * inverse_lengths)).astype(bf16)
        wanted = lax.broadcasted_iota(jnp.int32, (16, rank), 0) + at_ref[FIRST_RANK]
        picked = jnp.where(wanted == lax.broadcasted_iota(jnp.int32, (16, rank), 1), 1.0, 0.0)
        left_ref[2 * rows :, :] = picked.astype(bf16)
        own = jnp.sum(picked * inverse_lengths, axis=1, keepdims=True)
        inverse_ref[...] = jnp.broadcast_to(own, inverse_ref.shape)
        for copy in copies:
            copy.wait()

    right = right_ref[pl.ds(pl.multiple_of(step * width, width), width), :]
    product = lax.dot_general(left_ref[...], right, BOTH_LAST, preferred_element_type=f32)
    momentum = momentum_ref[...].astype(f32)
    new_momentum_ref[...] = (momentum - (1.0 - momentum_decay) * product[:rows]).astype(bf16)
    update_ref[...] = product[rows : 2 * rows].astype(bf16)
    q_next_ref[...] = (
        product[2 * rows : 2 * rows + shard_rank] * inverse_ref[:shard_rank, :1]
    )


def finish(at, momentum, solved, squares, pieces, scaling, shard_rank):
    rows, cols = momentum.shape
    rank = solved.shape[1]
    width = cols // 4
    columns = pl.BlockSpec((rows, width), lambda i: (0, i))
    out = jax.ShapeDtypeStruct((rows, cols), bf16)
    return pl.pallas_call(
        lambda *refs: finish_kernel(scaling, *refs),
        out_shape=[out, out, jax.ShapeDtypeStruct((shard_rank, cols), f32)],
        grid=(4,),
        in_specs=[
            SMEM,
            columns,
            pl.BlockSpec(solved.shape, lambda i: (0, 0)),
            pl.BlockSpec(squares.shape, lambda i: (0, 0, 0)),
        ]
        + [ANY] * 10,
        out_specs=[columns, columns, pl.BlockSpec((shard_rank, width), lambda i: (0, i))],
        scratch_shapes=[
            pltpu.VMEM((cols, rank), bf16),
            pltpu.VMEM((2 * rows + 16, rank), bf16),
            pltpu.VMEM((16, 128), f32),
            pltpu.SemaphoreType.DMA((10,)),
        ],
        compiler_params=pltpu.CompilerParams(vmem_limit_bytes=20 * MIB),
        cost_estimate=pl.CostEstimate(
            flops=4 * rows * cols * rank, bytes_accessed=8 * rows * cols, transcendentals=0
        ),
    )(at, momentum, solved, squares, *pieces)


def swap_cores(block):
    return lax.ppermute(block, "c", [(0, 1), (1, 0)])


def from_ahead(block, axis, by, parts=4):
    return lax.ppermute(block, axis, [((i + by) % parts, i) for i in range(parts)])


def all_of_four(block, axis):
    return [block] + [from_ahead(block, axis, by) for by in (1, 2, 3)]


def ring_of_four(block, axis, beside=None):
    middle = block.shape[0] // 2
    one, three = from_ahead(block, axis, 1), from_ahead(block, axis, 3)
    one, three, beside = lax.optimization_barrier((one, three, beside))
    across = (from_ahead(three[:middle], axis, 3), from_ahead(one[middle:], axis, 1))
    return (block, one, three) + across, beside


def exchange(pieces, axes):
    return lax.all_to_all(pieces, axes, 0, 0)


def per_device(momentum, q_basis):
    rows, cols = momentum.shape
    half = cols // 2
    shard_rank = q_basis.shape[0]
    rank = shard_rank * NZ * NY * 2
    core, at_x, at_y = lax.axis_index("c"), lax.axis_index("x"), lax.axis_index("y")
    position = (lax.axis_index("z") * NY + at_y) * 2 + core
    at = jnp.stack([at_y, core, at_x, position * shard_rank]).astype(jnp.int32)


    def columns(array, of_core):
        return lax.dynamic_slice_in_dim(array, of_core * half, half, 1)

    received = swap_cores(columns(q_basis, 1 - core))
    later, received = lax.optimization_barrier((at, received))
    mine, theirs = cut(later, momentum)
    other = swap_cores(theirs)

    basis = exchange(basis_copies(at, q_basis, received, NZ), "z").reshape(rank // NY, half)
    basis = all_of_four(basis, "y")
    proj_mine, proj_other = project(at, mine, other, basis)
    proj_chip = add(proj_mine, swap_cores(proj_other))
    projected, gram_keep, gram_send = gram_rows_of(at, all_of_four(proj_chip, "x"))

    gram_rows = add(gram_keep, swap_cores(gram_send))
    gram_rows, proj_swapped = lax.optimization_barrier((gram_rows, swap_cores(projected)))
    gram_rows = all_of_four(gram_rows, "y")
    gram_rows = sum_copies(exchange(sum_four_copies(gram_rows, NZ), "z"), 1)[0]
    gram_chip = jnp.concatenate([gram_rows, swap_cores(gram_rows)])
    inverse = inverse_factor(at, all_of_four(gram_chip, "x"))

    crossed = cross(at, mine, other, projected, proj_swapped)
    right = [crossed[0]] + [from_ahead(crossed[by], "y", NY - by) for by in (1, 2, 3)]
    right = whiten(inverse, right, bf16).reshape(NZ, half // (NY * NZ), rank)
    right = exchange(sum_copies(exchange(right, "z"), NZ), "z").reshape(half // NY, rank)
    solved = whiten(inverse, [projected], f32)

    parts = NY * 2 * NX
    squares = exchange(square_copies(right, parts), ("y", "c", "x"))
    pieces, (squares, swapped) = ring_of_four(right, "y", (squares, swap_cores(right)))
    pieces = pieces + (swapped,) + tuple(swap_cores(piece) for piece in pieces[1:])

    total_rows = rows * NZ * NY * 2
    total_cols = cols * NX
    scaling = math.sqrt(total_rows * total_cols / rank)
    return tuple(finish(at, momentum, solved, squares, pieces, scaling, shard_rank))


def solution(mesh):
    split = Mesh(mesh.devices.reshape(NZ, NY, 2, NX), ("z", "y", "c", "x"))
    spec = P(("z", "y", "c"), "x")
    return jax.shard_map(
        per_device,
        mesh=split,
        in_specs=(spec, spec),
        out_specs=(spec, spec, spec),
        check_vma=False,
    )
```

```python
import math

import jax
import jax.numpy as jnp
from jax import lax
from jax.experimental import pallas as pl
from jax.experimental.pallas import tpu as pltpu
from jax.sharding import Mesh
from jax.sharding import PartitionSpec as P

momentum_decay = 0.95
f32, bf16 = jnp.float32, jnp.bfloat16
HIGHEST = lax.Precision.HIGHEST
VMEM = pl.BlockSpec(memory_space=pltpu.VMEM)
SMEM = pl.BlockSpec(memory_space=pltpu.SMEM)
ANY = pl.BlockSpec(memory_space=pl.ANY)
BOTH_LAST = (((1,), (1,)), ((), ()))
BOTH_FIRST = (((0,), (0,)), ((), ()))
MIB = 2**20
NZ, NY, NX = 8, 4, 4
PIVOTS = 8
MAIN, TAIL = 768, 64
AT_Y, AT_CORE, AT_X, FIRST_RANK = range(4)


def ahead(index, by, parts):
    return lax.rem(index + by, parts)


def inverse_factor_kernel(at_ref, own_ref, next_ref, across_ref, last_ref, inverse_ref, work_ref, half_ref, done_ref):
    rank = work_ref.shape[0]
    part = rank // (NX * 2)
    for by, ref in enumerate((own_ref, next_ref, across_ref, last_ref)):
        base = ahead(at_ref[AT_X], by, NX) * 2
        for other in range(2):
            at_core = (at_ref[AT_CORE] + other) % 2
            start = pl.multiple_of((base + at_core) * part, part)
            work_ref[pl.ds(start, part), :] = ref[other * part : (other + 1) * part, :]
    gram = work_ref[...]
    diagonal = lax.broadcasted_iota(jnp.int32, gram.shape, 0) == lax.broadcasted_iota(
        jnp.int32, gram.shape, 1
    )
    ridge = 0.001 * jnp.sum(jnp.where(diagonal, gram, 0.0)) / rank
    work_ref[...] = jnp.where(diagonal, gram + ridge, gram)
    lane = lax.broadcasted_iota(jnp.int32, (1, rank), 1)
    per_y, per_half = NZ * PIVOTS, NZ * PIVOTS // 2
    half = rank // 2
    order = (lane % per_y) // PIVOTS * (NY * PIVOTS) + lane // per_y * PIVOTS + lane % PIVOTS

    def of_half(array, second):
        starts = [y * per_y + second * per_half for y in range(NY)]
        return jnp.concatenate([array[start : start + per_half] for start in starts], axis=0)

    half_ref[...] = of_half(work_ref[...], 0)

    def wide(value):
        return jnp.concatenate([value] * (rank // 128), axis=1)

    steps = range(PIVOTS)

    def eliminate(second, carry):
        for group in range(half // PIVOTS):
            at_z, at_y = divmod(group, NY)
            first_row = at_y * per_half + at_z * PIVOTS
            at = at_y * per_y + at_z * PIVOTS
            block = half_ref[first_row : first_row + PIVOTS, :]
            spread = [jnp.broadcast_to(block[:, at + t : at + t + 1], (PIVOTS, 128)) for t in steps]
            core = [[spread[t][s : s + 1, :] for t in range(s + 1)] for s in steps]
            inside = (lane >= at) & (lane < at + PIVOTS)
            row = [jnp.where(inside, (lane == at + s).astype(f32), block[s : s + 1, :]) for s in steps]
            inverse = [None] * PIVOTS
            ratio = [[None] * PIVOTS for _ in steps]
            for t in steps:
                inverse[t] = 1.0 / core[t][t]
                for s in range(t + 1, PIVOTS):
                    ratio[s][t] = core[s][t] * inverse[t]
                for s in range(t + 1, PIVOTS):
                    for u in range(t + 1, s + 1):
                        core[s][u] = core[s][u] - ratio[s][t] * core[u][t]
                    row[s] = row[s] - wide(ratio[s][t]) * row[t]
            for s in steps:
                done_ref[group * PIVOTS + s : group * PIVOTS + s + 1, :] = row[s] * wide(
                    lax.rsqrt(core[s][s])
                )
            solved = [row[s] * wide(inverse[s]) for s in steps]
            for s in reversed(steps):
                for t in range(s):
                    solved[t] = solved[t] - wide(ratio[s][t]) * solved[s]
            for y in range(NY):
                next_z = at_z + (0 if y > at_y else 1)
                if next_z == NZ // 2:
                    continue
                rows = slice(y * per_half + next_z * PIVOTS, (y + 1) * per_half)
                below = half_ref[rows, :]
                rest = jnp.where(inside, 0.0, below)
                for t in steps:
                    rest = rest - below[:, at + t : at + t + 1] * solved[t]
                half_ref[rows, :] = rest

        @pl.when(second == 0)
        def _():
            done = done_ref[...]
            lower = order <= lax.broadcasted_iota(jnp.int32, (half, rank), 0)
            inverse_ref[:half, :] = jnp.where(lower, done, 0.0)
            done = jnp.where(lower | (order >= half), done, 0.0)
            product = lax.dot_general(
                done, done, BOTH_FIRST, preferred_element_type=f32, precision=HIGHEST
            )
            rest = jnp.where(order < half, 0.0, of_half(work_ref[...], 1)) - of_half(product, 1)
            half_ref[...] = pltpu.roll(rest, rank - per_half, 1)

        @pl.when(second == 1)
        def _():
            inverse_ref[half:, :] = jnp.where(
                order <= lax.broadcasted_iota(jnp.int32, (half, rank), 0) + half,
                pltpu.roll(done_ref[...], per_half, 1),
                0.0,
            )

        return carry

    lax.fori_loop(0, 2, eliminate, 0)


def inverse_factor(at, pieces):
    rank = pieces[0].shape[1]
    return pl.pallas_call(
        inverse_factor_kernel,
        out_shape=jax.ShapeDtypeStruct((rank, rank), f32),
        in_specs=[SMEM] + [VMEM] * 4,
        out_specs=VMEM,
        scratch_shapes=[pltpu.VMEM((rows, rank), f32) for rows in (rank, rank // 2, rank // 2)],
        compiler_params=pltpu.CompilerParams(vmem_limit_bytes=8 * MIB),
        cost_estimate=pl.CostEstimate(flops=10**9, bytes_accessed=2**20, transcendentals=0),
    )(at, *pieces)


def project_kernel(at_ref, mine_ref, other_ref, *refs):
    pieces, (out_mine_ref, out_other_ref, basis_ref) = refs[:NY], refs[NY:]
    for by, ref in enumerate(pieces):
        size = ref.shape[0]
        start = pl.multiple_of(ahead(at_ref[AT_Y], by, NY) * size, size)
        basis_ref[pl.ds(start, size), :] = ref[...]
    width = mine_ref.shape[1] // 2
    out_mine_ref[...] = jnp.zeros_like(out_mine_ref)
    out_other_ref[...] = jnp.zeros_like(out_other_ref)

    def add(step, carry):
        columns = pl.ds(pl.multiple_of(step * width, 128), width)
        basis = basis_ref[:, columns]
        for ref, out_ref in ((mine_ref, out_mine_ref), (other_ref, out_other_ref)):
            out_ref[...] += lax.dot_general(
                ref[:, columns], basis, BOTH_LAST, preferred_element_type=f32
            )
        return carry

    lax.fori_loop(0, 2, add, 0)


def project(at, mine, other, pieces):
    rows, cols = mine.shape
    rank = pieces[0].shape[0] * NY
    return pl.pallas_call(
        project_kernel,
        out_shape=[jax.ShapeDtypeStruct((rows, rank), f32)] * 2,
        in_specs=[SMEM] + [VMEM] * 6,
        out_specs=[VMEM, VMEM],
        scratch_shapes=[pltpu.VMEM((rank, cols), bf16)],
        compiler_params=pltpu.CompilerParams(vmem_limit_bytes=12 * MIB),
        cost_estimate=pl.CostEstimate(
            flops=4 * rows * cols * rank, bytes_accessed=6 * rows * cols, transcendentals=0
        ),
    )(at, mine, other, *pieces)


def small(kernel, out, *args):
    specs = [SMEM if arg.dtype == jnp.int32 else VMEM for arg in args]
    return pl.pallas_call(
        kernel,
        out_shape=out,
        in_specs=specs,
        out_specs=VMEM,
        compiler_params=pltpu.CompilerParams(vmem_limit_bytes=8 * MIB),
        cost_estimate=pl.CostEstimate(flops=2**20, bytes_accessed=2**20, transcendentals=0),
    )(*args)


def add(one, two):
    def kernel(one_ref, two_ref, out_ref):
        out_ref[...] = one_ref[...] + two_ref[...]

    return small(kernel, jax.ShapeDtypeStruct(one.shape, f32), one, two)


def sum_four_copies(pieces, copies):
    def kernel(own_ref, one_ref, two_ref, three_ref, out_ref):
        total = (own_ref[...] + two_ref[...]) + (one_ref[...] + three_ref[...])
        for n in range(copies):
            out_ref[n] = total

    return small(kernel, jax.ShapeDtypeStruct((copies,) + pieces[0].shape, f32), *pieces)


def sum_copies(pieces, copies):
    def kernel(pieces_ref, out_ref):
        total = jnp.sum(pieces_ref[...].astype(f32), axis=0).astype(pieces_ref.dtype)
        for n in range(copies):
            out_ref[n] = total

    shape = (copies,) + pieces.shape[1:]
    return small(kernel, jax.ShapeDtypeStruct(shape, pieces.dtype), pieces)


def square_copies(right, copies):
    rank = right.shape[1]

    def kernel(right_ref, out_ref):
        right = right_ref[...].astype(f32)
        total = jnp.sum(right * right, axis=0, keepdims=True)
        for n in range(copies):
            out_ref[n] = total

    return small(kernel, jax.ShapeDtypeStruct((copies, 1, rank), f32), right)


def whiten(inverse, pieces, out):
    def kernel(inverse_ref, *refs):
        total = refs[0][...]
        for ref in refs[1:-1]:
            total = total + ref[...]
        refs[-1][...] = lax.dot_general(
            total, inverse_ref[...], BOTH_LAST, preferred_element_type=f32, precision=HIGHEST
        ).astype(out)

    return small(kernel, jax.ShapeDtypeStruct(pieces[0].shape, out), inverse, *pieces)


def gram_kernel(at_ref, own_ref, one_ref, two_ref, three_ref, projected_ref, keep_ref, send_ref, gram_ref):
    projected = (own_ref[...] + two_ref[...]) + (one_ref[...] + three_ref[...])
    projected_ref[...] = projected
    gram_ref[...] = lax.dot_general(
        projected, projected, BOTH_FIRST, preferred_element_type=f32, precision=HIGHEST
    )
    part = keep_ref.shape[0]
    for other, ref in enumerate((keep_ref, send_ref)):
        place = at_ref[AT_X] * 2 + (at_ref[AT_CORE] + other) % 2
        ref[...] = gram_ref[pl.ds(pl.multiple_of(place * part, part), part), :]


def gram_rows_of(at, pieces):
    rows, rank = pieces[0].shape
    part = jax.ShapeDtypeStruct((rank // (NX * 2), rank), f32)
    return pl.pallas_call(
        gram_kernel,
        out_shape=[jax.ShapeDtypeStruct((rows, rank), f32), part, part],
        in_specs=[SMEM] + [VMEM] * 4,
        out_specs=[VMEM] * 3,
        scratch_shapes=[pltpu.VMEM((rank, rank), f32)],
        compiler_params=pltpu.CompilerParams(vmem_limit_bytes=8 * MIB),
        cost_estimate=pl.CostEstimate(flops=2**28, bytes_accessed=2**20, transcendentals=0),
    )(at, *pieces)


def cross_kernel(at_ref, mine_ref, other_ref, left_mine_ref, left_other_ref, *refs):
    pieces, (terms_ref, whole_ref) = refs[:NY], refs[NY:]
    rows, rank = left_mine_ref.shape
    for n, ref in enumerate((left_mine_ref, left_other_ref)):
        left = ref[...]
        for t in range(3):
            term = left.astype(bf16)
            terms_ref[n * rows : (n + 1) * rows, t * rank : (t + 1) * rank] = term
            left = left - term.astype(f32)
    width = mine_ref.shape[1] // 2

    def multiply(step, carry):
        columns = pl.ds(pl.multiple_of(step * width, 128), width)
        momentum = jnp.concatenate([mine_ref[:, columns], other_ref[:, columns]], axis=0)
        product = lax.dot_general(momentum, terms_ref[...], BOTH_FIRST, preferred_element_type=f32)
        total = (product[:, 2 * rank :] + product[:, rank : 2 * rank]) + product[:, :rank]
        whole_ref[columns, :] = total
        return carry

    lax.fori_loop(0, 2, multiply, 0)
    for by, ref in enumerate(pieces):
        place = ahead(at_ref[AT_Y], by, NY)
        ref[:MAIN, :] = whole_ref[pl.ds(pl.multiple_of(place * MAIN, MAIN), MAIN), :]
        ref[MAIN:, :] = whole_ref[pl.ds(pl.multiple_of(NY * MAIN + place * TAIL, TAIL), TAIL), :]


def cross(at, mine, other, left_mine, left_other):
    rows, cols = mine.shape
    rank = left_mine.shape[1]
    return pl.pallas_call(
        cross_kernel,
        out_shape=[jax.ShapeDtypeStruct((cols // NY, rank), f32)] * NY,
        in_specs=[SMEM] + [VMEM] * 4,
        out_specs=[VMEM] * NY,
        scratch_shapes=[pltpu.VMEM((2 * rows, 3 * rank), bf16), pltpu.VMEM((cols, rank), f32)],
        compiler_params=pltpu.CompilerParams(vmem_limit_bytes=16 * MIB),
        cost_estimate=pl.CostEstimate(
            flops=12 * rows * cols * rank, bytes_accessed=4 * rows * cols + 8 * cols * rank, transcendentals=0
        ),
    )(at, mine, other, left_mine, left_other)


def prepare_left(scaling, at_ref, solved_ref, squares_ref, left_ref, inverse_ref):
    rows, rank = solved_ref.shape
    solved = solved_ref[...]
    squares = jnp.sum(squares_ref[...], axis=0)
    inverse_lengths = lax.rsqrt(squares + 1e-06)
    left_ref[:rows, :] = solved.astype(bf16)
    left_ref[rows : 2 * rows, :] = (solved * (scaling * inverse_lengths)).astype(bf16)
    wanted = lax.broadcasted_iota(jnp.int32, (16, rank), 0) + at_ref[FIRST_RANK]
    picked = jnp.where(wanted == lax.broadcasted_iota(jnp.int32, (16, rank), 1), 1.0, 0.0)
    left_ref[2 * rows :, :] = picked.astype(bf16)
    own = jnp.sum(picked * inverse_lengths, axis=1, keepdims=True)
    inverse_ref[...] = jnp.broadcast_to(own, inverse_ref.shape)


def write_blocks(column_of, right_ref, momentum_ref, out_refs, stage_refs, left_ref, inverse_ref, semaphores):
    taken_ref, stages = stage_refs[0], stage_refs[1:]
    blocks, rows, width = taken_ref.shape
    shard_rank = stages[2].shape[1]

    def take(n):
        columns = pl.ds(pl.multiple_of(column_of(n), 128), width)
        return pltpu.make_async_copy(momentum_ref.at[:, columns], taken_ref.at[n], semaphores.at[0, n])

    def give(n, out):
        columns = pl.ds(pl.multiple_of(column_of(n), 128), width)
        return pltpu.make_async_copy(
            stages[out].at[n], out_refs[out].at[:, columns], semaphores.at[1 + out, n]
        )

    def write(n, carry):
        right = right_ref[pl.ds(pl.multiple_of(n * width, width), width), :]
        product = lax.dot_general(left_ref[...], right, BOTH_LAST, preferred_element_type=f32)
        stages[1][n] = product[rows : 2 * rows].astype(bf16)
        stages[2][n] = product[2 * rows : 2 * rows + shard_rank] * inverse_ref[:shard_rank, :1]
        take(n).wait()
        momentum = taken_ref[n].astype(f32)
        stages[0][n] = (momentum - (1.0 - momentum_decay) * product[:rows]).astype(bf16)
        for out in range(3):
            give(n, out).start()
        return carry

    def start():
        for n in range(blocks):
            take(n).start()

    def wait():
        for n in range(blocks):
            for out in range(3):
                give(n, out).wait()

    return start, lambda: lax.fori_loop(0, blocks, write, 0), wait


def stages_of(blocks, rows, width, shard_rank):
    return [
        pltpu.VMEM((blocks, rows, width), bf16),
        pltpu.VMEM((blocks, rows, width), bf16),
        pltpu.VMEM((blocks, rows, width), bf16),
        pltpu.VMEM((blocks, shard_rank, width), f32),
        pltpu.SemaphoreType.DMA((4, blocks)),
    ]


def first_kernel(scaling, at_ref, momentum_ref, solved_ref, squares_ref, *refs):
    pieces, outs = refs[:6], refs[6:9]
    right_ref, left_ref, inverse_ref, loads = refs[9:13]
    stages, semaphores = refs[13:17], refs[17]
    half = momentum_ref.shape[1] // 2

    def column_of(n):
        side = lax.rem(at_ref[AT_CORE] + n // 3, 2)
        by = n % 3 + n % 3 // 2
        return side * half + ahead(at_ref[AT_Y], by, NY) * MAIN

    start, write, wait = write_blocks(
        column_of, right_ref, momentum_ref, outs, stages, left_ref, inverse_ref, semaphores
    )
    copies = [
        pltpu.make_async_copy(
            ref.at[pl.ds(0, MAIN), :], right_ref.at[pl.ds(n * MAIN, MAIN), :], loads.at[n]
        )
        for n, ref in enumerate(pieces)
    ]
    for copy in copies:
        copy.start()
    start()
    prepare_left(scaling, at_ref, solved_ref, squares_ref, left_ref, inverse_ref)
    for copy in copies:
        copy.wait()
    write()
    wait()


def second_kernel(scaling, at_ref, momentum_ref, solved_ref, squares_ref, *refs):
    pieces, outs = refs[:10], refs[13:16]
    main_ref, tail_ref, left_ref, inverse_ref = refs[16:20]
    main_stages, main_semaphores = refs[20:24], refs[24]
    tail_stages, tail_semaphores = refs[25:29], refs[29]
    half = momentum_ref.shape[1] // 2

    def side_of(n):
        return lax.rem(at_ref[AT_CORE] + n, 2)

    start_main, write_main, wait_main = write_blocks(
        lambda n: side_of(n) * half + ahead(at_ref[AT_Y], 2, NY) * MAIN,
        main_ref, momentum_ref, outs, main_stages, left_ref, inverse_ref, main_semaphores,
    )
    start_tail, write_tail, wait_tail = write_blocks(
        lambda n: side_of(n) * half + NY * MAIN,
        tail_ref, momentum_ref, outs, tail_stages, left_ref, inverse_ref, tail_semaphores,
    )
    start_main()
    start_tail()
    prepare_left(scaling, at_ref, solved_ref, squares_ref, left_ref, inverse_ref)
    for side in range(2):
        own, one, three, front, back = pieces[5 * side : 5 * side + 5]
        size = front.shape[0]
        main_ref[side * MAIN : side * MAIN + size, :] = front[...]
        main_ref[side * MAIN + size : (side + 1) * MAIN, :] = back[: MAIN - size, :]
        for by, ref, begin in ((0, own, MAIN), (1, one, MAIN), (3, three, MAIN), (2, back, MAIN - size)):
            place = side * NY * TAIL + ahead(at_ref[AT_Y], by, NY) * TAIL
            tail_ref[pl.ds(pl.multiple_of(place, TAIL), TAIL), :] = ref[begin : begin + TAIL, :]
    write_main()
    write_tail()
    wait_main()
    wait_tail()


def finish(at, momentum, solved, squares, near, far, scaling, shard_rank):
    rows, cols = momentum.shape
    rank = solved.shape[1]
    outs = [jax.ShapeDtypeStruct((rows, cols), bf16)] * 2 + [jax.ShapeDtypeStruct((shard_rank, cols), f32)]
    both = [pltpu.VMEM((2 * rows + 16, rank), bf16), pltpu.VMEM((16, 128), f32)]
    first = pl.pallas_call(
        lambda *refs: first_kernel(scaling, *refs),
        out_shape=outs,
        in_specs=[SMEM, ANY, VMEM, VMEM] + [ANY] * 6,
        out_specs=[ANY] * 3,
        scratch_shapes=[pltpu.VMEM((6 * MAIN, rank), bf16)]
        + both
        + [pltpu.SemaphoreType.DMA((6,))]
        + stages_of(6, rows, MAIN, shard_rank),
        compiler_params=pltpu.CompilerParams(vmem_limit_bytes=18 * MIB),
        cost_estimate=pl.CostEstimate(
            flops=3 * rows * cols * rank, bytes_accessed=6 * rows * cols, transcendentals=0
        ),
    )(at, momentum, solved, squares, *near)
    first = list(first)
    first[2], far = lax.optimization_barrier((first[2], far))
    far = far + tuple(swap_cores(block) for block in far)
    pieces = near[:3] + far[:2] + near[3:] + far[2:]
    return pl.pallas_call(
        lambda *refs: second_kernel(scaling, *refs),
        out_shape=outs,
        in_specs=[SMEM, ANY, VMEM, VMEM] + [VMEM] * 10 + [ANY] * 3,
        out_specs=[ANY] * 3,
        scratch_shapes=[pltpu.VMEM((2 * MAIN, rank), bf16), pltpu.VMEM((2 * NY * TAIL, rank), bf16)]
        + both
        + stages_of(2, rows, MAIN, shard_rank)
        + stages_of(2, rows, NY * TAIL, shard_rank),
        input_output_aliases={14: 0, 15: 1, 16: 2},
        compiler_params=pltpu.CompilerParams(vmem_limit_bytes=18 * MIB),
        cost_estimate=pl.CostEstimate(
            flops=rows * cols * rank, bytes_accessed=2 * rows * cols, transcendentals=0
        ),
    )(at, momentum, solved, squares, *pieces, *first)


def swap_cores(block):
    return lax.ppermute(block, "c", [(0, 1), (1, 0)])


def from_ahead(block, axis, by, parts=4):
    return lax.ppermute(block, axis, [((i + by) % parts, i) for i in range(parts)])


def all_of_four(block, axis):
    return [block] + [from_ahead(block, axis, by) for by in (1, 2, 3)]


def ring_of_four(block, axis, beside):
    middle = block.shape[0] // 2
    one, three = from_ahead(block, axis, 1), from_ahead(block, axis, 3)
    one, three, beside = lax.optimization_barrier((one, three, beside))
    across = (from_ahead(three[:middle], axis, 3), from_ahead(one[middle:], axis, 1))
    return (block, one, three), across, beside


def exchange(pieces, axes):
    return lax.all_to_all(pieces, axes, 0, 0)


def per_device(momentum, q_basis):
    rows, cols = momentum.shape
    half = cols // 2
    shard_rank = q_basis.shape[0]
    rank = shard_rank * NZ * NY * 2
    core, at_x, at_y = lax.axis_index("c"), lax.axis_index("x"), lax.axis_index("y")
    position = (lax.axis_index("z") * NY + at_y) * 2 + core
    at = jnp.stack([at_y, core, at_x, position * shard_rank]).astype(jnp.int32)


    def columns(array, of_core):
        return lax.dynamic_slice_in_dim(array, of_core * half, half, 1)

    basis_half = q_basis.astype(bf16)
    basis_own = columns(basis_half, core)
    basis_other = swap_cores(columns(basis_half, 1 - core))
    basis_chip = jnp.concatenate(
        [jnp.where(core == 0, basis_own, basis_other), jnp.where(core == 0, basis_other, basis_own)]
    )
    later, basis_chip, at = lax.optimization_barrier((momentum, basis_chip, at))
    mine = columns(later, core)
    other = swap_cores(columns(later, 1 - core))

    basis = exchange(jnp.broadcast_to(basis_chip[None], (NZ,) + basis_chip.shape), "z")
    basis = basis.reshape(rank // NY, half)
    proj_mine, proj_other = project(at, mine, other, all_of_four(basis, "y"))
    proj_chip = add(proj_mine, swap_cores(proj_other))
    projected, gram_keep, gram_send = gram_rows_of(at, all_of_four(proj_chip, "x"))

    gram_rows = add(gram_keep, swap_cores(gram_send))
    gram_rows, proj_swapped = lax.optimization_barrier((gram_rows, swap_cores(projected)))
    gram_rows = all_of_four(gram_rows, "y")
    gram_rows = sum_copies(exchange(sum_four_copies(gram_rows, NZ), "z"), 1)[0]
    gram_chip = jnp.concatenate([gram_rows, swap_cores(gram_rows)])
    inverse = inverse_factor(at, all_of_four(gram_chip, "x"))

    crossed = cross(at, mine, other, projected, proj_swapped)
    right = [crossed[0]] + [from_ahead(crossed[by], "y", NY - by) for by in (1, 2, 3)]
    right = whiten(inverse, right, bf16).reshape(NZ, half // (NY * NZ), rank)
    right = exchange(sum_copies(exchange(right, "z"), NZ), "z").reshape(half // NY, rank)
    solved = whiten(inverse, [projected], f32)

    parts = NY * 2 * NX
    squares = exchange(square_copies(right, parts), ("y", "c", "x"))
    near, far, (squares, swapped) = ring_of_four(right, "y", (squares, swap_cores(right)))
    near = near + (swapped,) + tuple(swap_cores(block) for block in near[1:])

    total_rows = rows * NZ * NY * 2
    total_cols = cols * NX
    scaling = math.sqrt(total_rows * total_cols / rank)
    return tuple(finish(at, momentum, solved, squares, near, far, scaling, shard_rank))


def solution(mesh):
    split = Mesh(mesh.devices.reshape(NZ, NY, 2, NX), ("z", "y", "c", "x"))
    spec = P(("z", "y", "c"), "x")
    return jax.shard_map(
        per_device,
        mesh=split,
        in_specs=(spec, spec),
        out_specs=(spec, spec, spec),
        check_vma=False,
    )
```

```python
import math

import jax
import jax.numpy as jnp
from jax import lax
from jax.experimental import pallas as pl
from jax.experimental.pallas import tpu as pltpu
from jax.sharding import Mesh
from jax.sharding import PartitionSpec as P

momentum_decay = 0.95
f32, bf16 = jnp.float32, jnp.bfloat16
HIGHEST = lax.Precision.HIGHEST
VMEM = pl.BlockSpec(memory_space=pltpu.VMEM)
SMEM = pl.BlockSpec(memory_space=pltpu.SMEM)
ANY = pl.BlockSpec(memory_space=pl.ANY)
BOTH_LAST = (((1,), (1,)), ((), ()))
BOTH_FIRST = (((0,), (0,)), ((), ()))
MIB = 2**20
NZ, NY, NX = 8, 4, 4
PIVOTS = 8
MAIN, TAIL = 768, 64
AT_Y, AT_CORE, AT_X, FIRST_RANK = range(4)


def ahead(index, by, parts):
    return lax.rem(index + by, parts)


def inverse_factor_kernel(at_ref, own_ref, next_ref, across_ref, last_ref, inverse_ref, work_ref, half_ref, done_ref):
    rank = work_ref.shape[0]
    part = rank // (NX * 2)
    for by, ref in enumerate((own_ref, next_ref, across_ref, last_ref)):
        base = ahead(at_ref[AT_X], by, NX) * 2
        for other in range(2):
            at_core = (at_ref[AT_CORE] + other) % 2
            start = pl.multiple_of((base + at_core) * part, part)
            work_ref[pl.ds(start, part), :] = ref[other * part : (other + 1) * part, :]
    gram = work_ref[...]
    diagonal = lax.broadcasted_iota(jnp.int32, gram.shape, 0) == lax.broadcasted_iota(
        jnp.int32, gram.shape, 1
    )
    ridge = 0.001 * jnp.sum(jnp.where(diagonal, gram, 0.0)) / rank
    work_ref[...] = jnp.where(diagonal, gram + ridge, gram)
    lane = lax.broadcasted_iota(jnp.int32, (1, rank), 1)
    per_y, per_half = NZ * PIVOTS, NZ * PIVOTS // 2
    half = rank // 2
    order = (lane % per_y) // PIVOTS * (NY * PIVOTS) + lane // per_y * PIVOTS + lane % PIVOTS

    def of_half(array, second):
        starts = [y * per_y + second * per_half for y in range(NY)]
        return jnp.concatenate([array[start : start + per_half] for start in starts], axis=0)

    half_ref[...] = of_half(work_ref[...], 0)

    def wide(value):
        return jnp.concatenate([value] * (rank // 128), axis=1)

    steps = range(PIVOTS)

    def eliminate(second, carry):
        for group in range(half // PIVOTS):
            at_z, at_y = divmod(group, NY)
            first_row = at_y * per_half + at_z * PIVOTS
            at = at_y * per_y + at_z * PIVOTS
            block = half_ref[first_row : first_row + PIVOTS, :]
            spread = [jnp.broadcast_to(block[:, at + t : at + t + 1], (PIVOTS, 128)) for t in steps]
            core = [[spread[t][s : s + 1, :] for t in range(s + 1)] for s in steps]
            inside = (lane >= at) & (lane < at + PIVOTS)
            row = [jnp.where(inside, (lane == at + s).astype(f32), block[s : s + 1, :]) for s in steps]
            inverse = [None] * PIVOTS
            ratio = [[None] * PIVOTS for _ in steps]
            for t in steps:
                inverse[t] = 1.0 / core[t][t]
                for s in range(t + 1, PIVOTS):
                    ratio[s][t] = core[s][t] * inverse[t]
                for s in range(t + 1, PIVOTS):
                    for u in range(t + 1, s + 1):
                        core[s][u] = core[s][u] - ratio[s][t] * core[u][t]
                    row[s] = row[s] - wide(ratio[s][t]) * row[t]
            for s in steps:
                done_ref[group * PIVOTS + s : group * PIVOTS + s + 1, :] = row[s] * wide(
                    lax.rsqrt(core[s][s])
                )
            solved = [row[s] * wide(inverse[s]) for s in steps]
            for s in reversed(steps):
                for t in range(s):
                    solved[t] = solved[t] - wide(ratio[s][t]) * solved[s]
            for y in range(NY):
                next_z = at_z + (0 if y > at_y else 1)
                if next_z == NZ // 2:
                    continue
                rows = slice(y * per_half + next_z * PIVOTS, (y + 1) * per_half)
                below = half_ref[rows, :]
                rest = jnp.where(inside, 0.0, below)
                for t in steps:
                    rest = rest - below[:, at + t : at + t + 1] * solved[t]
                half_ref[rows, :] = rest

        @pl.when(second == 0)
        def _():
            done = done_ref[...]
            lower = order <= lax.broadcasted_iota(jnp.int32, (half, rank), 0)
            inverse_ref[:half, :] = jnp.where(lower, done, 0.0)
            done = jnp.where(lower | (order >= half), done, 0.0)
            product = lax.dot_general(
                done, done, BOTH_FIRST, preferred_element_type=f32, precision=HIGHEST
            )
            rest = jnp.where(order < half, 0.0, of_half(work_ref[...], 1)) - of_half(product, 1)
            half_ref[...] = pltpu.roll(rest, rank - per_half, 1)

        @pl.when(second == 1)
        def _():
            inverse_ref[half:, :] = jnp.where(
                order <= lax.broadcasted_iota(jnp.int32, (half, rank), 0) + half,
                pltpu.roll(done_ref[...], per_half, 1),
                0.0,
            )

        return carry

    lax.fori_loop(0, 2, eliminate, 0)


def inverse_factor(at, pieces):
    rank = pieces[0].shape[1]
    return pl.pallas_call(
        inverse_factor_kernel,
        out_shape=jax.ShapeDtypeStruct((rank, rank), f32),
        in_specs=[SMEM] + [VMEM] * 4,
        out_specs=VMEM,
        scratch_shapes=[pltpu.VMEM((rows, rank), f32) for rows in (rank, rank // 2, rank // 2)],
        compiler_params=pltpu.CompilerParams(vmem_limit_bytes=8 * MIB),
        cost_estimate=pl.CostEstimate(flops=10**9, bytes_accessed=2**20, transcendentals=0),
    )(at, *pieces)


def project_kernel(at_ref, mine_ref, other_ref, *refs):
    pieces, (out_mine_ref, out_other_ref, basis_ref) = refs[:NY], refs[NY:]
    for by, ref in enumerate(pieces):
        size = ref.shape[0]
        start = pl.multiple_of(ahead(at_ref[AT_Y], by, NY) * size, size)
        basis_ref[pl.ds(start, size), :] = ref[...]
    width = mine_ref.shape[1] // 2
    out_mine_ref[...] = jnp.zeros_like(out_mine_ref)
    out_other_ref[...] = jnp.zeros_like(out_other_ref)

    def add(step, carry):
        columns = pl.ds(pl.multiple_of(step * width, 128), width)
        basis = basis_ref[:, columns]
        for ref, out_ref in ((mine_ref, out_mine_ref), (other_ref, out_other_ref)):
            out_ref[...] += lax.dot_general(
                ref[:, columns], basis, BOTH_LAST, preferred_element_type=f32
            )
        return carry

    lax.fori_loop(0, 2, add, 0)


def project(at, mine, other, pieces):
    rows, cols = mine.shape
    rank = pieces[0].shape[0] * NY
    return pl.pallas_call(
        project_kernel,
        out_shape=[jax.ShapeDtypeStruct((rows, rank), f32)] * 2,
        in_specs=[SMEM] + [VMEM] * 6,
        out_specs=[VMEM, VMEM],
        scratch_shapes=[pltpu.VMEM((rank, cols), bf16)],
        compiler_params=pltpu.CompilerParams(vmem_limit_bytes=12 * MIB),
        cost_estimate=pl.CostEstimate(
            flops=4 * rows * cols * rank, bytes_accessed=6 * rows * cols, transcendentals=0
        ),
    )(at, mine, other, *pieces)


def small(kernel, out, *args):
    specs = [SMEM if arg.dtype == jnp.int32 else VMEM for arg in args]
    return pl.pallas_call(
        kernel,
        out_shape=out,
        in_specs=specs,
        out_specs=VMEM,
        compiler_params=pltpu.CompilerParams(vmem_limit_bytes=8 * MIB),
        cost_estimate=pl.CostEstimate(flops=2**20, bytes_accessed=2**20, transcendentals=0),
    )(*args)


def add(one, two):
    def kernel(one_ref, two_ref, out_ref):
        out_ref[...] = one_ref[...] + two_ref[...]

    return small(kernel, jax.ShapeDtypeStruct(one.shape, f32), one, two)


def sum_four_copies(pieces, copies):
    def kernel(own_ref, one_ref, two_ref, three_ref, out_ref):
        total = (own_ref[...] + two_ref[...]) + (one_ref[...] + three_ref[...])
        for n in range(copies):
            out_ref[n] = total

    return small(kernel, jax.ShapeDtypeStruct((copies,) + pieces[0].shape, f32), *pieces)


def sum_copies(pieces, copies):
    def kernel(pieces_ref, out_ref):
        total = jnp.sum(pieces_ref[...].astype(f32), axis=0).astype(pieces_ref.dtype)
        for n in range(copies):
            out_ref[n] = total

    shape = (copies,) + pieces.shape[1:]
    return small(kernel, jax.ShapeDtypeStruct(shape, pieces.dtype), pieces)


def square_copies(right, copies):
    rank = right.shape[1]

    def kernel(right_ref, out_ref):
        right = right_ref[...].astype(f32)
        total = jnp.sum(right * right, axis=0, keepdims=True)
        for n in range(copies):
            out_ref[n] = total

    return small(kernel, jax.ShapeDtypeStruct((copies, 1, rank), f32), right)


def whiten(inverse, pieces, out):
    def kernel(inverse_ref, *refs):
        total = refs[0][...]
        for ref in refs[1:-1]:
            total = total + ref[...]
        refs[-1][...] = lax.dot_general(
            total, inverse_ref[...], BOTH_LAST, preferred_element_type=f32, precision=HIGHEST
        ).astype(out)

    return small(kernel, jax.ShapeDtypeStruct(pieces[0].shape, out), inverse, *pieces)


def gram_kernel(at_ref, own_ref, one_ref, two_ref, three_ref, projected_ref, keep_ref, send_ref, gram_ref):
    for by, ref in enumerate((own_ref, one_ref, two_ref, three_ref)):
        size = ref.shape[0]
        start = pl.multiple_of(ahead(at_ref[AT_X], by, NX) * size, size)
        projected_ref[pl.ds(start, size), :] = ref[...]
    projected = projected_ref[...]
    gram_ref[...] = lax.dot_general(
        projected, projected, BOTH_FIRST, preferred_element_type=f32, precision=HIGHEST
    )
    part = keep_ref.shape[0]
    for other, ref in enumerate((keep_ref, send_ref)):
        place = at_ref[AT_X] * 2 + (at_ref[AT_CORE] + other) % 2
        ref[...] = gram_ref[pl.ds(pl.multiple_of(place * part, part), part), :]


def gram_rows_of(at, pieces):
    size, rank = pieces[0].shape
    part = jax.ShapeDtypeStruct((rank // (NX * 2), rank), f32)
    return pl.pallas_call(
        gram_kernel,
        out_shape=[jax.ShapeDtypeStruct((size * NX, rank), f32), part, part],
        in_specs=[SMEM] + [VMEM] * 4,
        out_specs=[VMEM] * 3,
        scratch_shapes=[pltpu.VMEM((rank, rank), f32)],
        compiler_params=pltpu.CompilerParams(vmem_limit_bytes=8 * MIB),
        cost_estimate=pl.CostEstimate(flops=2**28, bytes_accessed=2**20, transcendentals=0),
    )(at, *pieces)


def add_in_blocks(at, one, two):
    rows, rank = one.shape
    size = rows // NX

    def kernel(at_ref, one_ref, two_ref, *outs):
        for by, ref in enumerate(outs):
            start = pl.multiple_of(ahead(at_ref[AT_X], by, NX) * size, size)
            ref[...] = one_ref[pl.ds(start, size), :] + two_ref[pl.ds(start, size), :]

    return pl.pallas_call(
        kernel,
        out_shape=[jax.ShapeDtypeStruct((size, rank), f32)] * NX,
        in_specs=[SMEM, VMEM, VMEM],
        out_specs=[VMEM] * NX,
        compiler_params=pltpu.CompilerParams(vmem_limit_bytes=8 * MIB),
        cost_estimate=pl.CostEstimate(flops=2**20, bytes_accessed=2**20, transcendentals=0),
    )(at, one, two)


def cross_kernel(at_ref, mine_ref, other_ref, left_mine_ref, left_other_ref, *refs):
    pieces, (terms_ref, whole_ref) = refs[:NY], refs[NY:]
    rows, rank = left_mine_ref.shape
    for n, ref in enumerate((left_mine_ref, left_other_ref)):
        left = ref[...]
        for t in range(3):
            term = left.astype(bf16)
            terms_ref[n * rows : (n + 1) * rows, t * rank : (t + 1) * rank] = term
            left = left - term.astype(f32)
    width = mine_ref.shape[1] // 2

    def multiply(step, carry):
        columns = pl.ds(pl.multiple_of(step * width, 128), width)
        momentum = jnp.concatenate([mine_ref[:, columns], other_ref[:, columns]], axis=0)
        product = lax.dot_general(momentum, terms_ref[...], BOTH_FIRST, preferred_element_type=f32)
        total = (product[:, 2 * rank :] + product[:, rank : 2 * rank]) + product[:, :rank]
        whole_ref[columns, :] = total
        return carry

    lax.fori_loop(0, 2, multiply, 0)
    for by, ref in enumerate(pieces):
        place = ahead(at_ref[AT_Y], by, NY)
        ref[:MAIN, :] = whole_ref[pl.ds(pl.multiple_of(place * MAIN, MAIN), MAIN), :]
        ref[MAIN:, :] = whole_ref[pl.ds(pl.multiple_of(NY * MAIN + place * TAIL, TAIL), TAIL), :]


def cross(at, mine, other, left_mine, left_other):
    rows, cols = mine.shape
    rank = left_mine.shape[1]
    return pl.pallas_call(
        cross_kernel,
        out_shape=[jax.ShapeDtypeStruct((cols // NY, rank), f32)] * NY,
        in_specs=[SMEM] + [VMEM] * 4,
        out_specs=[VMEM] * NY,
        scratch_shapes=[pltpu.VMEM((2 * rows, 3 * rank), bf16), pltpu.VMEM((cols, rank), f32)],
        compiler_params=pltpu.CompilerParams(vmem_limit_bytes=16 * MIB),
        cost_estimate=pl.CostEstimate(
            flops=12 * rows * cols * rank, bytes_accessed=4 * rows * cols + 8 * cols * rank, transcendentals=0
        ),
    )(at, mine, other, left_mine, left_other)


def prepare_left(scaling, at_ref, solved_ref, squares_ref, left_ref, inverse_ref):
    rows, rank = solved_ref.shape
    solved = solved_ref[...]
    squares = jnp.sum(squares_ref[...], axis=0)
    inverse_lengths = lax.rsqrt(squares + 1e-06)
    left_ref[:rows, :] = solved.astype(bf16)
    left_ref[rows : 2 * rows, :] = (solved * (scaling * inverse_lengths)).astype(bf16)
    wanted = lax.broadcasted_iota(jnp.int32, (16, rank), 0) + at_ref[FIRST_RANK]
    picked = jnp.where(wanted == lax.broadcasted_iota(jnp.int32, (16, rank), 1), 1.0, 0.0)
    left_ref[2 * rows :, :] = picked.astype(bf16)
    own = jnp.sum(picked * inverse_lengths, axis=1, keepdims=True)
    inverse_ref[...] = jnp.broadcast_to(own, inverse_ref.shape)


def write_blocks(column_of, right_ref, momentum_ref, out_refs, stage_refs, left_ref, inverse_ref, semaphores):
    taken_ref, stages = stage_refs[0], stage_refs[1:]
    blocks, rows, width = taken_ref.shape
    shard_rank = stages[2].shape[1]

    def take(n):
        columns = pl.ds(pl.multiple_of(column_of(n), 128), width)
        return pltpu.make_async_copy(momentum_ref.at[:, columns], taken_ref.at[n], semaphores.at[0, n])

    def give(n, out):
        columns = pl.ds(pl.multiple_of(column_of(n), 128), width)
        return pltpu.make_async_copy(
            stages[out].at[n], out_refs[out].at[:, columns], semaphores.at[1 + out, n]
        )

    def write(n, carry):
        right = right_ref[pl.ds(pl.multiple_of(n * width, width), width), :]
        product = lax.dot_general(left_ref[...], right, BOTH_LAST, preferred_element_type=f32)
        stages[1][n] = product[rows : 2 * rows].astype(bf16)
        stages[2][n] = product[2 * rows : 2 * rows + shard_rank] * inverse_ref[:shard_rank, :1]
        take(n).wait()
        momentum = taken_ref[n].astype(f32)
        stages[0][n] = (momentum - (1.0 - momentum_decay) * product[:rows]).astype(bf16)
        for out in range(3):
            give(n, out).start()
        return carry

    def start():
        for n in range(blocks):
            take(n).start()

    def wait():
        for n in range(blocks):
            for out in range(3):
                give(n, out).wait()

    return start, lambda: lax.fori_loop(0, blocks, write, 0), wait


def stages_of(blocks, rows, width, shard_rank):
    return [
        pltpu.VMEM((blocks, rows, width), bf16),
        pltpu.VMEM((blocks, rows, width), bf16),
        pltpu.VMEM((blocks, rows, width), bf16),
        pltpu.VMEM((blocks, shard_rank, width), f32),
        pltpu.SemaphoreType.DMA((4, blocks)),
    ]


def first_kernel(scaling, at_ref, momentum_ref, solved_ref, squares_ref, *refs):
    pieces, outs = refs[:6], refs[6:9]
    right_ref, left_ref, inverse_ref, loads = refs[9:13]
    stages, semaphores = refs[13:17], refs[17]
    half = momentum_ref.shape[1] // 2

    def column_of(n):
        side = lax.rem(at_ref[AT_CORE] + n // 3, 2)
        by = n % 3 + n % 3 // 2
        return side * half + ahead(at_ref[AT_Y], by, NY) * MAIN

    start, write, wait = write_blocks(
        column_of, right_ref, momentum_ref, outs, stages, left_ref, inverse_ref, semaphores
    )
    copies = [
        pltpu.make_async_copy(
            ref.at[pl.ds(0, MAIN), :], right_ref.at[pl.ds(n * MAIN, MAIN), :], loads.at[n]
        )
        for n, ref in enumerate(pieces)
    ]
    for copy in copies:
        copy.start()
    start()
    prepare_left(scaling, at_ref, solved_ref, squares_ref, left_ref, inverse_ref)
    for copy in copies:
        copy.wait()
    write()
    wait()


def second_kernel(scaling, at_ref, momentum_ref, solved_ref, squares_ref, *refs):
    pieces, outs = refs[:10], refs[13:16]
    main_ref, tail_ref, left_ref, inverse_ref = refs[16:20]
    main_stages, main_semaphores = refs[20:24], refs[24]
    tail_stages, tail_semaphores = refs[25:29], refs[29]
    half = momentum_ref.shape[1] // 2

    def side_of(n):
        return lax.rem(at_ref[AT_CORE] + n, 2)

    start_main, write_main, wait_main = write_blocks(
        lambda n: side_of(n) * half + ahead(at_ref[AT_Y], 2, NY) * MAIN,
        main_ref, momentum_ref, outs, main_stages, left_ref, inverse_ref, main_semaphores,
    )
    start_tail, write_tail, wait_tail = write_blocks(
        lambda n: side_of(n) * half + NY * MAIN,
        tail_ref, momentum_ref, outs, tail_stages, left_ref, inverse_ref, tail_semaphores,
    )
    start_main()
    start_tail()
    prepare_left(scaling, at_ref, solved_ref, squares_ref, left_ref, inverse_ref)
    for side in range(2):
        own, one, three, front, back = pieces[5 * side : 5 * side + 5]
        size = front.shape[0]
        main_ref[side * MAIN : side * MAIN + size, :] = front[...]
        main_ref[side * MAIN + size : (side + 1) * MAIN, :] = back[: MAIN - size, :]
        for by, ref, begin in ((0, own, MAIN), (1, one, MAIN), (3, three, MAIN), (2, back, MAIN - size)):
            place = side * NY * TAIL + ahead(at_ref[AT_Y], by, NY) * TAIL
            tail_ref[pl.ds(pl.multiple_of(place, TAIL), TAIL), :] = ref[begin : begin + TAIL, :]
    write_main()
    write_tail()
    wait_main()
    wait_tail()


def finish(at, momentum, solved, squares, near, far, scaling, shard_rank):
    rows, cols = momentum.shape
    rank = solved.shape[1]
    outs = [jax.ShapeDtypeStruct((rows, cols), bf16)] * 2 + [jax.ShapeDtypeStruct((shard_rank, cols), f32)]
    both = [pltpu.VMEM((2 * rows + 16, rank), bf16), pltpu.VMEM((16, 128), f32)]
    first = pl.pallas_call(
        lambda *refs: first_kernel(scaling, *refs),
        out_shape=outs,
        in_specs=[SMEM, ANY, VMEM, VMEM] + [ANY] * 6,
        out_specs=[ANY] * 3,
        scratch_shapes=[pltpu.VMEM((6 * MAIN, rank), bf16)]
        + both
        + [pltpu.SemaphoreType.DMA((6,))]
        + stages_of(6, rows, MAIN, shard_rank),
        compiler_params=pltpu.CompilerParams(vmem_limit_bytes=18 * MIB),
        cost_estimate=pl.CostEstimate(
            flops=3 * rows * cols * rank, bytes_accessed=6 * rows * cols, transcendentals=0
        ),
    )(at, momentum, solved, squares, *near)
    first = list(first)
    first[2], far = lax.optimization_barrier((first[2], far))
    far = far + tuple(swap_cores(block) for block in far)
    pieces = near[:3] + far[:2] + near[3:] + far[2:]
    return pl.pallas_call(
        lambda *refs: second_kernel(scaling, *refs),
        out_shape=outs,
        in_specs=[SMEM, ANY, VMEM, VMEM] + [VMEM] * 10 + [ANY] * 3,
        out_specs=[ANY] * 3,
        scratch_shapes=[pltpu.VMEM((2 * MAIN, rank), bf16), pltpu.VMEM((2 * NY * TAIL, rank), bf16)]
        + both
        + stages_of(2, rows, MAIN, shard_rank)
        + stages_of(2, rows, NY * TAIL, shard_rank),
        input_output_aliases={14: 0, 15: 1, 16: 2},
        compiler_params=pltpu.CompilerParams(vmem_limit_bytes=18 * MIB),
        cost_estimate=pl.CostEstimate(
            flops=rows * cols * rank, bytes_accessed=2 * rows * cols, transcendentals=0
        ),
    )(at, momentum, solved, squares, *pieces, *first)


def swap_cores(block):
    return lax.ppermute(block, "c", [(0, 1), (1, 0)])


def from_ahead(block, axis, by, parts=4):
    return lax.ppermute(block, axis, [((i + by) % parts, i) for i in range(parts)])


def all_of_four(block, axis):
    return [block] + [from_ahead(block, axis, by) for by in (1, 2, 3)]


def ring_of_four(block, axis, beside):
    middle = block.shape[0] // 2
    one, three = from_ahead(block, axis, 1), from_ahead(block, axis, 3)
    one, three, beside = lax.optimization_barrier((one, three, beside))
    across = (from_ahead(three[:middle], axis, 3), from_ahead(one[middle:], axis, 1))
    return (block, one, three), across, beside


def exchange(pieces, axes):
    return lax.all_to_all(pieces, axes, 0, 0)


def per_device(momentum, q_basis):
    rows, cols = momentum.shape
    half = cols // 2
    shard_rank = q_basis.shape[0]
    rank = shard_rank * NZ * NY * 2
    core, at_x, at_y = lax.axis_index("c"), lax.axis_index("x"), lax.axis_index("y")
    position = (lax.axis_index("z") * NY + at_y) * 2 + core
    at = jnp.stack([at_y, core, at_x, position * shard_rank]).astype(jnp.int32)


    def columns(array, of_core):
        return lax.dynamic_slice_in_dim(array, of_core * half, half, 1)

    basis_half = q_basis.astype(bf16)
    basis_own = columns(basis_half, core)
    sent = columns(basis_half, 1 - core)
    later, sent, at = lax.optimization_barrier((momentum, sent, at))
    mine, theirs = columns(later, core), columns(later, 1 - core)
    basis_other = swap_cores(sent)
    mine, theirs, basis_other = lax.optimization_barrier((mine, theirs, basis_other))
    other = swap_cores(theirs)
    basis_chip = jnp.concatenate(
        [jnp.where(core == 0, basis_own, basis_other), jnp.where(core == 0, basis_other, basis_own)]
    )
    basis = exchange(jnp.broadcast_to(basis_chip[None], (NZ,) + basis_chip.shape), "z")
    basis = basis.reshape(rank // NY, half)
    proj_mine, proj_other = project(at, mine, other, all_of_four(basis, "y"))
    blocks = add_in_blocks(at, proj_mine, swap_cores(proj_other))
    block = [blocks[0]] + [from_ahead(blocks[by], "x", NX - by) for by in (1, 2, 3)]
    block = sum_four_copies(block, 1)[0]
    projected, gram_keep, gram_send = gram_rows_of(at, all_of_four(block, "x"))

    gram_rows = add(gram_keep, swap_cores(gram_send))
    gram_rows, proj_swapped = lax.optimization_barrier((gram_rows, swap_cores(projected)))
    gram_rows = all_of_four(gram_rows, "y")
    gram_rows = sum_copies(exchange(sum_four_copies(gram_rows, NZ), "z"), 1)[0]
    gram_chip = jnp.concatenate([gram_rows, swap_cores(gram_rows)])
    inverse = inverse_factor(at, all_of_four(gram_chip, "x"))

    crossed = cross(at, mine, other, projected, proj_swapped)
    right = [crossed[0]] + [from_ahead(crossed[by], "y", NY - by) for by in (1, 2, 3)]
    right = whiten(inverse, right, bf16).reshape(NZ, half // (NY * NZ), rank)
    right = exchange(sum_copies(exchange(right, "z"), NZ), "z").reshape(half // NY, rank)
    solved = whiten(inverse, [projected], f32)

    parts = NY * 2 * NX
    squares = exchange(square_copies(right, parts), ("y", "c", "x"))
    near, far, (squares, swapped) = ring_of_four(right, "y", (squares, swap_cores(right)))
    near = near + (swapped,) + tuple(swap_cores(block) for block in near[1:])

    total_rows = rows * NZ * NY * 2
    total_cols = cols * NX
    scaling = math.sqrt(total_rows * total_cols / rank)
    return tuple(finish(at, momentum, solved, squares, near, far, scaling, shard_rank))


def solution(mesh):
    split = Mesh(mesh.devices.reshape(NZ, NY, 2, NX), ("z", "y", "c", "x"))
    spec = P(("z", "y", "c"), "x")
    return jax.shard_map(
        per_device,
        mesh=split,
        in_specs=(spec, spec),
        out_specs=(spec, spec, spec),
        check_vma=False,
    )
```

```python
import math

import jax
import jax.numpy as jnp
from jax import lax
from jax.experimental import pallas as pl
from jax.experimental.pallas import tpu as pltpu
from jax.sharding import Mesh
from jax.sharding import PartitionSpec as P

momentum_decay = 0.95
f32, bf16 = jnp.float32, jnp.bfloat16
HIGHEST = lax.Precision.HIGHEST
VMEM = pl.BlockSpec(memory_space=pltpu.VMEM)
SMEM = pl.BlockSpec(memory_space=pltpu.SMEM)
ANY = pl.BlockSpec(memory_space=pl.ANY)
BOTH_LAST = (((1,), (1,)), ((), ()))
BOTH_FIRST = (((0,), (0,)), ((), ()))
MIB = 2**20
NZ, NY, NX = 8, 4, 4
PIVOTS = 8
MAIN, TAIL = 768, 64
AT_Y, AT_CORE, AT_X, FIRST_RANK = range(4)


def ahead(index, by, parts):
    return lax.rem(index + by, parts)


def inverse_factor_kernel(gram_ref, inverse_ref, work_ref, half_ref, done_ref):
    rank = work_ref.shape[0]
    gram = gram_ref[...]
    diagonal = lax.broadcasted_iota(jnp.int32, gram.shape, 0) == lax.broadcasted_iota(
        jnp.int32, gram.shape, 1
    )
    ridge = 0.001 * jnp.sum(jnp.where(diagonal, gram, 0.0)) / rank
    work_ref[...] = jnp.where(diagonal, gram + ridge, gram)
    lane = lax.broadcasted_iota(jnp.int32, (1, rank), 1)
    per_y, per_half = NZ * PIVOTS, NZ * PIVOTS // 2
    half = rank // 2
    order = (lane % per_y) // PIVOTS * (NY * PIVOTS) + lane // per_y * PIVOTS + lane % PIVOTS

    def of_half(array, second):
        starts = [y * per_y + second * per_half for y in range(NY)]
        return jnp.concatenate([array[start : start + per_half] for start in starts], axis=0)

    half_ref[...] = of_half(work_ref[...], 0)

    def wide(value):
        return jnp.concatenate([value] * (rank // 128), axis=1)

    steps = range(PIVOTS)

    def eliminate(second, carry):
        for group in range(half // PIVOTS):
            at_z, at_y = divmod(group, NY)
            first_row = at_y * per_half + at_z * PIVOTS
            at = at_y * per_y + at_z * PIVOTS
            block = half_ref[first_row : first_row + PIVOTS, :]
            spread = [jnp.broadcast_to(block[:, at + t : at + t + 1], (PIVOTS, 128)) for t in steps]
            core = [[spread[t][s : s + 1, :] for t in range(s + 1)] for s in steps]
            inside = (lane >= at) & (lane < at + PIVOTS)
            row = [jnp.where(inside, (lane == at + s).astype(f32), block[s : s + 1, :]) for s in steps]
            inverse = [None] * PIVOTS
            ratio = [[None] * PIVOTS for _ in steps]
            for t in steps:
                inverse[t] = 1.0 / core[t][t]
                for s in range(t + 1, PIVOTS):
                    ratio[s][t] = core[s][t] * inverse[t]
                for s in range(t + 1, PIVOTS):
                    for u in range(t + 1, s + 1):
                        core[s][u] = core[s][u] - ratio[s][t] * core[u][t]
                    row[s] = row[s] - wide(ratio[s][t]) * row[t]
            for s in steps:
                done_ref[group * PIVOTS + s : group * PIVOTS + s + 1, :] = row[s] * wide(
                    lax.rsqrt(core[s][s])
                )
            solved = [row[s] * wide(inverse[s]) for s in steps]
            for s in reversed(steps):
                for t in range(s):
                    solved[t] = solved[t] - wide(ratio[s][t]) * solved[s]
            for y in range(NY):
                next_z = at_z + (0 if y > at_y else 1)
                if next_z == NZ // 2:
                    continue
                rows = slice(y * per_half + next_z * PIVOTS, (y + 1) * per_half)
                below = half_ref[rows, :]
                rest = jnp.where(inside, 0.0, below)
                for t in steps:
                    rest = rest - below[:, at + t : at + t + 1] * solved[t]
                half_ref[rows, :] = rest

        @pl.when(second == 0)
        def _():
            done = done_ref[...]
            lower = order <= lax.broadcasted_iota(jnp.int32, (half, rank), 0)
            inverse_ref[:half, :] = jnp.where(lower, done, 0.0)
            done = jnp.where(lower | (order >= half), done, 0.0)
            product = lax.dot_general(
                done, done, BOTH_FIRST, preferred_element_type=f32, precision=HIGHEST
            )
            rest = jnp.where(order < half, 0.0, of_half(work_ref[...], 1)) - of_half(product, 1)
            half_ref[...] = pltpu.roll(rest, rank - per_half, 1)

        @pl.when(second == 1)
        def _():
            inverse_ref[half:, :] = jnp.where(
                order <= lax.broadcasted_iota(jnp.int32, (half, rank), 0) + half,
                pltpu.roll(done_ref[...], per_half, 1),
                0.0,
            )

        return carry

    lax.fori_loop(0, 2, eliminate, 0)


def inverse_factor(gram_matrix):
    rank = gram_matrix.shape[0]
    return pl.pallas_call(
        inverse_factor_kernel,
        out_shape=jax.ShapeDtypeStruct((rank, rank), f32),
        in_specs=[VMEM],
        out_specs=VMEM,
        scratch_shapes=[pltpu.VMEM((rows, rank), f32) for rows in (rank, rank // 2, rank // 2)],
        compiler_params=pltpu.CompilerParams(vmem_limit_bytes=8 * MIB),
    )(gram_matrix)


def project_kernel(at_ref, mine_ref, other_ref, *refs):
    pieces, (out_mine_ref, out_other_ref, basis_ref) = refs[:NY], refs[NY:]
    for by, ref in enumerate(pieces):
        size = ref.shape[0]
        start = pl.multiple_of(ahead(at_ref[AT_Y], by, NY) * size, size)
        basis_ref[pl.ds(start, size), :] = ref[...]
    width = mine_ref.shape[1] // 2
    out_mine_ref[...] = jnp.zeros_like(out_mine_ref)
    out_other_ref[...] = jnp.zeros_like(out_other_ref)

    def add(step, carry):
        columns = pl.ds(pl.multiple_of(step * width, 128), width)
        basis = basis_ref[:, columns]
        for ref, out_ref in ((mine_ref, out_mine_ref), (other_ref, out_other_ref)):
            out_ref[...] += lax.dot_general(
                ref[:, columns], basis, BOTH_LAST, preferred_element_type=f32
            )
        return carry

    lax.fori_loop(0, 2, add, 0)


def project(at, mine, other, pieces):
    rows, cols = mine.shape
    rank = pieces[0].shape[0] * NY
    return pl.pallas_call(
        project_kernel,
        out_shape=[jax.ShapeDtypeStruct((rows, rank), f32)] * 2,
        in_specs=[SMEM] + [VMEM] * 6,
        out_specs=[VMEM, VMEM],
        scratch_shapes=[pltpu.VMEM((rank, cols), bf16)],
        compiler_params=pltpu.CompilerParams(vmem_limit_bytes=12 * MIB),
        cost_estimate=pl.CostEstimate(
            flops=4 * rows * cols * rank, bytes_accessed=6 * rows * cols, transcendentals=0
        ),
    )(at, mine, other, *pieces)


def small(kernel, out, *args):
    specs = [SMEM if arg.dtype == jnp.int32 else VMEM for arg in args]
    return pl.pallas_call(
        kernel,
        out_shape=out,
        in_specs=specs,
        out_specs=VMEM,
        compiler_params=pltpu.CompilerParams(vmem_limit_bytes=8 * MIB),
        cost_estimate=pl.CostEstimate(flops=2**20, bytes_accessed=2**20, transcendentals=0),
    )(*args)


def add(one, two):
    def kernel(one_ref, two_ref, out_ref):
        out_ref[...] = one_ref[...] + two_ref[...]

    return small(kernel, jax.ShapeDtypeStruct(one.shape, f32), one, two)


def sum_four_copies(pieces, copies):
    def kernel(own_ref, one_ref, two_ref, three_ref, out_ref):
        total = (own_ref[...] + two_ref[...]) + (one_ref[...] + three_ref[...])
        for n in range(copies):
            out_ref[n] = total

    return small(kernel, jax.ShapeDtypeStruct((copies,) + pieces[0].shape, f32), *pieces)


def sum_copies(pieces, copies):
    def kernel(pieces_ref, out_ref):
        total = jnp.sum(pieces_ref[...].astype(f32), axis=0).astype(pieces_ref.dtype)
        for n in range(copies):
            out_ref[n] = total

    shape = (copies,) + pieces.shape[1:]
    return small(kernel, jax.ShapeDtypeStruct(shape, pieces.dtype), pieces)


def square_copies(right, copies):
    rank = right.shape[1]

    def kernel(right_ref, out_ref):
        right = right_ref[...].astype(f32)
        total = jnp.sum(right * right, axis=0, keepdims=True)
        for n in range(copies):
            out_ref[n] = total

    return small(kernel, jax.ShapeDtypeStruct((copies, 1, rank), f32), right)


def whiten(inverse, pieces, out):
    def kernel(inverse_ref, *refs):
        total = refs[0][...]
        for ref in refs[1:-1]:
            total = total + ref[...]
        refs[-1][...] = lax.dot_general(
            total, inverse_ref[...], BOTH_LAST, preferred_element_type=f32, precision=HIGHEST
        ).astype(out)

    return small(kernel, jax.ShapeDtypeStruct(pieces[0].shape, out), inverse, *pieces)


def gram_kernel(at_ref, own_ref, one_ref, two_ref, three_ref, projected_ref, keep_ref, send_ref, gram_ref):
    for by, ref in enumerate((own_ref, one_ref, two_ref, three_ref)):
        size = ref.shape[0]
        start = pl.multiple_of(ahead(at_ref[AT_X], by, NX) * size, size)
        projected_ref[pl.ds(start, size), :] = ref[...]
    projected = projected_ref[...]
    gram_ref[...] = lax.dot_general(
        projected, projected, BOTH_FIRST, preferred_element_type=f32, precision=HIGHEST
    )
    part = keep_ref.shape[0]
    for other, ref in enumerate((keep_ref, send_ref)):
        place = at_ref[AT_X] * 2 + (at_ref[AT_CORE] + other) % 2
        ref[...] = gram_ref[pl.ds(pl.multiple_of(place * part, part), part), :]


def gram_rows_of(at, pieces):
    size, rank = pieces[0].shape
    part = jax.ShapeDtypeStruct((rank // (NX * 2), rank), f32)
    return pl.pallas_call(
        gram_kernel,
        out_shape=[jax.ShapeDtypeStruct((size * NX, rank), f32), part, part],
        in_specs=[SMEM] + [VMEM] * 4,
        out_specs=[VMEM] * 3,
        scratch_shapes=[pltpu.VMEM((rank, rank), f32)],
        compiler_params=pltpu.CompilerParams(vmem_limit_bytes=8 * MIB),
        cost_estimate=pl.CostEstimate(flops=2**28, bytes_accessed=2**20, transcendentals=0),
    )(at, *pieces)


def add_in_blocks(at, one, two):
    rows, rank = one.shape
    size = rows // NX

    def kernel(at_ref, one_ref, two_ref, *outs):
        for by, ref in enumerate(outs):
            start = pl.multiple_of(ahead(at_ref[AT_X], by, NX) * size, size)
            ref[...] = one_ref[pl.ds(start, size), :] + two_ref[pl.ds(start, size), :]

    return pl.pallas_call(
        kernel,
        out_shape=[jax.ShapeDtypeStruct((size, rank), f32)] * NX,
        in_specs=[SMEM, VMEM, VMEM],
        out_specs=[VMEM] * NX,
        compiler_params=pltpu.CompilerParams(vmem_limit_bytes=8 * MIB),
        cost_estimate=pl.CostEstimate(flops=2**20, bytes_accessed=2**20, transcendentals=0),
    )(at, one, two)


def cross_kernel(at_ref, mine_ref, other_ref, left_mine_ref, left_other_ref, *refs):
    pieces, (terms_ref, whole_ref) = refs[:NY], refs[NY:]
    rows, rank = left_mine_ref.shape
    for n, ref in enumerate((left_mine_ref, left_other_ref)):
        left = ref[...]
        for t in range(3):
            term = left.astype(bf16)
            terms_ref[n * rows : (n + 1) * rows, t * rank : (t + 1) * rank] = term
            left = left - term.astype(f32)
    width = mine_ref.shape[1] // 2

    def multiply(step, carry):
        columns = pl.ds(pl.multiple_of(step * width, 128), width)
        momentum = jnp.concatenate([mine_ref[:, columns], other_ref[:, columns]], axis=0)
        product = lax.dot_general(momentum, terms_ref[...], BOTH_FIRST, preferred_element_type=f32)
        total = (product[:, 2 * rank :] + product[:, rank : 2 * rank]) + product[:, :rank]
        whole_ref[columns, :] = total
        return carry

    lax.fori_loop(0, 2, multiply, 0)
    for by, ref in enumerate(pieces):
        place = ahead(at_ref[AT_Y], by, NY)
        ref[:MAIN, :] = whole_ref[pl.ds(pl.multiple_of(place * MAIN, MAIN), MAIN), :]
        ref[MAIN:, :] = whole_ref[pl.ds(pl.multiple_of(NY * MAIN + place * TAIL, TAIL), TAIL), :]


def cross(at, mine, other, left_mine, left_other):
    rows, cols = mine.shape
    rank = left_mine.shape[1]
    return pl.pallas_call(
        cross_kernel,
        out_shape=[jax.ShapeDtypeStruct((cols // NY, rank), f32)] * NY,
        in_specs=[SMEM] + [VMEM] * 4,
        out_specs=[VMEM] * NY,
        scratch_shapes=[pltpu.VMEM((2 * rows, 3 * rank), bf16), pltpu.VMEM((cols, rank), f32)],
        compiler_params=pltpu.CompilerParams(vmem_limit_bytes=16 * MIB),
        cost_estimate=pl.CostEstimate(
            flops=12 * rows * cols * rank, bytes_accessed=4 * rows * cols + 8 * cols * rank, transcendentals=0
        ),
    )(at, mine, other, left_mine, left_other)


def prepare_left(scaling, at_ref, solved_ref, squares_ref, left_ref, inverse_ref):
    rows, rank = solved_ref.shape
    solved = solved_ref[...]
    squares = jnp.sum(squares_ref[...], axis=0)
    inverse_lengths = lax.rsqrt(squares + 1e-06)
    left_ref[:rows, :] = solved.astype(bf16)
    left_ref[rows : 2 * rows, :] = (solved * (scaling * inverse_lengths)).astype(bf16)
    wanted = lax.broadcasted_iota(jnp.int32, (16, rank), 0) + at_ref[FIRST_RANK]
    picked = jnp.where(wanted == lax.broadcasted_iota(jnp.int32, (16, rank), 1), 1.0, 0.0)
    left_ref[2 * rows :, :] = picked.astype(bf16)
    own = jnp.sum(picked * inverse_lengths, axis=1, keepdims=True)
    inverse_ref[...] = jnp.broadcast_to(own, inverse_ref.shape)


def write_blocks(column_of, right_ref, momentum_ref, out_refs, stage_refs, left_ref, inverse_ref, semaphores):
    taken_ref, stages = stage_refs[0], stage_refs[1:]
    blocks, rows, width = taken_ref.shape
    shard_rank = stages[2].shape[1]

    def take(n):
        columns = pl.ds(pl.multiple_of(column_of(n), 128), width)
        return pltpu.make_async_copy(momentum_ref.at[:, columns], taken_ref.at[n], semaphores.at[0, n])

    def give(n, out):
        columns = pl.ds(pl.multiple_of(column_of(n), 128), width)
        return pltpu.make_async_copy(
            stages[out].at[n], out_refs[out].at[:, columns], semaphores.at[1 + out, n]
        )

    def write(n, carry):
        right = right_ref[pl.ds(pl.multiple_of(n * width, width), width), :]
        product = lax.dot_general(left_ref[...], right, BOTH_LAST, preferred_element_type=f32)
        stages[1][n] = product[rows : 2 * rows].astype(bf16)
        stages[2][n] = product[2 * rows : 2 * rows + shard_rank] * inverse_ref[:shard_rank, :1]
        take(n).wait()
        momentum = taken_ref[n].astype(f32)
        stages[0][n] = (momentum - (1.0 - momentum_decay) * product[:rows]).astype(bf16)
        for out in range(3):
            give(n, out).start()
        return carry

    def start():
        for n in range(blocks):
            take(n).start()

    def wait():
        for n in range(blocks):
            for out in range(3):
                give(n, out).wait()

    return start, lambda: lax.fori_loop(0, blocks, write, 0), wait


def stages_of(blocks, rows, width, shard_rank):
    return [
        pltpu.VMEM((blocks, rows, width), bf16),
        pltpu.VMEM((blocks, rows, width), bf16),
        pltpu.VMEM((blocks, rows, width), bf16),
        pltpu.VMEM((blocks, shard_rank, width), f32),
        pltpu.SemaphoreType.DMA((4, blocks)),
    ]


def first_kernel(scaling, at_ref, momentum_ref, solved_ref, squares_ref, *refs):
    pieces, outs = refs[:6], refs[6:9]
    right_ref, left_ref, inverse_ref, loads = refs[9:13]
    stages, semaphores = refs[13:17], refs[17]
    half = momentum_ref.shape[1] // 2

    def column_of(n):
        side = lax.rem(at_ref[AT_CORE] + n // 3, 2)
        by = n % 3 + n % 3 // 2
        return side * half + ahead(at_ref[AT_Y], by, NY) * MAIN

    start, write, wait = write_blocks(
        column_of, right_ref, momentum_ref, outs, stages, left_ref, inverse_ref, semaphores
    )
    copies = [
        pltpu.make_async_copy(
            ref.at[pl.ds(0, MAIN), :], right_ref.at[pl.ds(n * MAIN, MAIN), :], loads.at[n]
        )
        for n, ref in enumerate(pieces)
    ]
    for copy in copies:
        copy.start()
    start()
    prepare_left(scaling, at_ref, solved_ref, squares_ref, left_ref, inverse_ref)
    for copy in copies:
        copy.wait()
    write()
    wait()


def second_kernel(scaling, at_ref, momentum_ref, solved_ref, squares_ref, *refs):
    pieces, outs = refs[:10], refs[13:16]
    main_ref, tail_ref, left_ref, inverse_ref = refs[16:20]
    main_stages, main_semaphores = refs[20:24], refs[24]
    tail_stages, tail_semaphores = refs[25:29], refs[29]
    half = momentum_ref.shape[1] // 2

    def side_of(n):
        return lax.rem(at_ref[AT_CORE] + n, 2)

    start_main, write_main, wait_main = write_blocks(
        lambda n: side_of(n) * half + ahead(at_ref[AT_Y], 2, NY) * MAIN,
        main_ref, momentum_ref, outs, main_stages, left_ref, inverse_ref, main_semaphores,
    )
    start_tail, write_tail, wait_tail = write_blocks(
        lambda n: side_of(n) * half + NY * MAIN,
        tail_ref, momentum_ref, outs, tail_stages, left_ref, inverse_ref, tail_semaphores,
    )
    start_main()
    start_tail()
    prepare_left(scaling, at_ref, solved_ref, squares_ref, left_ref, inverse_ref)
    for side in range(2):
        own, one, three, front, back = pieces[5 * side : 5 * side + 5]
        size = front.shape[0]
        main_ref[side * MAIN : side * MAIN + size, :] = front[...]
        main_ref[side * MAIN + size : (side + 1) * MAIN, :] = back[: MAIN - size, :]
        for by, ref, begin in ((0, own, MAIN), (1, one, MAIN), (3, three, MAIN), (2, back, MAIN - size)):
            place = side * NY * TAIL + ahead(at_ref[AT_Y], by, NY) * TAIL
            tail_ref[pl.ds(pl.multiple_of(place, TAIL), TAIL), :] = ref[begin : begin + TAIL, :]
    write_main()
    write_tail()
    wait_main()
    wait_tail()


def finish(at, momentum, solved, squares, near, far, scaling, shard_rank):
    rows, cols = momentum.shape
    rank = solved.shape[1]
    outs = [jax.ShapeDtypeStruct((rows, cols), bf16)] * 2 + [jax.ShapeDtypeStruct((shard_rank, cols), f32)]
    both = [pltpu.VMEM((2 * rows + 16, rank), bf16), pltpu.VMEM((16, 128), f32)]
    first = pl.pallas_call(
        lambda *refs: first_kernel(scaling, *refs),
        out_shape=outs,
        in_specs=[SMEM, ANY, VMEM, VMEM] + [ANY] * 6,
        out_specs=[ANY] * 3,
        scratch_shapes=[pltpu.VMEM((6 * MAIN, rank), bf16)]
        + both
        + [pltpu.SemaphoreType.DMA((6,))]
        + stages_of(6, rows, MAIN, shard_rank),
        compiler_params=pltpu.CompilerParams(vmem_limit_bytes=18 * MIB),
        cost_estimate=pl.CostEstimate(
            flops=3 * rows * cols * rank, bytes_accessed=6 * rows * cols, transcendentals=0
        ),
    )(at, momentum, solved, squares, *near)
    first = list(first)
    first[2], far = lax.optimization_barrier((first[2], far))
    far = far + tuple(swap_cores(block) for block in far)
    pieces = near[:3] + far[:2] + near[3:] + far[2:]
    return pl.pallas_call(
        lambda *refs: second_kernel(scaling, *refs),
        out_shape=outs,
        in_specs=[SMEM, ANY, VMEM, VMEM] + [VMEM] * 10 + [ANY] * 3,
        out_specs=[ANY] * 3,
        scratch_shapes=[pltpu.VMEM((2 * MAIN, rank), bf16), pltpu.VMEM((2 * NY * TAIL, rank), bf16)]
        + both
        + stages_of(2, rows, MAIN, shard_rank)
        + stages_of(2, rows, NY * TAIL, shard_rank),
        input_output_aliases={14: 0, 15: 1, 16: 2},
        compiler_params=pltpu.CompilerParams(vmem_limit_bytes=18 * MIB),
        cost_estimate=pl.CostEstimate(
            flops=rows * cols * rank, bytes_accessed=2 * rows * cols, transcendentals=0
        ),
    )(at, momentum, solved, squares, *pieces, *first)


def swap_cores(block):
    return lax.ppermute(block, "c", [(0, 1), (1, 0)])


def from_ahead(block, axis, by, parts=4):
    return lax.ppermute(block, axis, [((i + by) % parts, i) for i in range(parts)])


def all_of_four(block, axis):
    return [block] + [from_ahead(block, axis, by) for by in (1, 2, 3)]


def ring_of_four(block, axis, beside):
    middle = block.shape[0] // 2
    one, three = from_ahead(block, axis, 1), from_ahead(block, axis, 3)
    one, three, beside = lax.optimization_barrier((one, three, beside))
    across = (from_ahead(three[:middle], axis, 3), from_ahead(one[middle:], axis, 1))
    return (block, one, three), across, beside


def exchange(pieces, axes):
    return lax.all_to_all(pieces, axes, 0, 0)


def per_device(momentum, q_basis):
    rows, cols = momentum.shape
    half = cols // 2
    shard_rank = q_basis.shape[0]
    rank = shard_rank * NZ * NY * 2
    core, at_x, at_y = lax.axis_index("c"), lax.axis_index("x"), lax.axis_index("y")
    position = (lax.axis_index("z") * NY + at_y) * 2 + core
    at = jnp.stack([at_y, core, at_x, position * shard_rank]).astype(jnp.int32)


    def columns(array, of_core):
        return lax.dynamic_slice_in_dim(array, of_core * half, half, 1)

    basis_half = q_basis.astype(bf16)
    basis_own = columns(basis_half, core)
    sent = columns(basis_half, 1 - core)
    later, sent, at = lax.optimization_barrier((momentum, sent, at))
    mine, theirs = columns(later, core), columns(later, 1 - core)
    basis_other = swap_cores(sent)
    mine, theirs, basis_other = lax.optimization_barrier((mine, theirs, basis_other))
    other = swap_cores(theirs)
    basis_chip = jnp.concatenate(
        [jnp.where(core == 0, basis_own, basis_other), jnp.where(core == 0, basis_other, basis_own)]
    )
    basis = exchange(jnp.broadcast_to(basis_chip[None], (NZ,) + basis_chip.shape), "z")
    basis = basis.reshape(rank // NY, half)
    proj_mine, proj_other = project(at, mine, other, all_of_four(basis, "y"))
    blocks = add_in_blocks(at, proj_mine, swap_cores(proj_other))
    block = [blocks[0]] + [from_ahead(blocks[by], "x", NX - by) for by in (1, 2, 3)]
    block = sum_four_copies(block, 1)[0]
    projected, gram_keep, gram_send = gram_rows_of(at, all_of_four(block, "x"))

    gram_rows = add(gram_keep, swap_cores(gram_send))
    gram_rows, proj_swapped = lax.optimization_barrier((gram_rows, swap_cores(projected)))
    gram_rows = all_of_four(gram_rows, "y")
    gram_rows = sum_copies(exchange(sum_four_copies(gram_rows, NZ), "z"), NX * 2)
    inverse = inverse_factor(exchange(gram_rows, ("x", "c")).reshape(rank, rank))

    crossed = cross(at, mine, other, projected, proj_swapped)
    right = [crossed[0]] + [from_ahead(crossed[by], "y", NY - by) for by in (1, 2, 3)]
    right = whiten(inverse, right, bf16).reshape(NZ, half // (NY * NZ), rank)
    right = exchange(sum_copies(exchange(right, "z"), NZ), "z").reshape(half // NY, rank)
    solved = whiten(inverse, [projected], f32)

    parts = NY * 2 * NX
    squares = exchange(square_copies(right, parts), ("y", "c", "x"))
    near, far, (squares, swapped) = ring_of_four(right, "y", (squares, swap_cores(right)))
    near = near + (swapped,) + tuple(swap_cores(block) for block in near[1:])

    total_rows = rows * NZ * NY * 2
    total_cols = cols * NX
    scaling = math.sqrt(total_rows * total_cols / rank)
    return tuple(finish(at, momentum, solved, squares, near, far, scaling, shard_rank))


def solution(mesh):
    split = Mesh(mesh.devices.reshape(NZ, NY, 2, NX), ("z", "y", "c", "x"))
    spec = P(("z", "y", "c"), "x")
    return jax.shard_map(
        per_device,
        mesh=split,
        in_specs=(spec, spec),
        out_specs=(spec, spec, spec),
        check_vma=False,
    )
```

```python
import math

import jax
import jax.numpy as jnp
from jax import lax
from jax.experimental import pallas as pl
from jax.experimental.pallas import tpu as pltpu
from jax.sharding import Mesh
from jax.sharding import PartitionSpec as P

momentum_decay = 0.95
f32, bf16 = jnp.float32, jnp.bfloat16
HIGHEST = lax.Precision.HIGHEST
VMEM = pl.BlockSpec(memory_space=pltpu.VMEM)
SMEM = pl.BlockSpec(memory_space=pltpu.SMEM)
ANY = pl.BlockSpec(memory_space=pl.ANY)
BOTH_LAST = (((1,), (1,)), ((), ()))
BOTH_FIRST = (((0,), (0,)), ((), ()))
MIB = 2**20
NZ, NY, NX = 8, 4, 4
PIVOTS = 8
MAIN, TAIL = 768, 64
AT_Y, AT_CORE, AT_X, FIRST_RANK = range(4)


def ahead(index, by, parts):
    return lax.rem(index + by, parts)


def inverse_factor_kernel(at_ref, own_ref, next_ref, across_ref, last_ref, inverse_ref, work_ref, half_ref, done_ref):
    rank = work_ref.shape[0]
    part = rank // (NX * 2)
    for by, ref in enumerate((own_ref, next_ref, across_ref, last_ref)):
        base = ahead(at_ref[AT_X], by, NX) * 2
        for other in range(2):
            at_core = (at_ref[AT_CORE] + other) % 2
            start = pl.multiple_of((base + at_core) * part, part)
            work_ref[pl.ds(start, part), :] = ref[other * part : (other + 1) * part, :]
    gram = work_ref[...]
    diagonal = lax.broadcasted_iota(jnp.int32, gram.shape, 0) == lax.broadcasted_iota(
        jnp.int32, gram.shape, 1
    )
    ridge = 0.001 * jnp.sum(jnp.where(diagonal, gram, 0.0)) / rank
    work_ref[...] = jnp.where(diagonal, gram + ridge, gram)
    lane = lax.broadcasted_iota(jnp.int32, (1, rank), 1)
    per_y, per_half = NZ * PIVOTS, NZ * PIVOTS // 2
    half = rank // 2
    order = (lane % per_y) // PIVOTS * (NY * PIVOTS) + lane // per_y * PIVOTS + lane % PIVOTS

    def of_half(array, second):
        starts = [y * per_y + second * per_half for y in range(NY)]
        return jnp.concatenate([array[start : start + per_half] for start in starts], axis=0)

    half_ref[...] = of_half(work_ref[...], 0)

    def wide(value):
        return jnp.concatenate([value] * (rank // 128), axis=1)

    steps = range(PIVOTS)

    def eliminate(second, carry):
        for group in range(half // PIVOTS):
            at_z, at_y = divmod(group, NY)
            first_row = at_y * per_half + at_z * PIVOTS
            at = at_y * per_y + at_z * PIVOTS
            block = half_ref[first_row : first_row + PIVOTS, :]
            spread = [jnp.broadcast_to(block[:, at + t : at + t + 1], (PIVOTS, 128)) for t in steps]
            core = [[spread[t][s : s + 1, :] for t in range(s + 1)] for s in steps]
            inside = (lane >= at) & (lane < at + PIVOTS)
            row = [jnp.where(inside, (lane == at + s).astype(f32), block[s : s + 1, :]) for s in steps]
            inverse = [None] * PIVOTS
            ratio = [[None] * PIVOTS for _ in steps]
            for t in steps:
                inverse[t] = 1.0 / core[t][t]
                for s in range(t + 1, PIVOTS):
                    ratio[s][t] = core[s][t] * inverse[t]
                for s in range(t + 1, PIVOTS):
                    for u in range(t + 1, s + 1):
                        core[s][u] = core[s][u] - ratio[s][t] * core[u][t]
                    row[s] = row[s] - wide(ratio[s][t]) * row[t]
            for s in steps:
                done_ref[group * PIVOTS + s : group * PIVOTS + s + 1, :] = row[s] * wide(
                    lax.rsqrt(core[s][s])
                )
            solved = [row[s] * wide(inverse[s]) for s in steps]
            for s in reversed(steps):
                for t in range(s):
                    solved[t] = solved[t] - wide(ratio[s][t]) * solved[s]
            for y in range(NY):
                next_z = at_z + (0 if y > at_y else 1)
                if next_z == NZ // 2:
                    continue
                rows = slice(y * per_half + next_z * PIVOTS, (y + 1) * per_half)
                below = half_ref[rows, :]
                rest = jnp.where(inside, 0.0, below)
                for t in steps:
                    rest = rest - below[:, at + t : at + t + 1] * solved[t]
                half_ref[rows, :] = rest

        @pl.when(second == 0)
        def _():
            done = done_ref[...]
            lower = order <= lax.broadcasted_iota(jnp.int32, (half, rank), 0)
            inverse_ref[:half, :] = jnp.where(lower, done, 0.0)
            done = jnp.where(lower | (order >= half), done, 0.0)
            product = lax.dot_general(
                done, done, BOTH_FIRST, preferred_element_type=f32, precision=HIGHEST
            )
            rest = jnp.where(order < half, 0.0, of_half(work_ref[...], 1)) - of_half(product, 1)
            half_ref[...] = pltpu.roll(rest, rank - per_half, 1)

        @pl.when(second == 1)
        def _():
            inverse_ref[half:, :] = jnp.where(
                order <= lax.broadcasted_iota(jnp.int32, (half, rank), 0) + half,
                pltpu.roll(done_ref[...], per_half, 1),
                0.0,
            )

        return carry

    lax.fori_loop(0, 2, eliminate, 0)


def inverse_factor(at, pieces):
    rank = pieces[0].shape[1]
    return pl.pallas_call(
        inverse_factor_kernel,
        out_shape=jax.ShapeDtypeStruct((rank, rank), f32),
        in_specs=[SMEM] + [VMEM] * 4,
        out_specs=VMEM,
        scratch_shapes=[pltpu.VMEM((rows, rank), f32) for rows in (rank, rank // 2, rank // 2)],
        compiler_params=pltpu.CompilerParams(vmem_limit_bytes=8 * MIB),
        cost_estimate=pl.CostEstimate(flops=10**9, bytes_accessed=2**20, transcendentals=0),
    )(at, *pieces)


def project_kernel(at_ref, mine_ref, other_ref, *refs):
    pieces, (out_mine_ref, out_other_ref, basis_ref) = refs[:NY], refs[NY:]
    for by, ref in enumerate(pieces):
        size = ref.shape[0]
        start = pl.multiple_of(ahead(at_ref[AT_Y], by, NY) * size, size)
        basis_ref[pl.ds(start, size), :] = ref[...]
    width = mine_ref.shape[1] // 2
    out_mine_ref[...] = jnp.zeros_like(out_mine_ref)
    out_other_ref[...] = jnp.zeros_like(out_other_ref)

    def add(step, carry):
        columns = pl.ds(pl.multiple_of(step * width, 128), width)
        basis = basis_ref[:, columns]
        for ref, out_ref in ((mine_ref, out_mine_ref), (other_ref, out_other_ref)):
            out_ref[...] += lax.dot_general(
                ref[:, columns], basis, BOTH_LAST, preferred_element_type=f32
            )
        return carry

    lax.fori_loop(0, 2, add, 0)


def project(at, mine, other, pieces):
    rows, cols = mine.shape
    rank = pieces[0].shape[0] * NY
    return pl.pallas_call(
        project_kernel,
        out_shape=[jax.ShapeDtypeStruct((rows, rank), f32)] * 2,
        in_specs=[SMEM] + [VMEM] * 6,
        out_specs=[VMEM, VMEM],
        scratch_shapes=[pltpu.VMEM((rank, cols), bf16)],
        compiler_params=pltpu.CompilerParams(vmem_limit_bytes=12 * MIB),
        cost_estimate=pl.CostEstimate(
            flops=4 * rows * cols * rank, bytes_accessed=6 * rows * cols, transcendentals=0
        ),
    )(at, mine, other, *pieces)


def small(kernel, out, *args):
    specs = [SMEM if arg.dtype == jnp.int32 else VMEM for arg in args]
    return pl.pallas_call(
        kernel,
        out_shape=out,
        in_specs=specs,
        out_specs=VMEM,
        compiler_params=pltpu.CompilerParams(vmem_limit_bytes=8 * MIB),
        cost_estimate=pl.CostEstimate(flops=2**20, bytes_accessed=2**20, transcendentals=0),
    )(*args)


def add(one, two):
    def kernel(one_ref, two_ref, out_ref):
        out_ref[...] = one_ref[...] + two_ref[...]

    return small(kernel, jax.ShapeDtypeStruct(one.shape, f32), one, two)


def sum_four_copies(pieces, copies):
    def kernel(own_ref, one_ref, two_ref, three_ref, out_ref):
        total = (own_ref[...] + two_ref[...]) + (one_ref[...] + three_ref[...])
        for n in range(copies):
            out_ref[n] = total

    return small(kernel, jax.ShapeDtypeStruct((copies,) + pieces[0].shape, f32), *pieces)


def sum_copies(pieces, copies):
    def kernel(pieces_ref, out_ref):
        total = jnp.sum(pieces_ref[...].astype(f32), axis=0).astype(pieces_ref.dtype)
        for n in range(copies):
            out_ref[n] = total

    shape = (copies,) + pieces.shape[1:]
    return small(kernel, jax.ShapeDtypeStruct(shape, pieces.dtype), pieces)


def square_copies(right, copies):
    rank = right.shape[1]

    def kernel(right_ref, out_ref):
        right = right_ref[...].astype(f32)
        total = jnp.sum(right * right, axis=0, keepdims=True)
        for n in range(copies):
            out_ref[n] = total

    return small(kernel, jax.ShapeDtypeStruct((copies, 1, rank), f32), right)


def whiten(inverse, pieces, out):
    def kernel(inverse_ref, *refs):
        total = refs[0][...]
        for ref in refs[1:-1]:
            total = total + ref[...]
        refs[-1][...] = lax.dot_general(
            total, inverse_ref[...], BOTH_LAST, preferred_element_type=f32, precision=HIGHEST
        ).astype(out)

    return small(kernel, jax.ShapeDtypeStruct(pieces[0].shape, out), inverse, *pieces)


def gram_kernel(at_ref, own_ref, one_ref, two_ref, three_ref, projected_ref, keep_ref, send_ref, gram_ref):
    for by, ref in enumerate((own_ref, one_ref, two_ref, three_ref)):
        size = ref.shape[0]
        start = pl.multiple_of(ahead(at_ref[AT_X], by, NX) * size, size)
        projected_ref[pl.ds(start, size), :] = ref[...]
    projected = projected_ref[...]
    gram_ref[...] = lax.dot_general(
        projected, projected, BOTH_FIRST, preferred_element_type=f32, precision=HIGHEST
    )
    part = keep_ref.shape[0]
    for other, ref in enumerate((keep_ref, send_ref)):
        place = at_ref[AT_X] * 2 + (at_ref[AT_CORE] + other) % 2
        ref[...] = gram_ref[pl.ds(pl.multiple_of(place * part, part), part), :]


def gram_rows_of(at, pieces):
    size, rank = pieces[0].shape
    part = jax.ShapeDtypeStruct((rank // (NX * 2), rank), f32)
    return pl.pallas_call(
        gram_kernel,
        out_shape=[jax.ShapeDtypeStruct((size * NX, rank), f32), part, part],
        in_specs=[SMEM] + [VMEM] * 4,
        out_specs=[VMEM] * 3,
        scratch_shapes=[pltpu.VMEM((rank, rank), f32)],
        compiler_params=pltpu.CompilerParams(vmem_limit_bytes=8 * MIB),
        cost_estimate=pl.CostEstimate(flops=2**28, bytes_accessed=2**20, transcendentals=0),
    )(at, *pieces)


def add_in_blocks(at, one, two):
    rows, rank = one.shape
    size = rows // NX

    def kernel(at_ref, one_ref, two_ref, *outs):
        for by, ref in enumerate(outs):
            start = pl.multiple_of(ahead(at_ref[AT_X], by, NX) * size, size)
            ref[...] = one_ref[pl.ds(start, size), :] + two_ref[pl.ds(start, size), :]

    return pl.pallas_call(
        kernel,
        out_shape=[jax.ShapeDtypeStruct((size, rank), f32)] * NX,
        in_specs=[SMEM, VMEM, VMEM],
        out_specs=[VMEM] * NX,
        compiler_params=pltpu.CompilerParams(vmem_limit_bytes=8 * MIB),
        cost_estimate=pl.CostEstimate(flops=2**20, bytes_accessed=2**20, transcendentals=0),
    )(at, one, two)


def cross_kernel(at_ref, mine_ref, other_ref, left_mine_ref, left_other_ref, *refs):
    pieces, (terms_ref, whole_ref) = refs[:NY], refs[NY:]
    rows, rank = left_mine_ref.shape
    for n, ref in enumerate((left_mine_ref, left_other_ref)):
        left = ref[...]
        for t in range(3):
            term = left.astype(bf16)
            terms_ref[n * rows : (n + 1) * rows, t * rank : (t + 1) * rank] = term
            left = left - term.astype(f32)
    width = mine_ref.shape[1] // 2

    def multiply(step, carry):
        columns = pl.ds(pl.multiple_of(step * width, 128), width)
        momentum = jnp.concatenate([mine_ref[:, columns], other_ref[:, columns]], axis=0)
        product = lax.dot_general(momentum, terms_ref[...], BOTH_FIRST, preferred_element_type=f32)
        total = (product[:, 2 * rank :] + product[:, rank : 2 * rank]) + product[:, :rank]
        whole_ref[columns, :] = total
        return carry

    lax.fori_loop(0, 2, multiply, 0)
    for by, ref in enumerate(pieces):
        place = ahead(at_ref[AT_Y], by, NY)
        ref[:MAIN, :] = whole_ref[pl.ds(pl.multiple_of(place * MAIN, MAIN), MAIN), :]
        ref[MAIN:, :] = whole_ref[pl.ds(pl.multiple_of(NY * MAIN + place * TAIL, TAIL), TAIL), :]


def cross(at, mine, other, left_mine, left_other):
    rows, cols = mine.shape
    rank = left_mine.shape[1]
    return pl.pallas_call(
        cross_kernel,
        out_shape=[jax.ShapeDtypeStruct((cols // NY, rank), f32)] * NY,
        in_specs=[SMEM] + [VMEM] * 4,
        out_specs=[VMEM] * NY,
        scratch_shapes=[pltpu.VMEM((2 * rows, 3 * rank), bf16), pltpu.VMEM((cols, rank), f32)],
        compiler_params=pltpu.CompilerParams(vmem_limit_bytes=16 * MIB),
        cost_estimate=pl.CostEstimate(
            flops=12 * rows * cols * rank, bytes_accessed=4 * rows * cols + 8 * cols * rank, transcendentals=0
        ),
    )(at, mine, other, left_mine, left_other)


def prepare_left(scaling, at_ref, solved_ref, squares_ref, left_ref, inverse_ref):
    rows, rank = solved_ref.shape
    solved = solved_ref[...]
    squares = jnp.sum(squares_ref[...], axis=0)
    inverse_lengths = lax.rsqrt(squares + 1e-06)
    left_ref[:rows, :] = solved.astype(bf16)
    left_ref[rows : 2 * rows, :] = (solved * (scaling * inverse_lengths)).astype(bf16)
    wanted = lax.broadcasted_iota(jnp.int32, (16, rank), 0) + at_ref[FIRST_RANK]
    picked = jnp.where(wanted == lax.broadcasted_iota(jnp.int32, (16, rank), 1), 1.0, 0.0)
    left_ref[2 * rows :, :] = picked.astype(bf16)
    own = jnp.sum(picked * inverse_lengths, axis=1, keepdims=True)
    inverse_ref[...] = jnp.broadcast_to(own, inverse_ref.shape)


def write_blocks(column_of, right_ref, momentum_ref, out_refs, stage_refs, left_ref, inverse_ref, semaphores):
    taken_ref, stages = stage_refs[0], stage_refs[1:]
    blocks, rows, width = taken_ref.shape
    shard_rank = stages[2].shape[1]

    def take(n):
        columns = pl.ds(pl.multiple_of(column_of(n), 128), width)
        return pltpu.make_async_copy(momentum_ref.at[:, columns], taken_ref.at[n], semaphores.at[0, n])

    def give(n, out):
        columns = pl.ds(pl.multiple_of(column_of(n), 128), width)
        return pltpu.make_async_copy(
            stages[out].at[n], out_refs[out].at[:, columns], semaphores.at[1 + out, n]
        )

    def write(n, carry):
        right = right_ref[pl.ds(pl.multiple_of(n * width, width), width), :]
        product = lax.dot_general(left_ref[...], right, BOTH_LAST, preferred_element_type=f32)
        stages[1][n] = product[rows : 2 * rows].astype(bf16)
        stages[2][n] = product[2 * rows : 2 * rows + shard_rank] * inverse_ref[:shard_rank, :1]
        take(n).wait()
        momentum = taken_ref[n].astype(f32)
        stages[0][n] = (momentum - (1.0 - momentum_decay) * product[:rows]).astype(bf16)
        for out in range(3):
            give(n, out).start()
        return carry

    def start():
        for n in range(blocks):
            take(n).start()

    def wait():
        for n in range(blocks):
            for out in range(3):
                give(n, out).wait()

    return start, lambda: lax.fori_loop(0, blocks, write, 0), wait


def stages_of(blocks, rows, width, shard_rank):
    return [
        pltpu.VMEM((blocks, rows, width), bf16),
        pltpu.VMEM((blocks, rows, width), bf16),
        pltpu.VMEM((blocks, rows, width), bf16),
        pltpu.VMEM((blocks, shard_rank, width), f32),
        pltpu.SemaphoreType.DMA((4, blocks)),
    ]


def first_kernel(scaling, at_ref, momentum_ref, solved_ref, squares_ref, *refs):
    pieces, outs = refs[:6], refs[6:9]
    right_ref, left_ref, inverse_ref, loads = refs[9:13]
    stages, semaphores = refs[13:17], refs[17]
    half = momentum_ref.shape[1] // 2

    def column_of(n):
        side = lax.rem(at_ref[AT_CORE] + n // 3, 2)
        by = n % 3 + n % 3 // 2
        return side * half + ahead(at_ref[AT_Y], by, NY) * MAIN

    start, write, wait = write_blocks(
        column_of, right_ref, momentum_ref, outs, stages, left_ref, inverse_ref, semaphores
    )
    copies = [
        pltpu.make_async_copy(
            ref.at[pl.ds(0, MAIN), :], right_ref.at[pl.ds(n * MAIN, MAIN), :], loads.at[n]
        )
        for n, ref in enumerate(pieces)
    ]
    for copy in copies:
        copy.start()
    start()
    prepare_left(scaling, at_ref, solved_ref, squares_ref, left_ref, inverse_ref)
    for copy in copies:
        copy.wait()
    write()
    wait()


def second_kernel(scaling, at_ref, momentum_ref, solved_ref, squares_ref, *refs):
    pieces, outs = refs[:10], refs[13:16]
    main_ref, tail_ref, left_ref, inverse_ref = refs[16:20]
    main_stages, main_semaphores = refs[20:24], refs[24]
    tail_stages, tail_semaphores = refs[25:29], refs[29]
    half = momentum_ref.shape[1] // 2

    def side_of(n):
        return lax.rem(at_ref[AT_CORE] + n, 2)

    start_main, write_main, wait_main = write_blocks(
        lambda n: side_of(n) * half + ahead(at_ref[AT_Y], 2, NY) * MAIN,
        main_ref, momentum_ref, outs, main_stages, left_ref, inverse_ref, main_semaphores,
    )
    start_tail, write_tail, wait_tail = write_blocks(
        lambda n: side_of(n) * half + NY * MAIN,
        tail_ref, momentum_ref, outs, tail_stages, left_ref, inverse_ref, tail_semaphores,
    )
    start_main()
    start_tail()
    prepare_left(scaling, at_ref, solved_ref, squares_ref, left_ref, inverse_ref)
    for side in range(2):
        own, one, three, front, back = pieces[5 * side : 5 * side + 5]
        size = front.shape[0]
        main_ref[side * MAIN : side * MAIN + size, :] = front[...]
        main_ref[side * MAIN + size : (side + 1) * MAIN, :] = back[: MAIN - size, :]
        for by, ref, begin in ((0, own, MAIN), (1, one, MAIN), (3, three, MAIN), (2, back, MAIN - size)):
            place = side * NY * TAIL + ahead(at_ref[AT_Y], by, NY) * TAIL
            tail_ref[pl.ds(pl.multiple_of(place, TAIL), TAIL), :] = ref[begin : begin + TAIL, :]
    write_main()
    write_tail()
    wait_main()
    wait_tail()


def finish(at, momentum, solved, squares, near, far, scaling, shard_rank):
    rows, cols = momentum.shape
    rank = solved.shape[1]
    outs = [jax.ShapeDtypeStruct((rows, cols), bf16)] * 2 + [jax.ShapeDtypeStruct((shard_rank, cols), f32)]
    both = [pltpu.VMEM((2 * rows + 16, rank), bf16), pltpu.VMEM((16, 128), f32)]
    first = pl.pallas_call(
        lambda *refs: first_kernel(scaling, *refs),
        out_shape=outs,
        in_specs=[SMEM, ANY, VMEM, VMEM] + [ANY] * 6,
        out_specs=[ANY] * 3,
        scratch_shapes=[pltpu.VMEM((6 * MAIN, rank), bf16)]
        + both
        + [pltpu.SemaphoreType.DMA((6,))]
        + stages_of(6, rows, MAIN, shard_rank),
        compiler_params=pltpu.CompilerParams(vmem_limit_bytes=18 * MIB),
        cost_estimate=pl.CostEstimate(
            flops=3 * rows * cols * rank, bytes_accessed=6 * rows * cols, transcendentals=0
        ),
    )(at, momentum, solved, squares, *near)
    first = list(first)
    first[2], far = lax.optimization_barrier((first[2], far))
    far = far + tuple(swap_cores(block) for block in far)
    pieces = near[:3] + far[:2] + near[3:] + far[2:]
    return pl.pallas_call(
        lambda *refs: second_kernel(scaling, *refs),
        out_shape=outs,
        in_specs=[SMEM, ANY, VMEM, VMEM] + [VMEM] * 10 + [ANY] * 3,
        out_specs=[ANY] * 3,
        scratch_shapes=[pltpu.VMEM((2 * MAIN, rank), bf16), pltpu.VMEM((2 * NY * TAIL, rank), bf16)]
        + both
        + stages_of(2, rows, MAIN, shard_rank)
        + stages_of(2, rows, NY * TAIL, shard_rank),
        input_output_aliases={14: 0, 15: 1, 16: 2},
        compiler_params=pltpu.CompilerParams(vmem_limit_bytes=18 * MIB),
        cost_estimate=pl.CostEstimate(
            flops=rows * cols * rank, bytes_accessed=2 * rows * cols, transcendentals=0
        ),
    )(at, momentum, solved, squares, *pieces, *first)


def swap_cores(block):
    return lax.ppermute(block, "c", [(0, 1), (1, 0)])


def from_ahead(block, axis, by, parts=4):
    return lax.ppermute(block, axis, [((i + by) % parts, i) for i in range(parts)])


def all_of_four(block, axis):
    return [block] + [from_ahead(block, axis, by) for by in (1, 2, 3)]


def ring_of_four(block, axis, beside):
    middle = block.shape[0] // 2
    one, three = from_ahead(block, axis, 1), from_ahead(block, axis, 3)
    block, one, three, beside = lax.optimization_barrier((block, one, three, beside))
    across = (from_ahead(three[:middle], axis, 3), from_ahead(one[middle:], axis, 1))
    return (block, one, three), across, beside


def exchange(pieces, axes):
    return lax.all_to_all(pieces, axes, 0, 0)


def per_device(momentum, q_basis):
    rows, cols = momentum.shape
    half = cols // 2
    shard_rank = q_basis.shape[0]
    rank = shard_rank * NZ * NY * 2
    core, at_x, at_y = lax.axis_index("c"), lax.axis_index("x"), lax.axis_index("y")
    position = (lax.axis_index("z") * NY + at_y) * 2 + core
    at = jnp.stack([at_y, core, at_x, position * shard_rank]).astype(jnp.int32)


    def columns(array, of_core):
        return lax.dynamic_slice_in_dim(array, of_core * half, half, 1)

    basis_half = q_basis.astype(bf16)
    basis_own = columns(basis_half, core)
    sent = columns(basis_half, 1 - core)
    later, sent, at = lax.optimization_barrier((momentum, sent, at))
    mine, theirs = columns(later, core), columns(later, 1 - core)
    basis_other = swap_cores(sent)
    mine, theirs, basis_other = lax.optimization_barrier((mine, theirs, basis_other))
    other = swap_cores(theirs)
    basis_chip = jnp.concatenate(
        [jnp.where(core == 0, basis_own, basis_other), jnp.where(core == 0, basis_other, basis_own)]
    )
    basis = exchange(jnp.broadcast_to(basis_chip[None], (NZ,) + basis_chip.shape), "z")
    basis = basis.reshape(rank // NY, half)
    proj_mine, proj_other = project(at, mine, other, all_of_four(basis, "y"))
    blocks = add_in_blocks(at, proj_mine, swap_cores(proj_other))
    block = [blocks[0]] + [from_ahead(blocks[by], "x", NX - by) for by in (1, 2, 3)]
    block = sum_four_copies(block, 1)[0]
    projected, gram_keep, gram_send = gram_rows_of(at, all_of_four(block, "x"))

    gram_rows = add(gram_keep, swap_cores(gram_send))
    gram_rows, proj_swapped = lax.optimization_barrier((gram_rows, swap_cores(projected)))
    gram_rows = all_of_four(gram_rows, "y")
    gram_rows = sum_copies(exchange(sum_four_copies(gram_rows, NZ), "z"), 1)[0]
    gram_chip = jnp.concatenate([gram_rows, swap_cores(gram_rows)])
    inverse = inverse_factor(at, all_of_four(gram_chip, "x"))

    crossed = cross(at, mine, other, projected, proj_swapped)
    right = [crossed[0]] + [from_ahead(crossed[by], "y", NY - by) for by in (1, 2, 3)]
    right = whiten(inverse, right, bf16).reshape(NZ, half // (NY * NZ), rank)
    right = exchange(sum_copies(exchange(right, "z"), NZ), "z").reshape(half // NY, rank)
    solved = whiten(inverse, [projected], f32)

    parts = NY * 2 * NX
    squares = exchange(square_copies(right, parts), ("y", "c", "x"))
    near, far, squares = ring_of_four(right, "y", squares)
    near = near + tuple(swap_cores(block) for block in near)

    total_rows = rows * NZ * NY * 2
    total_cols = cols * NX
    scaling = math.sqrt(total_rows * total_cols / rank)
    return tuple(finish(at, momentum, solved, squares, near, far, scaling, shard_rank))


def solution(mesh):
    split = Mesh(mesh.devices.reshape(NZ, NY, 2, NX), ("z", "y", "c", "x"))
    spec = P(("z", "y", "c"), "x")
    return jax.shard_map(
        per_device,
        mesh=split,
        in_specs=(spec, spec),
        out_specs=(spec, spec, spec),
        check_vma=False,
    )
```

```python
import math

import jax
import jax.numpy as jnp
from jax import lax
from jax.experimental import pallas as pl
from jax.experimental.pallas import tpu as pltpu
from jax.sharding import Mesh
from jax.sharding import PartitionSpec as P

momentum_decay = 0.95
f32, bf16 = jnp.float32, jnp.bfloat16
HIGHEST = lax.Precision.HIGHEST
VMEM = pl.BlockSpec(memory_space=pltpu.VMEM)
SMEM = pl.BlockSpec(memory_space=pltpu.SMEM)
ANY = pl.BlockSpec(memory_space=pl.ANY)
BOTH_LAST = (((1,), (1,)), ((), ()))
BOTH_FIRST = (((0,), (0,)), ((), ()))
MIB = 2**20
NZ, NY, NX = 8, 4, 4
PIVOTS = 8
MAIN, TAIL = 768, 64
AT_Y, AT_CORE, AT_X, FIRST_RANK = range(4)


def ahead(index, by, parts):
    return lax.rem(index + by, parts)


def inverse_factor_kernel(at_ref, own_ref, next_ref, across_ref, last_ref, inverse_ref, work_ref, half_ref, done_ref):
    rank = work_ref.shape[0]
    part = rank // (NX * 2)
    for by, ref in enumerate((own_ref, next_ref, across_ref, last_ref)):
        base = ahead(at_ref[AT_X], by, NX) * 2
        for other in range(2):
            at_core = (at_ref[AT_CORE] + other) % 2
            start = pl.multiple_of((base + at_core) * part, part)
            work_ref[pl.ds(start, part), :] = ref[other * part : (other + 1) * part, :]
    gram = work_ref[...]
    diagonal = lax.broadcasted_iota(jnp.int32, gram.shape, 0) == lax.broadcasted_iota(
        jnp.int32, gram.shape, 1
    )
    ridge = 0.001 * jnp.sum(jnp.where(diagonal, gram, 0.0)) / rank
    work_ref[...] = jnp.where(diagonal, gram + ridge, gram)
    lane = lax.broadcasted_iota(jnp.int32, (1, rank), 1)
    per_y, per_half = NZ * PIVOTS, NZ * PIVOTS // 2
    half = rank // 2
    order = (lane % per_y) // PIVOTS * (NY * PIVOTS) + lane // per_y * PIVOTS + lane % PIVOTS

    def of_half(array, second):
        starts = [y * per_y + second * per_half for y in range(NY)]
        return jnp.concatenate([array[start : start + per_half] for start in starts], axis=0)

    half_ref[...] = of_half(work_ref[...], 0)

    def wide(value):
        return jnp.concatenate([value] * (rank // 128), axis=1)

    steps = range(PIVOTS)

    def eliminate(second, carry):
        for group in range(half // PIVOTS):
            at_z, at_y = divmod(group, NY)
            first_row = at_y * per_half + at_z * PIVOTS
            at = at_y * per_y + at_z * PIVOTS
            block = half_ref[first_row : first_row + PIVOTS, :]
            spread = [jnp.broadcast_to(block[:, at + t : at + t + 1], (PIVOTS, 128)) for t in steps]
            core = [[spread[t][s : s + 1, :] for t in range(s + 1)] for s in steps]
            inside = (lane >= at) & (lane < at + PIVOTS)
            row = [jnp.where(inside, (lane == at + s).astype(f32), block[s : s + 1, :]) for s in steps]
            inverse = [None] * PIVOTS
            ratio = [[None] * PIVOTS for _ in steps]
            for t in steps:
                inverse[t] = 1.0 / core[t][t]
                for s in range(t + 1, PIVOTS):
                    ratio[s][t] = core[s][t] * inverse[t]
                for s in range(t + 1, PIVOTS):
                    for u in range(t + 1, s + 1):
                        core[s][u] = core[s][u] - ratio[s][t] * core[u][t]
                    row[s] = row[s] - wide(ratio[s][t]) * row[t]
            for s in steps:
                done_ref[group * PIVOTS + s : group * PIVOTS + s + 1, :] = row[s] * wide(
                    lax.rsqrt(core[s][s])
                )
            solved = [row[s] * wide(inverse[s]) for s in steps]
            for s in reversed(steps):
                for t in range(s):
                    solved[t] = solved[t] - wide(ratio[s][t]) * solved[s]
            for y in range(NY):
                next_z = at_z + (0 if y > at_y else 1)
                if next_z == NZ // 2:
                    continue
                rows = slice(y * per_half + next_z * PIVOTS, (y + 1) * per_half)
                below = half_ref[rows, :]
                rest = jnp.where(inside, 0.0, below)
                for t in steps:
                    rest = rest - below[:, at + t : at + t + 1] * solved[t]
                half_ref[rows, :] = rest

        @pl.when(second == 0)
        def _():
            done = done_ref[...]
            lower = order <= lax.broadcasted_iota(jnp.int32, (half, rank), 0)
            inverse_ref[:half, :] = jnp.where(lower, done, 0.0)
            done = jnp.where(lower | (order >= half), done, 0.0)
            product = lax.dot_general(
                done, done, BOTH_FIRST, preferred_element_type=f32, precision=HIGHEST
            )
            rest = jnp.where(order < half, 0.0, of_half(work_ref[...], 1)) - of_half(product, 1)
            half_ref[...] = pltpu.roll(rest, rank - per_half, 1)

        @pl.when(second == 1)
        def _():
            inverse_ref[half:, :] = jnp.where(
                order <= lax.broadcasted_iota(jnp.int32, (half, rank), 0) + half,
                pltpu.roll(done_ref[...], per_half, 1),
                0.0,
            )

        return carry

    lax.fori_loop(0, 2, eliminate, 0)


def inverse_factor(at, pieces):
    rank = pieces[0].shape[1]
    return pl.pallas_call(
        inverse_factor_kernel,
        out_shape=jax.ShapeDtypeStruct((rank, rank), f32),
        in_specs=[SMEM] + [VMEM] * 4,
        out_specs=VMEM,
        scratch_shapes=[pltpu.VMEM((rows, rank), f32) for rows in (rank, rank // 2, rank // 2)],
        compiler_params=pltpu.CompilerParams(vmem_limit_bytes=8 * MIB),
        cost_estimate=pl.CostEstimate(flops=10**9, bytes_accessed=2**20, transcendentals=0),
    )(at, *pieces)


def project_kernel(at_ref, mine_ref, other_ref, *refs):
    pieces, (out_mine_ref, out_other_ref, basis_ref) = refs[:NY], refs[NY:]
    for by, ref in enumerate(pieces):
        size = ref.shape[0]
        start = pl.multiple_of(ahead(at_ref[AT_Y], by, NY) * size, size)
        basis_ref[pl.ds(start, size), :] = ref[...]
    width = mine_ref.shape[1] // 2
    out_mine_ref[...] = jnp.zeros_like(out_mine_ref)
    out_other_ref[...] = jnp.zeros_like(out_other_ref)

    def add(step, carry):
        columns = pl.ds(pl.multiple_of(step * width, 128), width)
        basis = basis_ref[:, columns]
        for ref, out_ref in ((mine_ref, out_mine_ref), (other_ref, out_other_ref)):
            out_ref[...] += lax.dot_general(
                ref[:, columns], basis, BOTH_LAST, preferred_element_type=f32
            )
        return carry

    lax.fori_loop(0, 2, add, 0)


def project(at, mine, other, pieces):
    rows, cols = mine.shape
    rank = pieces[0].shape[0] * NY
    return pl.pallas_call(
        project_kernel,
        out_shape=[jax.ShapeDtypeStruct((rows, rank), f32)] * 2,
        in_specs=[SMEM] + [VMEM] * 6,
        out_specs=[VMEM, VMEM],
        scratch_shapes=[pltpu.VMEM((rank, cols), bf16)],
        compiler_params=pltpu.CompilerParams(vmem_limit_bytes=12 * MIB),
        cost_estimate=pl.CostEstimate(
            flops=4 * rows * cols * rank, bytes_accessed=6 * rows * cols, transcendentals=0
        ),
    )(at, mine, other, *pieces)


def small(kernel, out, *args):
    specs = [SMEM if arg.dtype == jnp.int32 else VMEM for arg in args]
    return pl.pallas_call(
        kernel,
        out_shape=out,
        in_specs=specs,
        out_specs=VMEM,
        compiler_params=pltpu.CompilerParams(vmem_limit_bytes=8 * MIB),
        cost_estimate=pl.CostEstimate(flops=2**20, bytes_accessed=2**20, transcendentals=0),
    )(*args)


def add(one, two):
    def kernel(one_ref, two_ref, out_ref):
        out_ref[...] = one_ref[...] + two_ref[...]

    return small(kernel, jax.ShapeDtypeStruct(one.shape, f32), one, two)


def sum_four_copies(pieces, copies):
    def kernel(own_ref, one_ref, two_ref, three_ref, out_ref):
        total = (own_ref[...] + two_ref[...]) + (one_ref[...] + three_ref[...])
        for n in range(copies):
            out_ref[n] = total

    return small(kernel, jax.ShapeDtypeStruct((copies,) + pieces[0].shape, f32), *pieces)


def sum_copies(pieces, copies):
    def kernel(pieces_ref, out_ref):
        total = jnp.sum(pieces_ref[...].astype(f32), axis=0).astype(pieces_ref.dtype)
        for n in range(copies):
            out_ref[n] = total

    shape = (copies,) + pieces.shape[1:]
    return small(kernel, jax.ShapeDtypeStruct(shape, pieces.dtype), pieces)


def square_copies(right, copies):
    rank = right.shape[1]

    def kernel(right_ref, out_ref):
        right = right_ref[...].astype(f32)
        total = jnp.sum(right * right, axis=0, keepdims=True)
        for n in range(copies):
            out_ref[n] = total

    return small(kernel, jax.ShapeDtypeStruct((copies, 1, rank), f32), right)


def whiten(inverse, pieces, out):
    def kernel(inverse_ref, *refs):
        total = refs[0][...]
        for ref in refs[1:-1]:
            total = total + ref[...]
        refs[-1][...] = lax.dot_general(
            total, inverse_ref[...], BOTH_LAST, preferred_element_type=f32, precision=HIGHEST
        ).astype(out)

    return small(kernel, jax.ShapeDtypeStruct(pieces[0].shape, out), inverse, *pieces)


def gram_kernel(at_ref, own_ref, one_ref, two_ref, three_ref, projected_ref, keep_ref, send_ref, gram_ref):
    for by, ref in enumerate((own_ref, one_ref, two_ref, three_ref)):
        size = ref.shape[0]
        start = pl.multiple_of(ahead(at_ref[AT_X], by, NX) * size, size)
        projected_ref[pl.ds(start, size), :] = ref[...]
    projected = projected_ref[...]
    gram_ref[...] = lax.dot_general(
        projected, projected, BOTH_FIRST, preferred_element_type=f32, precision=HIGHEST
    )
    part = keep_ref.shape[0]
    for other, ref in enumerate((keep_ref, send_ref)):
        place = at_ref[AT_X] * 2 + (at_ref[AT_CORE] + other) % 2
        ref[...] = gram_ref[pl.ds(pl.multiple_of(place * part, part), part), :]


def gram_rows_of(at, pieces):
    size, rank = pieces[0].shape
    part = jax.ShapeDtypeStruct((rank // (NX * 2), rank), f32)
    return pl.pallas_call(
        gram_kernel,
        out_shape=[jax.ShapeDtypeStruct((size * NX, rank), f32), part, part],
        in_specs=[SMEM] + [VMEM] * 4,
        out_specs=[VMEM] * 3,
        scratch_shapes=[pltpu.VMEM((rank, rank), f32)],
        compiler_params=pltpu.CompilerParams(vmem_limit_bytes=8 * MIB),
        cost_estimate=pl.CostEstimate(flops=2**28, bytes_accessed=2**20, transcendentals=0),
    )(at, *pieces)


def add_in_blocks(at, one, two):
    rows, rank = one.shape
    size = rows // NX

    def kernel(at_ref, one_ref, two_ref, *outs):
        for by, ref in enumerate(outs):
            start = pl.multiple_of(ahead(at_ref[AT_X], by, NX) * size, size)
            ref[...] = one_ref[pl.ds(start, size), :] + two_ref[pl.ds(start, size), :]

    return pl.pallas_call(
        kernel,
        out_shape=[jax.ShapeDtypeStruct((size, rank), f32)] * NX,
        in_specs=[SMEM, VMEM, VMEM],
        out_specs=[VMEM] * NX,
        compiler_params=pltpu.CompilerParams(vmem_limit_bytes=8 * MIB),
        cost_estimate=pl.CostEstimate(flops=2**20, bytes_accessed=2**20, transcendentals=0),
    )(at, one, two)


def cross_kernel(at_ref, mine_ref, other_ref, left_mine_ref, left_other_ref, *refs):
    pieces, (terms_ref, whole_ref) = refs[:NY], refs[NY:]
    rows, rank = left_mine_ref.shape
    for n, ref in enumerate((left_mine_ref, left_other_ref)):
        left = ref[...]
        for t in range(3):
            term = left.astype(bf16)
            terms_ref[n * rows : (n + 1) * rows, t * rank : (t + 1) * rank] = term
            left = left - term.astype(f32)
    width = mine_ref.shape[1] // 2

    def multiply(step, carry):
        columns = pl.ds(pl.multiple_of(step * width, 128), width)
        momentum = jnp.concatenate([mine_ref[:, columns], other_ref[:, columns]], axis=0)
        product = lax.dot_general(momentum, terms_ref[...], BOTH_FIRST, preferred_element_type=f32)
        total = (product[:, 2 * rank :] + product[:, rank : 2 * rank]) + product[:, :rank]
        whole_ref[columns, :] = total
        return carry

    lax.fori_loop(0, 2, multiply, 0)
    for by, ref in enumerate(pieces):
        place = ahead(at_ref[AT_Y], by, NY)
        ref[:MAIN, :] = whole_ref[pl.ds(pl.multiple_of(place * MAIN, MAIN), MAIN), :]
        ref[MAIN:, :] = whole_ref[pl.ds(pl.multiple_of(NY * MAIN + place * TAIL, TAIL), TAIL), :]


def cross(at, mine, other, left_mine, left_other):
    rows, cols = mine.shape
    rank = left_mine.shape[1]
    return pl.pallas_call(
        cross_kernel,
        out_shape=[jax.ShapeDtypeStruct((cols // NY, rank), f32)] * NY,
        in_specs=[SMEM] + [VMEM] * 4,
        out_specs=[VMEM] * NY,
        scratch_shapes=[pltpu.VMEM((2 * rows, 3 * rank), bf16), pltpu.VMEM((cols, rank), f32)],
        compiler_params=pltpu.CompilerParams(vmem_limit_bytes=16 * MIB),
        cost_estimate=pl.CostEstimate(
            flops=12 * rows * cols * rank, bytes_accessed=4 * rows * cols + 8 * cols * rank, transcendentals=0
        ),
    )(at, mine, other, left_mine, left_other)


def prepare_left(scaling, at_ref, solved_ref, squares_ref, left_ref, inverse_ref):
    rows, rank = solved_ref.shape
    solved = solved_ref[...]
    squares = jnp.sum(squares_ref[...], axis=0)
    inverse_lengths = lax.rsqrt(squares + 1e-06)
    left_ref[:rows, :] = solved.astype(bf16)
    left_ref[rows : 2 * rows, :] = (solved * (scaling * inverse_lengths)).astype(bf16)
    wanted = lax.broadcasted_iota(jnp.int32, (16, rank), 0) + at_ref[FIRST_RANK]
    picked = jnp.where(wanted == lax.broadcasted_iota(jnp.int32, (16, rank), 1), 1.0, 0.0)
    left_ref[2 * rows :, :] = picked.astype(bf16)
    own = jnp.sum(picked * inverse_lengths, axis=1, keepdims=True)
    inverse_ref[...] = jnp.broadcast_to(own, inverse_ref.shape)


def write_blocks(column_of, right_ref, momentum_ref, out_refs, stage_refs, left_ref, inverse_ref, semaphores):
    taken_ref, stages = stage_refs[0], stage_refs[1:]
    blocks, rows, width = taken_ref.shape
    shard_rank = stages[2].shape[1]

    def take(n):
        columns = pl.ds(pl.multiple_of(column_of(n), 128), width)
        return pltpu.make_async_copy(momentum_ref.at[:, columns], taken_ref.at[n], semaphores.at[0, n])

    def give(n, out):
        columns = pl.ds(pl.multiple_of(column_of(n), 128), width)
        return pltpu.make_async_copy(
            stages[out].at[n], out_refs[out].at[:, columns], semaphores.at[1 + out, n]
        )

    def write(n, carry):
        right = right_ref[pl.ds(pl.multiple_of(n * width, width), width), :]
        product = lax.dot_general(left_ref[...], right, BOTH_LAST, preferred_element_type=f32)
        stages[1][n] = product[rows : 2 * rows].astype(bf16)
        stages[2][n] = product[2 * rows : 2 * rows + shard_rank] * inverse_ref[:shard_rank, :1]
        take(n).wait()
        momentum = taken_ref[n].astype(f32)
        stages[0][n] = (momentum - (1.0 - momentum_decay) * product[:rows]).astype(bf16)
        for out in range(3):
            give(n, out).start()
        return carry

    def start():
        for n in range(blocks):
            take(n).start()

    def wait():
        for n in range(blocks):
            for out in range(3):
                give(n, out).wait()

    return start, lambda: lax.fori_loop(0, blocks, write, 0), wait


def stages_of(blocks, rows, width, shard_rank):
    return [
        pltpu.VMEM((blocks, rows, width), bf16),
        pltpu.VMEM((blocks, rows, width), bf16),
        pltpu.VMEM((blocks, rows, width), bf16),
        pltpu.VMEM((blocks, shard_rank, width), f32),
        pltpu.SemaphoreType.DMA((4, blocks)),
    ]


def first_kernel(scaling, at_ref, momentum_ref, solved_ref, squares_ref, *refs):
    pieces, outs = refs[:6], refs[6:9]
    right_ref, left_ref, inverse_ref, loads = refs[9:13]
    stages, semaphores = refs[13:17], refs[17]
    half = momentum_ref.shape[1] // 2

    def column_of(n):
        side = lax.rem(at_ref[AT_CORE] + n // 3, 2)
        by = n % 3 + n % 3 // 2
        return side * half + ahead(at_ref[AT_Y], by, NY) * MAIN

    start, write, wait = write_blocks(
        column_of, right_ref, momentum_ref, outs, stages, left_ref, inverse_ref, semaphores
    )
    copies = [
        pltpu.make_async_copy(
            ref.at[pl.ds(0, MAIN), :], right_ref.at[pl.ds(n * MAIN, MAIN), :], loads.at[n]
        )
        for n, ref in enumerate(pieces)
    ]
    for copy in copies:
        copy.start()
    start()
    prepare_left(scaling, at_ref, solved_ref, squares_ref, left_ref, inverse_ref)
    for copy in copies:
        copy.wait()
    write()
    wait()


def second_kernel(scaling, at_ref, momentum_ref, solved_ref, squares_ref, *refs):
    pieces, outs = refs[:10], refs[13:16]
    main_ref, tail_ref, left_ref, inverse_ref = refs[16:20]
    main_stages, main_semaphores = refs[20:24], refs[24]
    tail_stages, tail_semaphores = refs[25:29], refs[29]
    half = momentum_ref.shape[1] // 2

    def side_of(n):
        return lax.rem(at_ref[AT_CORE] + n, 2)

    start_main, write_main, wait_main = write_blocks(
        lambda n: side_of(n) * half + ahead(at_ref[AT_Y], 2, NY) * MAIN,
        main_ref, momentum_ref, outs, main_stages, left_ref, inverse_ref, main_semaphores,
    )
    start_tail, write_tail, wait_tail = write_blocks(
        lambda n: side_of(n) * half + NY * MAIN,
        tail_ref, momentum_ref, outs, tail_stages, left_ref, inverse_ref, tail_semaphores,
    )
    start_main()
    start_tail()
    prepare_left(scaling, at_ref, solved_ref, squares_ref, left_ref, inverse_ref)
    for side in range(2):
        own, one, three, front, back = pieces[5 * side : 5 * side + 5]
        size = front.shape[0]
        main_ref[side * MAIN : side * MAIN + size, :] = front[...]
        main_ref[side * MAIN + size : (side + 1) * MAIN, :] = back[: MAIN - size, :]
        for by, ref, begin in ((0, own, MAIN), (1, one, MAIN), (3, three, MAIN), (2, back, MAIN - size)):
            place = side * NY * TAIL + ahead(at_ref[AT_Y], by, NY) * TAIL
            tail_ref[pl.ds(pl.multiple_of(place, TAIL), TAIL), :] = ref[begin : begin + TAIL, :]
    write_main()
    write_tail()
    wait_main()
    wait_tail()


def finish(at, momentum, solved, squares, near, far, scaling, shard_rank):
    rows, cols = momentum.shape
    rank = solved.shape[1]
    outs = [jax.ShapeDtypeStruct((rows, cols), bf16)] * 2 + [jax.ShapeDtypeStruct((shard_rank, cols), f32)]
    both = [pltpu.VMEM((2 * rows + 16, rank), bf16), pltpu.VMEM((16, 128), f32)]
    first = pl.pallas_call(
        lambda *refs: first_kernel(scaling, *refs),
        out_shape=outs,
        in_specs=[SMEM, ANY, VMEM, VMEM] + [ANY] * 6,
        out_specs=[ANY] * 3,
        scratch_shapes=[pltpu.VMEM((6 * MAIN, rank), bf16)]
        + both
        + [pltpu.SemaphoreType.DMA((6,))]
        + stages_of(6, rows, MAIN, shard_rank),
        compiler_params=pltpu.CompilerParams(vmem_limit_bytes=18 * MIB),
        cost_estimate=pl.CostEstimate(
            flops=3 * rows * cols * rank, bytes_accessed=6 * rows * cols, transcendentals=0
        ),
    )(at, momentum, solved, squares, *near)
    first = list(first)
    first[2], far = lax.optimization_barrier((first[2], far))
    far = far + tuple(swap_cores(block) for block in far)
    pieces = near[:3] + far[:2] + near[3:] + far[2:]
    return pl.pallas_call(
        lambda *refs: second_kernel(scaling, *refs),
        out_shape=outs,
        in_specs=[SMEM, ANY, VMEM, VMEM] + [VMEM] * 10 + [ANY] * 3,
        out_specs=[ANY] * 3,
        scratch_shapes=[pltpu.VMEM((2 * MAIN, rank), bf16), pltpu.VMEM((2 * NY * TAIL, rank), bf16)]
        + both
        + stages_of(2, rows, MAIN, shard_rank)
        + stages_of(2, rows, NY * TAIL, shard_rank),
        input_output_aliases={14: 0, 15: 1, 16: 2},
        compiler_params=pltpu.CompilerParams(vmem_limit_bytes=18 * MIB),
        cost_estimate=pl.CostEstimate(
            flops=rows * cols * rank, bytes_accessed=2 * rows * cols, transcendentals=0
        ),
    )(at, momentum, solved, squares, *pieces, *first)


def swap_cores(block):
    return lax.ppermute(block, "c", [(0, 1), (1, 0)])


def from_ahead(block, axis, by, parts=4):
    return lax.ppermute(block, axis, [((i + by) % parts, i) for i in range(parts)])


def all_of_four(block, axis):
    return [block] + [from_ahead(block, axis, by) for by in (1, 2, 3)]


def ring_of_four(block, axis, beside):
    middle = block.shape[0] // 2
    one, three = from_ahead(block, axis, 1), from_ahead(block, axis, 3)
    block, one, three, beside = lax.optimization_barrier((block, one, three, beside))
    across = (from_ahead(three[:middle], axis, 3), from_ahead(one[middle:], axis, 1))
    return (block, one, three), across, beside


def exchange(pieces, axes):
    return lax.all_to_all(pieces, axes, 0, 0)


def per_device(momentum, q_basis):
    rows, cols = momentum.shape
    half = cols // 2
    shard_rank = q_basis.shape[0]
    rank = shard_rank * NZ * NY * 2
    core, at_x, at_y = lax.axis_index("c"), lax.axis_index("x"), lax.axis_index("y")
    position = (lax.axis_index("z") * NY + at_y) * 2 + core
    at = jnp.stack([at_y, core, at_x, position * shard_rank]).astype(jnp.int32)


    def columns(array, of_core):
        return lax.dynamic_slice_in_dim(array, of_core * half, half, 1)

    basis_half = q_basis.astype(bf16)
    basis_own = columns(basis_half, core)
    sent = columns(basis_half, 1 - core)
    later, sent, at = lax.optimization_barrier((momentum, sent, at))
    mine, theirs = columns(later, core), columns(later, 1 - core)
    basis_other = swap_cores(sent)
    mine, theirs, basis_other = lax.optimization_barrier((mine, theirs, basis_other))
    other = swap_cores(theirs)
    basis_chip = jnp.concatenate(
        [jnp.where(core == 0, basis_own, basis_other), jnp.where(core == 0, basis_other, basis_own)]
    )
    basis = exchange(jnp.broadcast_to(basis_chip[None], (NZ,) + basis_chip.shape), "z")
    basis = basis.reshape(rank // NY, half)
    proj_mine, proj_other = project(at, mine, other, all_of_four(basis, "y"))
    blocks = add_in_blocks(at, proj_mine, swap_cores(proj_other))
    block = [blocks[0]] + [from_ahead(blocks[by], "x", NX - by) for by in (1, 2, 3)]
    block = sum_four_copies(block, 1)[0]
    projected, gram_keep, gram_send = gram_rows_of(at, all_of_four(block, "x"))

    gram_rows = add(gram_keep, swap_cores(gram_send))
    gram_rows, projected = lax.optimization_barrier((gram_rows, projected))
    proj_swapped = swap_cores(projected)
    gram_rows = all_of_four(gram_rows, "y")
    gram_rows = sum_copies(exchange(sum_four_copies(gram_rows, NZ), "z"), 1)[0]
    gram_chip = jnp.concatenate([gram_rows, swap_cores(gram_rows)])
    inverse = inverse_factor(at, all_of_four(gram_chip, "x"))

    crossed = cross(at, mine, other, projected, proj_swapped)
    right = [crossed[0]] + [from_ahead(crossed[by], "y", NY - by) for by in (1, 2, 3)]
    right = whiten(inverse, right, bf16).reshape(NZ, half // (NY * NZ), rank)
    right = exchange(sum_copies(exchange(right, "z"), NZ), "z").reshape(half // NY, rank)
    solved = whiten(inverse, [projected], f32)

    parts = NY * 2 * NX
    squares = exchange(square_copies(right, parts), ("y", "c", "x"))
    near, far, squares = ring_of_four(right, "y", squares)
    near = near + tuple(swap_cores(block) for block in near)

    total_rows = rows * NZ * NY * 2
    total_cols = cols * NX
    scaling = math.sqrt(total_rows * total_cols / rank)
    return tuple(finish(at, momentum, solved, squares, near, far, scaling, shard_rank))


def solution(mesh):
    split = Mesh(mesh.devices.reshape(NZ, NY, 2, NX), ("z", "y", "c", "x"))
    spec = P(("z", "y", "c"), "x")
    return jax.shard_map(
        per_device,
        mesh=split,
        in_specs=(spec, spec),
        out_specs=(spec, spec, spec),
        check_vma=False,
    )
```
